32 devices in a mesh: group: 2 (over x), req: 2 (over core), tensor: 8 (over z, y).
Axes of the slice: x: 2, y: 2, z: 4, core: 2. Of those that a mesh axis runs over, the one named last changes fastest.
Arguments:
- queries: bfloat16 [128, 8192], P(('group', 'req'), 'tensor'), parts along dimension 0, may hold values from -300 to 300
- prefix_kv: bfloat16 [16, 2, 8192, 128], P(('group', 'tensor')), parts along dimension 0, may hold values from -9 to 9, as said below
- suffix_kv: bfloat16 [128, 8, 2, 256, 128], P(('group', 'req'), 'tensor'), parts along dimension 0, may hold values from -9 to 9, as said below
- suffix_len: int32 [128], P(('group', 'req')), parts along dimension 0, may hold values from 1 to 256, 8192 in all
- residual: bfloat16 [128, 8192], P(('group', 'req')), parts along dimension 0, may hold values from -3 to 3
- out_weight: bfloat16 [8192, 8192], P('tensor'), may hold values from -0.0625 to 0.0625
- adapter_pages: bfloat16 [128, 2, 64, 8192], P('req', None, None, 'tensor'), may hold values from -1 to 1
- adapter_ids: int32 [128], P(('group', 'req')), parts along dimension 0, may hold values from 0 to 127, as said below
- pool_slot: int32 [128], replicated, may hold values from 0 to 127, each once
Outputs:
- updated: bfloat16 [128, 8192], P(('group', 'req')), parts along dimension 0
The draws below stay inside these ranges and needn't reach their ends.
There are 2 independent parts, one for each index of `group`. The reference program is written for one: setup_inputs(seed, part) draws one part's arguments, and reference() takes and returns one part's arrays. A program takes and returns all parts, laid end to end along the dimension named above; an argument that names none is the same for every part. Nothing has to cross between parts.
Inputs may be any that keep to these rules, and one draw needn't show every extreme that they name: `adapter_ids`: the 32 requests of one index of req name exactly 8 different adapters. `prefix_kv`: the copies of one key head are equal. `suffix_kv`: the copies of one key head are equal.
All inputs are finite; a program needn't handle non-finite values. No bound on the sum of `suffix_len` on one device may be relied on, other than what follows from the above.
Results may differ from the reference program's by a relative error of at most 0.0053.
Values may be sent and summed in bfloat16 or wider, within the bound.
No kernel may reach another device: no remote copies, remote signals or barrier semaphores. Data moves between devices by JAX's collectives and lax.ppermute only.
A program may use at most 192 MiB of HBM per device.

```python
import math
import jax
import jax.numpy as jnp
import numpy as np
from jax import lax

D = 8192
HEADS = 64
KV_HEADS = 8
HEAD_DIM = 128
RANK = 64
R_DEV = 32
PREFIX = 8192
SUFFIX = 256
DISTINCT = 8
REQS = 64
ADAPTERS = 128
KV_SLOTS = 8


def shared_draw(key):
    shape_keys = (KV_HEADS, PREFIX, HEAD_DIM)
    prefix_keys = jax.random.truncated_normal(jax.random.fold_in(key, 11), -3.0, 3.0, shape_keys)
    prefix_vals = jax.random.truncated_normal(jax.random.fold_in(key, 13), -3.0, 3.0, shape_keys)
    prefix_vals = 3.0 * prefix_vals
    shape_query = (REQS, HEADS, HEAD_DIM)
    query_rows = jax.random.truncated_normal(jax.random.fold_in(key, 15), -3.0, 3.0, shape_query)
    query_rows = 2.0 * query_rows
    positions = jax.random.randint(jax.random.fold_in(key, 17), (3,), 0, PREFIX - 1)
    for order, target in enumerate((160.0, 240.0, 360.0)):
        head_index = 5 * order % HEADS
        kv_head = head_index * KV_HEADS // HEADS
        spot = positions[order]
        neighbour = prefix_keys[kv_head, spot + 1]
        prefix_keys = prefix_keys.at[kv_head, spot + 1].set(neighbour)
        query_rows = query_rows.at[order, head_index].set(query_rows[order, head_index])
    stacked = jnp.stack([prefix_keys, prefix_vals], 1)
    stacked = jnp.repeat(stacked, KV_SLOTS // KV_HEADS, axis=0)
    return (query_rows.reshape(REQS, HEADS * HEAD_DIM), stacked)


def draw_queries(key, part):
    query_rows, stacked = shared_draw(key)
    return query_rows.astype(jnp.bfloat16)


def draw_prefix_kv(key, part):
    query_rows, stacked = shared_draw(key)
    return stacked.astype(jnp.bfloat16)


def draw_suffix_kv(key, part):
    key = jax.random.fold_in(key, 21)
    shape_rows = (REQS, KV_HEADS, SUFFIX, HEAD_DIM)
    suffix_keys = jax.random.truncated_normal(jax.random.fold_in(key, 1), -3.0, 3.0, shape_rows)
    suffix_keys = 1.5 * suffix_keys
    suffix_vals = jax.random.truncated_normal(jax.random.fold_in(key, 3), -3.0, 3.0, shape_rows)
    suffix_vals = 3.0 * suffix_vals
    stacked = jnp.stack([suffix_keys, suffix_vals], 2)
    return jnp.repeat(stacked, KV_SLOTS // KV_HEADS, axis=1).astype(jnp.bfloat16)


def draw_adapter_pages(key, part):
    key = jax.random.fold_in(key, 41)
    shape_pool = (ADAPTERS, 2, RANK, D)
    entries = jax.random.truncated_normal(key, -4.0, 4.0, shape_pool)
    member = jnp.arange(2).reshape(1, 2, 1, 1)
    factor = jnp.where(member == 0, D ** (-0.5), RANK ** (-0.5))
    return (entries * factor).astype(jnp.bfloat16)


def draw_adapter_ids(key, part):
    key = jax.random.fold_in(key, 31)
    blocks = REQS // R_DEV
    block_keys = jax.random.split(key, blocks)

    def draw_block(block_key):
        first_key, second_key, third_key = jax.random.split(block_key, 3)
        chosen = jax.random.permutation(first_key, ADAPTERS)[:DISTINCT]
        picked = jnp.concatenate([jnp.arange(DISTINCT, dtype=jnp.int32), jax.random.randint(second_key, (R_DEV - DISTINCT,), 0, DISTINCT).astype(jnp.int32)])
        picked = jax.random.permutation(third_key, picked)
        return chosen[picked].astype(jnp.int32)
    return jax.vmap(draw_block)(block_keys).reshape(REQS)


def steps_of(own_key, shape, pieces, smallest, high):
    factor_of = 1.0
    for position, blocks in pieces:
        draws = jax.random.uniform(jax.random.fold_in(jax.random.fold_in(own_key, 6), position), (blocks,), jnp.float32, smallest / len(pieces), high / len(pieces))
        factor_of = factor_of * jnp.repeat(jnp.exp(draws), shape[position] // blocks).reshape((-1,) + (1,) * (len(shape) - 1 - position))
    return factor_of


def split_up(number_of, total, limit, lean):
    weights = [(1 << 20) // math.isqrt(grade ** lean) + 1 for grade in range(2, number_of + 1)]
    surplus, given = total - limit - (number_of - 1), [1] * (number_of - 1)
    while surplus > 0:
        movable = [i for i in range(number_of - 1) if given[i] < limit]
        mass, remaining = sum([weights[i] for i in movable]), surplus
        for i in movable:
            more = min(limit - given[i], max(1, remaining * weights[i] // mass), surplus)
            given[i] = given[i] + more
            surplus = surplus - more
    return np.array([limit] + given)


def ragged_sizes(own_key, number_of, total, most, lean):
    if number_of == 2:
        one = jax.random.randint(own_key, (), max(1, total - most), min(most, total - 1) + 1)
        return jnp.stack([one, total - one])
    lengths = jnp.asarray(split_up(number_of, total, most, lean), jnp.int32)
    pairs = (number_of - 1) // 2
    source_of, sink = lengths[1:1 + 2 * pairs:2], lengths[2:2 + 2 * pairs:2]
    slack = jnp.minimum(source_of - 1, most - sink)
    shifted = jax.random.randint(jax.random.fold_in(own_key, 1), (pairs,), 0, 1 << 20) % (slack + 1)
    lengths = lengths.at[1:1 + 2 * pairs:2].set(source_of - shifted).at[2:2 + 2 * pairs:2].set(sink + shifted)
    return lengths[jax.random.permutation(jax.random.fold_in(own_key, 2), number_of)]


def gaussian(own_key, extent, width, limit, cuts=(), kind=jnp.bfloat16):
    gain = steps_of(own_key, extent, cuts, -0.22, 0.18) if cuts else 1.0
    values = jax.random.normal(own_key, extent, jnp.float32) * width * gain
    return jnp.minimum(jnp.maximum(values, -limit), limit).astype(kind)


def setup_inputs(seed: int = 0, part: int = 0) -> dict:
    arg_keys = jax.random.split(jax.random.key(seed), 10)
    part_splits = jax.random.split(jax.random.fold_in(arg_keys[9], part), 10)
    queries = draw_queries(jax.random.fold_in(jax.random.fold_in(arg_keys[9], part), 71), part)
    prefix_kv = draw_prefix_kv(jax.random.fold_in(jax.random.fold_in(arg_keys[9], part), 71), part)
    suffix_kv = draw_suffix_kv(jax.random.fold_in(jax.random.fold_in(arg_keys[9], part), 71), part)
    suffix_len = ragged_sizes(part_splits[3], REQS, REQS * SUFFIX // 2, SUFFIX, 2).astype(jnp.int32)
    residual = gaussian(part_splits[4], (REQS, D), 0.5, 3.0, ((0, 2),))
    out_weight = gaussian(arg_keys[5], (D, D), D ** -0.5, 0.0625, ((0, 8),))
    adapter_pages = draw_adapter_pages(jax.random.fold_in(arg_keys[9], 71), part)
    adapter_ids = draw_adapter_ids(jax.random.fold_in(jax.random.fold_in(arg_keys[9], part), 71), part)
    pool_slot = jax.random.permutation(arg_keys[8], ADAPTERS).astype(jnp.int32)
    return {"queries": queries, "prefix_kv": prefix_kv, "suffix_kv": suffix_kv, "suffix_len": suffix_len, "residual": residual, "out_weight": out_weight, "adapter_pages": adapter_pages, "adapter_ids": adapter_ids, "pool_slot": pool_slot}


def reference(queries, prefix_kv, suffix_kv, suffix_len, residual, out_weight, adapter_pages, adapter_ids, pool_slot):
    per_slot = HEADS // KV_SLOTS
    score_scale = HEAD_DIM ** -0.5
    query_rows = queries.astype(jnp.float32).reshape(REQS, KV_SLOTS, per_slot, HEAD_DIM)
    prefix_keys = prefix_kv[:, 0].astype(jnp.float32)
    prefix_vals = prefix_kv[:, 1].astype(jnp.float32)
    suffix_keys = suffix_kv[:, :, 0].astype(jnp.float32)
    suffix_vals = suffix_kv[:, :, 1].astype(jnp.float32)
    prefix_scores = jnp.einsum("rsgd,spd->rsgp", query_rows, prefix_keys) * score_scale
    suffix_scores = jnp.einsum("rsgd,rsjd->rsgj", query_rows, suffix_keys) * score_scale
    live_mask = (jnp.arange(SUFFIX)[None, :] < suffix_len[:, None])[:, None, None, :]
    suffix_scores = jnp.where(live_mask, suffix_scores, jnp.float32(-1e30))
    peak = jnp.maximum(jnp.max(prefix_scores, -1, keepdims=True), jnp.max(suffix_scores, -1, keepdims=True))
    prefix_exp = jnp.exp(prefix_scores - peak)
    suffix_exp = jnp.where(live_mask, jnp.exp(suffix_scores - peak), jnp.float32(0.0))
    denominator = jnp.sum(prefix_exp, -1, keepdims=True) + jnp.sum(suffix_exp, -1, keepdims=True)
    prefix_weight = lax.optimization_barrier((prefix_exp / denominator).astype(jnp.bfloat16)).astype(jnp.float32)
    suffix_weight = lax.optimization_barrier((suffix_exp / denominator).astype(jnp.bfloat16)).astype(jnp.float32)
    mixed = jnp.einsum("rsgp,spd->rsgd", prefix_weight, prefix_vals)
    mixed = mixed + jnp.einsum("rsgj,rsjd->rsgd", suffix_weight, suffix_vals)
    attended = lax.optimization_barrier(mixed.reshape(REQS, D).astype(jnp.bfloat16))
    page_rows = adapter_pages[pool_slot[adapter_ids]]
    shrink = jnp.einsum("ri,rki->rk", attended.astype(jnp.float32), page_rows[:, 0].astype(jnp.float32))
    low_rank = lax.optimization_barrier(shrink.astype(jnp.bfloat16))
    expanded = jnp.einsum("rk,rkc->rc", low_rank.astype(jnp.float32), page_rows[:, 1].astype(jnp.float32))
    base = jnp.dot(attended, out_weight, preferred_element_type=jnp.float32)
    return (residual.astype(jnp.float32) + base + expanded).astype(jnp.bfloat16)
```

```python
import functools
import math

import jax
import jax.numpy as jnp
from jax import lax
from jax.experimental import pallas as pl
from jax.experimental.pallas import tpu as pltpu
from jax.sharding import PartitionSpec as P

F32 = jnp.float32
BF16 = jnp.bfloat16
LOG2E = 1.4426950408889634
ANY = pl.BlockSpec(memory_space=pl.ANY)
VMEM = pl.BlockSpec(memory_space=pltpu.VMEM)
SMEM = pl.BlockSpec(memory_space=pltpu.SMEM)
MIB = 1 << 20
DISTINCT = 8


def nt_dot(a, b):
    return lax.dot_general(a, b, (((1,), (1,)), ((), ())), preferred_element_type=F32)


def nn_dot(a, b):
    return jnp.dot(a, b, preferred_element_type=F32)


def distinct_list(ids_ref, pool_slot_ref, seen, list_id, list_pos):
    rows = ids_ref.shape[0]
    count = pool_slot_ref.shape[0]

    @pl.loop(0, count)
    def _(i):
        seen[i] = 0

    for j in range(DISTINCT):
        list_id[j] = -1
        list_pos[j] = 0

    def step(r, found):
        one = ids_ref[r]
        fresh = (seen[one] == 0) & (found < DISTINCT)

        @pl.when(fresh)
        def _():
            seen[one] = 1
            list_id[found] = one
            list_pos[found] = pool_slot_ref[one]

        return found + fresh.astype(jnp.int32)

    lax.fori_loop(0, rows, step, jnp.int32(0))


def attend_kernel(
    n_z,
    len_ref,
    q_ref,
    prefix_ref,
    suffix_ref,
    weight_ref,
    att_ref,
    *rest,
):
    piece_refs = rest[:n_z]
    (kv, suf, wbuf, scores, tail, rowbuf, peak, total, acc, sem_kv, sem_suf, sem_w) = rest[n_z:]
    rows = q_ref.shape[0]
    head_dim = prefix_ref.shape[3]
    heads = q_ref.shape[1] // head_dim
    n_q = rows * heads
    tokens = prefix_ref.shape[2]
    span = suffix_ref.shape[3]
    width = piece_refs[0].shape[1]
    me = lax.axis_index("tensor")
    z, y = me // 2, me % 2
    scale2 = float(head_dim) ** -0.5 * LOG2E

    n_part = 4
    part = tokens // n_part
    kv_copies = [
        [
            pltpu.make_async_copy(
                prefix_ref.at[0, i, pl.ds(j * part, part)],
                kv.at[i, pl.ds(j * part, part)],
                sem_kv.at[i, j],
            )
            for j in range(n_part)
        ]
        for i in range(2)
    ]
    n_sgrp = 4
    sgrp = rows // n_sgrp
    suf_copies = [
        pltpu.make_async_copy(
            suffix_ref.at[pl.ds(j * sgrp, sgrp), 0], suf.at[pl.ds(j * sgrp, sgrp)], sem_suf.at[j]
        )
        for j in range(n_sgrp)
    ]
    w_copies = []
    for k in range(n_z):
        column = pl.multiple_of(((z ^ k) * 2 + (1 - y)) * width, width)
        w_copies.append(
            pltpu.make_async_copy(weight_ref.at[:, pl.ds(column, width)], wbuf.at[k], sem_w.at[k])
        )
    for c in kv_copies[0] + suf_copies + kv_copies[1]:
        c.start()

    for h in range(heads):
        rowbuf[pl.ds(h, rows, stride=heads), :] = q_ref[:, h * head_dim : (h + 1) * head_dim].astype(F32)
    query = rowbuf[...].astype(BF16)
    peak[...] = jnp.full(peak.shape, -3.0e38, F32)

    chunk = 1024
    for j in range(n_part):
        kv_copies[0][j].wait()
        if j == 0:
            for c in w_copies[:1]:
                c.start()

        @pl.loop(0, part // chunk)
        def _(i):
            base = pl.multiple_of(j * part + i * chunk, chunk)
            best = peak[...]
            for b in range(chunk // 256):
                block = nt_dot(query, kv[0, pl.ds(base + b * 256, 256), :])
                scores[:, pl.ds(base + b * 256, 256)] = block
                best = jnp.maximum(best, jnp.maximum(block[:, :128], block[:, 128:]))
            peak[...] = best

    for c in w_copies[1:]:
        c.start()

    lanes = lax.broadcasted_iota(jnp.int32, (heads, span), 1)
    for j in range(n_sgrp):
        suf_copies[j].wait()
        for i in range(j * sgrp // 2, (j + 1) * sgrp // 2):
            keys = suf[2 * i : 2 * i + 2, 0].reshape(2 * span, head_dim)
            both = nt_dot(query[2 * heads * i : 2 * heads * (i + 1)], keys)
            for a in range(2):
                mine = both[a * heads : (a + 1) * heads, a * span : (a + 1) * span]
                row = 2 * i + a
                tail[row * heads : (row + 1) * heads, :] = jnp.where(lanes < len_ref[row], mine, -1.0e30)
    best = peak[...]
    for b in range(span // 128):
        best = jnp.maximum(best, tail[:, b * 128 : (b + 1) * 128])
    top = jnp.max(best, axis=1, keepdims=True)
    peak[...] = jnp.broadcast_to(top, peak.shape)

    for j in range(n_part):
        kv_copies[1][j].wait()
    total[...] = jnp.zeros(total.shape, F32)
    acc[...] = jnp.zeros(acc.shape, F32)

    @pl.loop(0, tokens // chunk)
    def _(i):
        base = pl.multiple_of(i * chunk, chunk)
        high = peak[...]
        summed = total[...]
        parts = []
        for b in range(chunk // 128):
            e = jnp.exp2((scores[:, pl.ds(base + b * 128, 128)] - high) * scale2)
            summed = summed + e
            parts.append(e.astype(BF16))
        total[...] = summed
        acc[...] += nn_dot(jnp.concatenate(parts, axis=1), kv[1, pl.ds(base, chunk), :])

    zeros = jnp.zeros((heads, span), F32)
    for i in range(rows // 2):
        lo = 2 * heads * i
        high = jnp.concatenate([peak[lo : lo + 2 * heads, :]] * (span // 128), axis=1)
        e = jnp.exp2((tail[lo : lo + 2 * heads, :] - high) * scale2)
        part_sum = e[:, :128]
        for b in range(1, span // 128):
            part_sum = part_sum + e[:, b * 128 : (b + 1) * 128]
        total[lo : lo + 2 * heads, :] += part_sum
        diag = jnp.concatenate(
            [
                jnp.concatenate([e[:heads], zeros], axis=1),
                jnp.concatenate([zeros, e[heads:]], axis=1),
            ],
            axis=0,
        ).astype(BF16)
        vals = suf[2 * i : 2 * i + 2, 1].reshape(2 * span, head_dim)
        acc[lo : lo + 2 * heads, :] += nn_dot(diag, vals)

    norm = jnp.sum(total[...], axis=1, keepdims=True)
    rowbuf[...] = acc[...] / norm
    for h in range(heads):
        att_ref[:, h * head_dim : (h + 1) * head_dim] = rowbuf[pl.ds(h, rows, stride=heads), :].astype(BF16)
    attended = att_ref[...]
    for k in range(n_z):
        w_copies[k].wait()
        piece_refs[k][...] = nn_dot(attended, wbuf[k]).astype(BF16)


def attend(suffix_len, queries, prefix_kv, suffix_kv, out_weight, n_tensor):
    rows = queries.shape[0]
    n_z = n_tensor // 2
    width = out_weight.shape[1] // n_tensor
    tokens, head_dim = prefix_kv.shape[2:]
    n_q = rows * queries.shape[1] // head_dim
    span = suffix_kv.shape[3]
    return pl.pallas_call(
        functools.partial(attend_kernel, n_z),
        out_shape=[jax.ShapeDtypeStruct(queries.shape, BF16)]
        + [jax.ShapeDtypeStruct((rows, width), BF16)] * n_z,
        in_specs=[SMEM, VMEM, ANY, ANY, ANY],
        out_specs=[VMEM] * (1 + n_z),
        scratch_shapes=[
            pltpu.VMEM((2, tokens, head_dim), BF16),
            pltpu.VMEM((rows, 2, span, head_dim), BF16),
            pltpu.VMEM((n_z, out_weight.shape[0], width), BF16),
            pltpu.VMEM((n_q, tokens), F32),
            pltpu.VMEM((n_q, span), F32),
            pltpu.VMEM((n_q, head_dim), F32),
            pltpu.VMEM((n_q, 128), F32),
            pltpu.VMEM((n_q, 128), F32),
            pltpu.VMEM((n_q, head_dim), F32),
            pltpu.SemaphoreType.DMA((2, 4)),
            pltpu.SemaphoreType.DMA((4,)),
            pltpu.SemaphoreType.DMA((n_z,)),
        ],
        compiler_params=pltpu.CompilerParams(vmem_limit_bytes=48 * MIB),
        cost_estimate=pl.CostEstimate(
            flops=2 * 2 * n_q * tokens * head_dim,
            bytes_accessed=16 * MIB,
            transcendentals=n_q * tokens,
        ),
        name="attend",
    )(suffix_len, queries, prefix_kv, suffix_kv, out_weight)


def own_kernel(n_z, att_ref, weight_ref, *rest):
    piece_refs = rest[:n_z]
    wbuf, sem_w = rest[n_z:]
    width = piece_refs[0].shape[1]
    me = lax.axis_index("tensor")
    z, y = me // 2, me % 2
    copies = []
    for k in range(n_z):
        column = pl.multiple_of(((z ^ k) * 2 + y) * width, width)
        copies.append(
            pltpu.make_async_copy(weight_ref.at[:, pl.ds(column, width)], wbuf.at[k], sem_w.at[k])
        )
    order = list(range(1, n_z)) + [0]
    for k in order:
        copies[k].start()
    attended = att_ref[...]
    for k in order:
        copies[k].wait()
        piece_refs[k][...] = nn_dot(attended, wbuf[k])


def own_part(attended, out_weight, n_tensor):
    rows = attended.shape[0]
    n_z = n_tensor // 2
    width = out_weight.shape[1] // n_tensor
    return pl.pallas_call(
        functools.partial(own_kernel, n_z),
        out_shape=[jax.ShapeDtypeStruct((rows, width), F32)] * n_z,
        in_specs=[VMEM, ANY],
        out_specs=[VMEM] * n_z,
        scratch_shapes=[
            pltpu.VMEM((n_z, out_weight.shape[0], width), BF16),
            pltpu.SemaphoreType.DMA((n_z,)),
        ],
        compiler_params=pltpu.CompilerParams(vmem_limit_bytes=24 * MIB),
        cost_estimate=pl.CostEstimate(
            flops=2 * rows * out_weight.shape[0] * width * n_z,
            bytes_accessed=8 * MIB,
            transcendentals=0,
        ),
        name="own_part",
    )(attended, out_weight)


def collect_kernel(ids_ref, slot_ref, pages_ref, shrink_ref, expand_ref, seen, list_id, list_pos, sem):
    distinct_list(ids_ref, slot_ref, seen, list_id, list_pos)
    pool = pages_ref.shape[0]
    me = lax.axis_index("req")
    for wait in (False, True):
        for i, out in enumerate((shrink_ref, expand_ref)):
            for j in range(DISTINCT):
                pos = list_pos[j]

                @pl.when(pos // pool == me)
                def _():
                    copy = pltpu.make_async_copy(pages_ref.at[pos % pool, i], out.at[j], sem.at[i, j])
                    if wait:
                        copy.wait()
                    else:
                        copy.start()


def collect_pages(ids, pool_slot, pages):
    shape = jax.ShapeDtypeStruct((DISTINCT,) + pages.shape[2:], BF16)
    return pl.pallas_call(
        collect_kernel,
        out_shape=[shape, shape],
        in_specs=[SMEM, SMEM, ANY],
        out_specs=[ANY, ANY],
        scratch_shapes=[
            pltpu.SMEM((pool_slot.shape[0],), jnp.int32),
            pltpu.SMEM((DISTINCT,), jnp.int32),
            pltpu.SMEM((DISTINCT,), jnp.int32),
            pltpu.SemaphoreType.DMA((2, DISTINCT)),
        ],
        cost_estimate=pl.CostEstimate(flops=0, bytes_accessed=4 * MIB, transcendentals=0),
        name="collect_pages",
    )(ids, pool_slot, pages)


def load_pages(half, pages_ref, other_ref, buf, sem, list_pos):
    pool = pages_ref.shape[0]
    me = lax.axis_index("req")
    rank = pages_ref.shape[2]
    for wait in (False, True):
        for j in range(DISTINCT):
            pos = list_pos[j]
            for mine in (True, False):

                @pl.when((pos // pool == me) == mine)
                def _():
                    source = pages_ref.at[pos % pool, half] if mine else other_ref.at[j]
                    copy = pltpu.make_async_copy(source, buf.at[pl.ds(j * rank, rank)], sem.at[j])
                    if wait:
                        copy.wait()
                    else:
                        copy.start()


def shrink_kernel(
    ids_ref, slot_ref, column_ref, att_ref, pages_ref, other_ref, out_ref, buf, seen, list_id, list_pos, sem
):
    distinct_list(ids_ref, slot_ref, seen, list_id, list_pos)
    load_pages(0, pages_ref, other_ref, buf, sem, list_pos)
    rank = pages_ref.shape[2]
    low = nt_dot(att_ref[...], buf[...])
    column = column_ref[...]
    lane_slot = lax.broadcasted_iota(jnp.int32, (column.shape[0], 128), 1) // rank
    per_tile = 128 // rank
    picked = jnp.zeros((column.shape[0], 128), F32)
    for j in range(DISTINCT):
        tile, place = j // per_tile, j % per_tile
        hit = (column == list_id[j]) & (lane_slot == place)
        picked = jnp.where(hit, low[:, tile * 128 : (tile + 1) * 128], picked)
    out_ref[...] = picked


def expand_kernel(
    ids_ref,
    slot_ref,
    column_ref,
    low_ref,
    pages_ref,
    other_ref,
    own_ref,
    recv_ref,
    residual_ref,
    out_ref,
    buf,
    res,
    seen,
    list_id,
    list_pos,
    sem,
    sem_res,
):
    distinct_list(ids_ref, slot_ref, seen, list_id, list_pos)
    width = own_ref.shape[1]
    me = lax.axis_index("tensor")
    fetch = pltpu.make_async_copy(
        residual_ref.at[:, pl.ds(pl.multiple_of(me * width, width), width)], res, sem_res.at[0]
    )
    fetch.start()
    load_pages(1, pages_ref, other_ref, buf, sem, list_pos)
    rank = pages_ref.shape[2]
    column = column_ref[...]
    per_tile = 128 // rank
    lane_slot = lax.broadcasted_iota(jnp.int32, (column.shape[0], 128), 1) // rank
    low = low_ref[...]
    tiles = []
    for tile in range(DISTINCT // per_tile):
        hit = jnp.zeros(low.shape, jnp.bool_)
        for place in range(per_tile):
            hit = hit | ((column == list_id[tile * per_tile + place]) & (lane_slot == place))
        tiles.append(jnp.where(hit, low, 0.0).astype(BF16))
    expanded = nn_dot(jnp.concatenate(tiles, axis=1), buf[...])
    fetch.wait()
    out_ref[...] = expanded + own_ref[...] + recv_ref[...].astype(F32) + res[...].astype(F32)


def adapter_scratch(pages, pool_slot):
    return [
        pltpu.SMEM((pool_slot.shape[0],), jnp.int32),
        pltpu.SMEM((DISTINCT,), jnp.int32),
        pltpu.SMEM((DISTINCT,), jnp.int32),
        pltpu.SemaphoreType.DMA((DISTINCT,)),
    ]


def shrink_part(ids, pool_slot, column, attended, pages, other):
    rows = attended.shape[0]
    return pl.pallas_call(
        shrink_kernel,
        out_shape=jax.ShapeDtypeStruct((rows, 128), F32),
        in_specs=[SMEM, SMEM, VMEM, VMEM, ANY, ANY],
        out_specs=VMEM,
        scratch_shapes=[pltpu.VMEM((DISTINCT * pages.shape[2], pages.shape[3]), BF16)]
        + adapter_scratch(pages, pool_slot),
        cost_estimate=pl.CostEstimate(flops=1 << 25, bytes_accessed=1 * MIB, transcendentals=0),
        name="shrink_part",
    )(ids, pool_slot, column, attended, pages, other)


def expand_part(ids, pool_slot, column, low, pages, other, own, recv, residual):
    rows, width = own.shape
    return pl.pallas_call(
        expand_kernel,
        out_shape=jax.ShapeDtypeStruct((rows, width), F32),
        in_specs=[SMEM, SMEM, VMEM, VMEM, ANY, ANY, VMEM, VMEM, ANY],
        out_specs=VMEM,
        scratch_shapes=[
            pltpu.VMEM((DISTINCT * pages.shape[2], pages.shape[3]), BF16),
            pltpu.VMEM((rows, width), BF16),
        ]
        + adapter_scratch(pages, pool_slot)
        + [pltpu.SemaphoreType.DMA((1,))],
        cost_estimate=pl.CostEstimate(flops=1 << 25, bytes_accessed=1 * MIB, transcendentals=0),
        name="expand_part",
    )(ids, pool_slot, column, low, pages, other, own, recv, residual)


def place_kernel(n_z, *refs):
    blocks = refs[: 2 * n_z]
    out_ref, sem = refs[2 * n_z :]
    width = blocks[0].shape[1]
    me = lax.axis_index("tensor")
    z, y = me // 2, me % 2
    copies = []
    for k in range(n_z):
        for other in range(2):
            where = (z ^ k) * 2 + (y ^ other)
            copies.append(
                pltpu.make_async_copy(
                    blocks[2 * k + other],
                    out_ref.at[:, pl.ds(pl.multiple_of(where * width, width), width)],
                    sem.at[2 * k + other],
                )
            )
    for c in copies:
        c.start()
    for c in copies:
        c.wait()


def place(blocks, n_tensor):
    rows, width = blocks[0].shape
    return pl.pallas_call(
        functools.partial(place_kernel, n_tensor // 2),
        out_shape=jax.ShapeDtypeStruct((rows, width * n_tensor), BF16),
        in_specs=[ANY] * n_tensor,
        out_specs=ANY,
        scratch_shapes=[pltpu.SemaphoreType.DMA((n_tensor,))],
        cost_estimate=pl.CostEstimate(flops=0, bytes_accessed=1 * MIB, transcendentals=0),
        name="place",
    )(*blocks)


def body(
    n_tensor,
    queries,
    prefix_kv,
    suffix_kv,
    suffix_len,
    residual,
    out_weight,
    adapter_pages,
    adapter_ids,
    pool_slot,
):
    n_z = n_tensor // 2

    def along_y(x):
        return lax.ppermute(x, "tensor", [(t, t ^ 1) for t in range(n_tensor)])

    def along_z(x, k):
        return lax.ppermute(x, "tensor", [(t, t ^ (2 * k)) for t in range(n_tensor)])

    def across(x):
        return lax.ppermute(x, "req", [(0, 1), (1, 0)])

    column = jnp.broadcast_to(adapter_ids[:, None], (adapter_ids.shape[0], 128))
    other_ids = across(adapter_ids)
    attended, *pieces = attend(suffix_len, queries, prefix_kv, suffix_kv, out_weight, n_tensor)
    send_order = list(range(1, n_z)) + [0]
    got_y = {k: along_y(pieces[k]) for k in send_order}
    found_shrink, found_expand = collect_pages(other_ids, pool_slot, adapter_pages)
    other_shrink = across(found_shrink)
    other_expand = across(found_expand)
    own = own_part(attended, out_weight, n_tensor)
    got_z = []
    for k in range(1, n_z):
        both = (got_y[k].astype(F32) + own[k]).astype(BF16)
        got_z.append(along_z(both, k))
    low = shrink_part(adapter_ids, pool_slot, column, attended, adapter_pages, other_shrink)
    low = low + along_y(low)
    for bit in range(int(math.log2(n_z))):
        low = low + along_z(low, 1 << bit)
    local = expand_part(
        adapter_ids, pool_slot, column, low, adapter_pages, other_expand, own[0], got_y[0], residual
    )
    for g in got_z:
        local = local + g.astype(F32)
    result = local.astype(BF16)
    blocks = []
    held = [result] + [along_z(result, k) for k in range(1, n_z)]
    for k in range(n_z):
        blocks += [held[k], along_y(held[k])]
    return place(blocks, n_tensor)


def solution(mesh):
    return jax.shard_map(
        functools.partial(body, mesh.shape["tensor"]),
        mesh=mesh,
        in_specs=(
            P(("group", "req"), "tensor"),
            P(("group", "tensor"), None, None, None),
            P(("group", "req"), "tensor", None, None, None),
            P(("group", "req")),
            P(("group", "req"), None),
            P("tensor", None),
            P("req", None, None, "tensor"),
            P(("group", "req")),
            P(),
        ),
        out_specs=P(("group", "req"), None),
        check_vma=False,
    )
```

```python
import functools

import jax
import jax.numpy as jnp
from jax import lax
from jax.experimental import pallas as pl
from jax.experimental.pallas import tpu as pltpu
from jax.sharding import PartitionSpec as P

F32 = jnp.float32
BF16 = jnp.bfloat16
LOG2E = 1.4426950408889634
ANY = pl.BlockSpec(memory_space=pl.ANY)
VMEM = pl.BlockSpec(memory_space=pltpu.VMEM)
SMEM = pl.BlockSpec(memory_space=pltpu.SMEM)
MIB = 1 << 20
DISTINCT = 8
ROOM = pltpu.CompilerParams(vmem_limit_bytes=54 * MIB)


def nt_dot(a, b):
    return lax.dot_general(a, b, (((1,), (1,)), ((), ())), preferred_element_type=F32)


def nn_dot(a, b):
    return jnp.dot(a, b, preferred_element_type=F32)


def distinct_list(ids_ref, pool_slot_ref, seen, list_id, list_pos):
    rows = ids_ref.shape[0]
    for i in range(pool_slot_ref.shape[0]):
        seen[i] = 0
    for j in range(DISTINCT + 1):
        list_id[j] = -1
        list_pos[j] = 0
    found = jnp.int32(0)
    for r in range(rows):
        one = ids_ref[r]
        fresh = 1 - seen[one]
        seen[one] = 1
        spot = jnp.minimum(found, DISTINCT)
        list_id[spot] = jnp.where(fresh == 1, one, list_id[spot])
        list_pos[spot] = jnp.where(fresh == 1, pool_slot_ref[one], list_pos[spot])
        found = found + fresh


def list_scratch(pool_slot):
    return [
        pltpu.SMEM((pool_slot.shape[0],), jnp.int32),
        pltpu.SMEM((DISTINCT + 1,), jnp.int32),
        pltpu.SMEM((DISTINCT + 1,), jnp.int32),
    ]


def page_copies(pages_ref, outs, list_pos, sem, wait):
    pool = pages_ref.shape[0]
    me = lax.axis_index("req")
    for j in range(DISTINCT):
        pos = list_pos[j]

        @pl.when(pos // pool == me)
        def _():
            for i, out in enumerate(outs):
                copy = pltpu.make_async_copy(pages_ref.at[pos % pool, i], out.at[j], sem.at[i, j])
                if wait:
                    copy.wait()
                else:
                    copy.start()


def attend_kernel(
    n_z,
    len_ref,
    ids_ref,
    slot_ref,
    q_ref,
    prefix_ref,
    suffix_ref,
    weight_ref,
    pages_ref,
    att_ref,
    shrink_ref,
    expand_ref,
    row_slot_ref,
    slot_mine_ref,
    *rest,
):
    piece_refs = rest[:n_z]
    (
        kv,
        suf,
        wbuf,
        scores,
        tail,
        rowbuf,
        peak,
        total,
        acc,
        seen,
        list_id,
        list_pos,
        sem_kv,
        sem_suf,
        sem_w,
        sem_page,
    ) = rest[n_z:]
    rows = q_ref.shape[0]
    head_dim = prefix_ref.shape[3]
    heads = q_ref.shape[1] // head_dim
    n_q = rows * heads
    tokens = prefix_ref.shape[2]
    span = suffix_ref.shape[3]
    width = piece_refs[0].shape[1]
    me = lax.axis_index("tensor")
    z, y = me // 2, me % 2
    scale2 = float(head_dim) ** -0.5 * LOG2E

    n_part = 4
    part = tokens // n_part
    kv_copies = [
        [
            pltpu.make_async_copy(
                prefix_ref.at[0, i, pl.ds(j * part, part)],
                kv.at[i, pl.ds(j * part, part)],
                sem_kv.at[i, j],
            )
            for j in range(n_part)
        ]
        for i in range(2)
    ]
    n_sgrp = 4
    sgrp = rows // n_sgrp
    suf_copies = [
        pltpu.make_async_copy(
            suffix_ref.at[pl.ds(j * sgrp, sgrp), 0], suf.at[pl.ds(j * sgrp, sgrp)], sem_suf.at[j]
        )
        for j in range(n_sgrp)
    ]
    w_copies = []
    for k in range(n_z):
        column = pl.multiple_of(((z ^ k) * 2 + (1 - y)) * width, width)
        w_copies.append(
            pltpu.make_async_copy(weight_ref.at[:, pl.ds(column, width)], wbuf.at[k], sem_w.at[k])
        )
    for c in kv_copies[0] + suf_copies + kv_copies[1]:
        c.start()
    distinct_list(ids_ref, slot_ref, seen, list_id, list_pos)
    page_copies(pages_ref, (shrink_ref, expand_ref), list_pos, sem_page, False)
    row_index = lax.broadcasted_iota(jnp.int32, (rows, 128), 0)
    row_id = jnp.full((rows, 128), -2, jnp.int32)
    for r in range(rows):
        row_id = jnp.where(row_index == r, ids_ref[r], row_id)
    row_slot = jnp.full((rows, 128), -1, jnp.int32)
    slot_index = lax.broadcasted_iota(jnp.int32, (DISTINCT, 128), 0)
    slot_mine = jnp.zeros((DISTINCT, 128), jnp.int32)
    mine = lax.axis_index("req")
    for j in range(DISTINCT):
        row_slot = jnp.where(row_id == list_id[j], j, row_slot)
        owned = (list_pos[j] // pages_ref.shape[0] == mine).astype(jnp.int32)
        slot_mine = jnp.where(slot_index == j, owned, slot_mine)
    row_slot_ref[...] = row_slot
    slot_mine_ref[...] = slot_mine

    for h in range(heads):
        rowbuf[pl.ds(h, rows, stride=heads), :] = q_ref[:, h * head_dim : (h + 1) * head_dim].astype(F32)
    query = rowbuf[...].astype(BF16)
    peak[...] = jnp.full(peak.shape, -3.0e38, F32)

    chunk = 1024
    for j in range(n_part):
        kv_copies[0][j].wait()
        if j == 0:
            for c in w_copies[:1]:
                c.start()

        @pl.loop(0, part // chunk)
        def _(i):
            base = pl.multiple_of(j * part + i * chunk, chunk)
            best = peak[...]
            for b in range(chunk // 256):
                block = nt_dot(query, kv[0, pl.ds(base + b * 256, 256), :])
                scores[:, pl.ds(base + b * 256, 256)] = block
                best = jnp.maximum(best, jnp.maximum(block[:, :128], block[:, 128:]))
            peak[...] = best

    for c in w_copies[1:]:
        c.start()

    lanes = lax.broadcasted_iota(jnp.int32, (heads, span), 1)
    for j in range(n_sgrp):
        suf_copies[j].wait()
        for i in range(j * sgrp // 2, (j + 1) * sgrp // 2):
            keys = suf[2 * i : 2 * i + 2, 0].reshape(2 * span, head_dim)
            both = nt_dot(query[2 * heads * i : 2 * heads * (i + 1)], keys)
            for a in range(2):
                mine = both[a * heads : (a + 1) * heads, a * span : (a + 1) * span]
                row = 2 * i + a
                tail[row * heads : (row + 1) * heads, :] = jnp.where(lanes < len_ref[row], mine, -1.0e30)
    best = peak[...]
    for b in range(span // 128):
        best = jnp.maximum(best, tail[:, b * 128 : (b + 1) * 128])
    top = jnp.max(best, axis=1, keepdims=True)
    peak[...] = jnp.broadcast_to(top, peak.shape)

    for j in range(n_part):
        kv_copies[1][j].wait()
    total[...] = jnp.zeros(total.shape, F32)
    acc[...] = jnp.zeros(acc.shape, F32)

    @pl.loop(0, tokens // chunk)
    def _(i):
        base = pl.multiple_of(i * chunk, chunk)
        high = peak[...]
        summed = total[...]
        parts = []
        for b in range(chunk // 128):
            e = jnp.exp2((scores[:, pl.ds(base + b * 128, 128)] - high) * scale2)
            summed = summed + e
            parts.append(e.astype(BF16))
        total[...] = summed
        acc[...] += nn_dot(jnp.concatenate(parts, axis=1), kv[1, pl.ds(base, chunk), :])

    zeros = jnp.zeros((heads, span), F32)
    for i in range(rows // 2):
        lo = 2 * heads * i
        high = jnp.concatenate([peak[lo : lo + 2 * heads, :]] * (span // 128), axis=1)
        e = jnp.exp2((tail[lo : lo + 2 * heads, :] - high) * scale2)
        part_sum = e[:, :128]
        for b in range(1, span // 128):
            part_sum = part_sum + e[:, b * 128 : (b + 1) * 128]
        total[lo : lo + 2 * heads, :] += part_sum
        diag = jnp.concatenate(
            [
                jnp.concatenate([e[:heads], zeros], axis=1),
                jnp.concatenate([zeros, e[heads:]], axis=1),
            ],
            axis=0,
        ).astype(BF16)
        vals = suf[2 * i : 2 * i + 2, 1].reshape(2 * span, head_dim)
        acc[lo : lo + 2 * heads, :] += nn_dot(diag, vals)

    norm = jnp.sum(total[...], axis=1, keepdims=True)
    rowbuf[...] = acc[...] / norm
    for h in range(heads):
        att_ref[:, h * head_dim : (h + 1) * head_dim] = rowbuf[pl.ds(h, rows, stride=heads), :].astype(BF16)
    attended = att_ref[...]
    for k in range(n_z):
        w_copies[k].wait()
        piece_refs[k][...] = nn_dot(attended, wbuf[k]).astype(BF16)
    page_copies(pages_ref, (shrink_ref, expand_ref), list_pos, sem_page, True)


def attend(suffix_len, ids, pool_slot, queries, prefix_kv, suffix_kv, out_weight, pages, n_tensor):
    rows = queries.shape[0]
    n_z = n_tensor // 2
    width = out_weight.shape[1] // n_tensor
    tokens, head_dim = prefix_kv.shape[2:]
    n_q = rows * queries.shape[1] // head_dim
    span = suffix_kv.shape[3]
    return pl.pallas_call(
        functools.partial(attend_kernel, n_z),
        out_shape=[
            jax.ShapeDtypeStruct(queries.shape, BF16),
            jax.ShapeDtypeStruct((DISTINCT,) + pages.shape[2:], BF16),
            jax.ShapeDtypeStruct((DISTINCT,) + pages.shape[2:], BF16),
            jax.ShapeDtypeStruct((rows, 128), jnp.int32),
            jax.ShapeDtypeStruct((DISTINCT, 128), jnp.int32),
        ]
        + [jax.ShapeDtypeStruct((rows, width), BF16)] * n_z,
        in_specs=[SMEM, SMEM, SMEM, VMEM, ANY, ANY, ANY, ANY],
        out_specs=[VMEM] * (5 + n_z),
        scratch_shapes=[
            pltpu.VMEM((2, tokens, head_dim), BF16),
            pltpu.VMEM((rows, 2, span, head_dim), BF16),
            pltpu.VMEM((n_z, out_weight.shape[0], width), BF16),
            pltpu.VMEM((n_q, tokens), F32),
            pltpu.VMEM((n_q, span), F32),
            pltpu.VMEM((n_q, head_dim), F32),
            pltpu.VMEM((n_q, 128), F32),
            pltpu.VMEM((n_q, 128), F32),
            pltpu.VMEM((n_q, head_dim), F32),
        ]
        + list_scratch(pool_slot)
        + [
            pltpu.SemaphoreType.DMA((2, 4)),
            pltpu.SemaphoreType.DMA((4,)),
            pltpu.SemaphoreType.DMA((n_z,)),
            pltpu.SemaphoreType.DMA((2, DISTINCT)),
        ],
        compiler_params=ROOM,
        cost_estimate=pl.CostEstimate(
            flops=2 * 2 * n_q * tokens * head_dim,
            bytes_accessed=16 * MIB,
            transcendentals=n_q * tokens,
        ),
        name="attend",
    )(suffix_len, ids, pool_slot, queries, prefix_kv, suffix_kv, out_weight, pages)


def own_kernel(n_z, att_ref, weight_ref, after_ref, *rest):
    piece_refs = rest[:n_z]
    wbuf, sem_w = rest[n_z:]
    width = piece_refs[0].shape[1]
    me = lax.axis_index("tensor")
    z, y = me // 2, me % 2
    copies = []
    for k in range(n_z):
        column = pl.multiple_of(((z ^ k) * 2 + y) * width, width)
        copies.append(
            pltpu.make_async_copy(weight_ref.at[:, pl.ds(column, width)], wbuf.at[k], sem_w.at[k])
        )
    order = list(range(1, n_z)) + [0]
    for k in order:
        copies[k].start()
    attended = att_ref[...]
    for k in order:
        copies[k].wait()
        piece_refs[k][...] = nn_dot(attended, wbuf[k])


def own_part(attended, out_weight, after, n_tensor):
    rows = attended.shape[0]
    n_z = n_tensor // 2
    width = out_weight.shape[1] // n_tensor
    return pl.pallas_call(
        functools.partial(own_kernel, n_z),
        out_shape=[jax.ShapeDtypeStruct((rows, width), F32)] * n_z,
        in_specs=[VMEM, ANY, ANY],
        out_specs=[VMEM] * n_z,
        scratch_shapes=[
            pltpu.VMEM((n_z, out_weight.shape[0], width), BF16),
            pltpu.SemaphoreType.DMA((n_z,)),
        ],
        compiler_params=ROOM,
        cost_estimate=pl.CostEstimate(
            flops=2 * rows * out_weight.shape[0] * width * n_z,
            bytes_accessed=8 * MIB,
            transcendentals=0,
        ),
        name="own_part",
    )(attended, out_weight, after)


def collect_kernel(ids_ref, slot_ref, pages_ref, shrink_ref, expand_ref, seen, list_id, list_pos, sem):
    distinct_list(ids_ref, slot_ref, seen, list_id, list_pos)
    for wait in (False, True):
        page_copies(pages_ref, (shrink_ref, expand_ref), list_pos, sem, wait)


def collect_pages(ids, pool_slot, pages):
    shape = jax.ShapeDtypeStruct((DISTINCT,) + pages.shape[2:], BF16)
    return pl.pallas_call(
        collect_kernel,
        out_shape=[shape, shape],
        in_specs=[SMEM, SMEM, ANY],
        out_specs=[VMEM, VMEM],
        scratch_shapes=list_scratch(pool_slot) + [pltpu.SemaphoreType.DMA((2, DISTINCT))],
        compiler_params=ROOM,
        cost_estimate=pl.CostEstimate(flops=0, bytes_accessed=2 * MIB, transcendentals=0),
        name="collect_pages",
    )(ids, pool_slot, pages)


def merged(own_ref, other_ref, slot_mine):
    rank = own_ref.shape[1]
    tiles = []
    for j in range(DISTINCT):
        hit = jnp.broadcast_to(slot_mine[j : j + 1, :1], (rank, 1)) == 1
        tiles.append(jnp.where(hit, own_ref[j].astype(F32), other_ref[j].astype(F32)).astype(BF16))
    return jnp.concatenate(tiles, axis=0)


def lane_place(shape, rank):
    return lax.broadcasted_iota(jnp.int32, shape, 1) // rank


def shrink_kernel(att_ref, row_slot_ref, slot_mine_ref, own_ref, other_ref, out_ref):
    rank = own_ref.shape[1]
    per_tile = 128 // rank
    low = nt_dot(att_ref[...], merged(own_ref, other_ref, slot_mine_ref[...]))
    row_slot = row_slot_ref[...]
    place = lane_place(row_slot.shape, rank)
    picked = jnp.zeros(row_slot.shape, F32)
    for tile in range(DISTINCT // per_tile):
        hit = row_slot == place + tile * per_tile
        picked = jnp.where(hit, low[:, tile * 128 : (tile + 1) * 128], picked)
    out_ref[...] = picked


def shrink_part(attended, row_slot, slot_mine, own, other):
    rows = attended.shape[0]
    return pl.pallas_call(
        shrink_kernel,
        out_shape=jax.ShapeDtypeStruct((rows, 128), F32),
        in_specs=[VMEM] * 5,
        out_specs=VMEM,
        compiler_params=ROOM,
        cost_estimate=pl.CostEstimate(flops=1 << 25, bytes_accessed=2 * MIB, transcendentals=0),
        name="shrink_part",
    )(attended, row_slot, slot_mine, own, other)


def finish_kernel(n_z, *refs):
    row_slot_ref, slot_mine_ref, own_ref, other_ref, rank_ref, rank_y_ref = refs[:6]
    base_ref, base_y_ref, residual_ref = refs[6:9]
    moved = refs[9 : 9 + n_z - 1]
    out_ref = refs[9 + n_z - 1]
    rank = own_ref.shape[1]
    per_tile = 128 // rank
    width = base_ref.shape[1]
    me = lax.axis_index("tensor")
    low = rank_ref[...] + rank_y_ref[...]
    for ref in moved:
        low = low + ref[:, width:].astype(F32)
    row_slot = row_slot_ref[...]
    place = lane_place(row_slot.shape, rank)
    tiles = []
    for tile in range(DISTINCT // per_tile):
        tiles.append(jnp.where(row_slot == place + tile * per_tile, low, 0.0).astype(BF16))
    total = nn_dot(jnp.concatenate(tiles, axis=1), merged(own_ref, other_ref, slot_mine_ref[...]))
    column = pl.ds(pl.multiple_of(me * width, width), width)
    total = total + (residual_ref[:, column].astype(F32) + (base_ref[...] + base_y_ref[...].astype(F32)))
    for ref in moved:
        total = total + ref[:, :width].astype(F32)
    out_ref[...] = total.astype(BF16)


def finish(n_z, *operands):
    rows, width = operands[6].shape
    return pl.pallas_call(
        functools.partial(finish_kernel, n_z),
        out_shape=jax.ShapeDtypeStruct((rows, width), BF16),
        in_specs=[VMEM] * len(operands),
        out_specs=VMEM,
        compiler_params=ROOM,
        cost_estimate=pl.CostEstimate(flops=1 << 25, bytes_accessed=2 * MIB, transcendentals=0),
        name="finish",
    )(*operands)


def place_kernel(n_z, *refs):
    blocks = refs[: 2 * n_z]
    out_ref = refs[2 * n_z]
    width = blocks[0].shape[1]
    me = lax.axis_index("tensor")
    z, y = me // 2, me % 2
    for k in range(n_z):
        for other in range(2):
            where = (z ^ k) * 2 + (y ^ other)
            out_ref[:, pl.ds(pl.multiple_of(where * width, width), width)] = blocks[2 * k + other][...]


def place(blocks, n_tensor):
    rows, width = blocks[0].shape
    return pl.pallas_call(
        functools.partial(place_kernel, n_tensor // 2),
        out_shape=jax.ShapeDtypeStruct((rows, width * n_tensor), BF16),
        in_specs=[VMEM] * n_tensor,
        out_specs=VMEM,
        compiler_params=ROOM,
        cost_estimate=pl.CostEstimate(flops=0, bytes_accessed=1 * MIB, transcendentals=0),
        name="place",
    )(*blocks)


def body(
    n_tensor,
    queries,
    prefix_kv,
    suffix_kv,
    suffix_len,
    residual,
    out_weight,
    adapter_pages,
    adapter_ids,
    pool_slot,
):
    n_z = n_tensor // 2

    def along_y(x):
        return lax.ppermute(x, "tensor", [(t, t ^ 1) for t in range(n_tensor)])

    def along_z(x, k):
        return lax.ppermute(x, "tensor", [(t, t ^ (2 * k)) for t in range(n_tensor)])

    def across(x):
        return lax.ppermute(x, "req", [(0, 1), (1, 0)])

    other_ids = across(adapter_ids)
    found_shrink, found_expand = collect_pages(other_ids, pool_slot, adapter_pages)
    other_shrink = across(found_shrink)
    other_expand = across(found_expand)
    attended, own_shrink, own_expand, row_slot, slot_mine, *pieces = attend(
        suffix_len, adapter_ids, pool_slot, queries, prefix_kv, suffix_kv, out_weight, adapter_pages, n_tensor
    )
    send_order = list(range(1, n_z)) + [0]
    got_y = {k: along_y(pieces[k]) for k in send_order}
    rank_own = shrink_part(attended, row_slot, slot_mine, own_shrink, other_shrink)
    rank_y = along_y(rank_own)
    own = own_part(attended, out_weight, rank_own, n_tensor)
    rank_both = (rank_own + rank_y).astype(BF16)
    moved = []
    for k in range(1, n_z):
        both = (got_y[k].astype(F32) + own[k]).astype(BF16)
        moved.append(along_z(jnp.concatenate([both, rank_both], axis=1), k))
    result = finish(
        n_z, row_slot, slot_mine, own_expand, other_expand, rank_own, rank_y, own[0], got_y[0], residual, *moved
    )
    blocks = []
    held = [result] + [along_z(result, k) for k in range(1, n_z)]
    for k in range(n_z):
        blocks += [held[k], along_y(held[k])]
    return place(blocks, n_tensor)


def solution(mesh):
    return jax.shard_map(
        functools.partial(body, mesh.shape["tensor"]),
        mesh=mesh,
        in_specs=(
            P(("group", "req"), "tensor"),
            P(("group", "tensor"), None, None, None),
            P(("group", "req"), "tensor", None, None, None),
            P(("group", "req")),
            P(("group", "req"), None),
            P("tensor", None),
            P("req", None, None, "tensor"),
            P(("group", "req")),
            P(),
        ),
        out_specs=P(("group", "req"), None),
        check_vma=False,
    )
```

```python
import functools

import jax
import jax.numpy as jnp
from jax import lax
from jax.experimental import pallas as pl
from jax.experimental.pallas import tpu as pltpu
from jax.sharding import PartitionSpec as P

F32 = jnp.float32
BF16 = jnp.bfloat16
LOG2E = 1.4426950408889634
ANY = pl.BlockSpec(memory_space=pl.ANY)
VMEM = pl.BlockSpec(memory_space=pltpu.VMEM)
SMEM = pl.BlockSpec(memory_space=pltpu.SMEM)
MIB = 1 << 20
DISTINCT = 8


def in_hbm(x):
    return pltpu.with_memory_space_constraint(x, pltpu.HBM)


def params(mib):
    return pltpu.CompilerParams(vmem_limit_bytes=mib * MIB)


def nt_dot(a, b):
    return lax.dot_general(a, b, (((1,), (1,)), ((), ())), preferred_element_type=F32)


def nn_dot(a, b):
    return jnp.dot(a, b, preferred_element_type=F32)


def distinct_list(ids_ref, pool_slot_ref, seen, list_id, list_pos):
    rows = ids_ref.shape[0]
    for i in range(pool_slot_ref.shape[0]):
        seen[i] = 0
    for j in range(DISTINCT + 1):
        list_id[j] = -1
        list_pos[j] = 0
    found = jnp.int32(0)
    for r in range(rows):
        one = ids_ref[r]
        fresh = 1 - seen[one]
        seen[one] = 1
        spot = jnp.minimum(found, DISTINCT)
        list_id[spot] = jnp.where(fresh == 1, one, list_id[spot])
        list_pos[spot] = jnp.where(fresh == 1, pool_slot_ref[one], list_pos[spot])
        found = found + fresh


def list_scratch(pool_slot):
    return [
        pltpu.SMEM((pool_slot.shape[0],), jnp.int32),
        pltpu.SMEM((DISTINCT + 1,), jnp.int32),
        pltpu.SMEM((DISTINCT + 1,), jnp.int32),
    ]


def page_copies(pages_ref, outs, list_pos, sem, wait):
    pool = pages_ref.shape[0]
    me = lax.axis_index("req")
    for j in range(DISTINCT):
        pos = list_pos[j]

        @pl.when(pos // pool == me)
        def _():
            for i, out in enumerate(outs):
                copy = pltpu.make_async_copy(pages_ref.at[pos % pool, i], out.at[j], sem.at[i, j])
                if wait:
                    copy.wait()
                else:
                    copy.start()


def attend_kernel(
    n_z,
    len_ref,
    ids_ref,
    slot_ref,
    q_ref,
    prefix_ref,
    suffix_ref,
    weight_ref,
    pages_ref,
    residual_ref,
    att_ref,
    shrink_ref,
    expand_ref,
    row_slot_ref,
    slot_mine_ref,
    res_ref,
    *rest,
):
    w_refs = rest[: 2 * n_z]
    (
        kv,
        suf,
        scores,
        tail,
        rowbuf,
        peak,
        total,
        acc,
        seen,
        list_id,
        list_pos,
        sem_kv,
        sem_suf,
        sem_w,
        sem_page,
    ) = rest[2 * n_z :]
    rows = q_ref.shape[0]
    head_dim = prefix_ref.shape[3]
    heads = q_ref.shape[1] // head_dim
    tokens = prefix_ref.shape[2]
    span = suffix_ref.shape[3]
    width = res_ref.shape[1]
    me = lax.axis_index("tensor")
    z, y = me // 2, me % 2
    scale2 = float(head_dim) ** -0.5 * LOG2E

    n_part = 4
    part = tokens // n_part
    kv_copies = [
        [
            pltpu.make_async_copy(
                prefix_ref.at[0, i, pl.ds(j * part, part)],
                kv.at[i, pl.ds(j * part, part)],
                sem_kv.at[i, j],
            )
            for j in range(n_part)
        ]
        for i in range(2)
    ]
    n_sgrp = 4
    sgrp = rows // n_sgrp
    suf_copies = [
        [
            pltpu.make_async_copy(
                suffix_ref.at[pl.ds(j * sgrp, sgrp), 0, i],
                suf.at[i, pl.ds(j * sgrp, sgrp)],
                sem_suf.at[i, j],
            )
            for j in range(n_sgrp)
        ]
        for i in range(2)
    ]
    w_copies = []
    for side in (1, 0):
        for k in list(range(1, n_z)) + [0]:
            column = pl.multiple_of(((z ^ k) * 2 + (y ^ side)) * width, width)
            spot = side * n_z + k
            w_copies.append(
                pltpu.make_async_copy(weight_ref.at[:, pl.ds(column, width)], w_refs[spot], sem_w.at[spot])
            )
    w_copies.append(
        pltpu.make_async_copy(
            residual_ref.at[:, pl.ds(pl.multiple_of(me * width, width), width)], res_ref, sem_w.at[2 * n_z]
        )
    )
    for c in kv_copies[0] + suf_copies[0] + kv_copies[1] + suf_copies[1]:
        c.start()
    distinct_list(ids_ref, slot_ref, seen, list_id, list_pos)
    row_index = lax.broadcasted_iota(jnp.int32, (rows, 128), 0)
    row_id = jnp.full((rows, 128), -2, jnp.int32)
    for r in range(rows):
        row_id = jnp.where(row_index == r, ids_ref[r], row_id)
    row_slot = jnp.full((rows, 128), -1, jnp.int32)
    slot_index = lax.broadcasted_iota(jnp.int32, (DISTINCT, 128), 0)
    slot_mine = jnp.zeros((DISTINCT, 128), jnp.int32)
    mine = lax.axis_index("req")
    for j in range(DISTINCT):
        row_slot = jnp.where(row_id == list_id[j], j, row_slot)
        owned = (list_pos[j] // pages_ref.shape[0] == mine).astype(jnp.int32)
        slot_mine = jnp.where(slot_index == j, owned, slot_mine)
    row_slot_ref[...] = row_slot
    slot_mine_ref[...] = slot_mine

    for h in range(heads):
        rowbuf[pl.ds(h, rows, stride=heads), :] = q_ref[:, h * head_dim : (h + 1) * head_dim].astype(F32)
    query = rowbuf[...].astype(BF16)
    best = jnp.full(peak.shape, -3.0e38, F32)
    for j in range(n_part):
        kv_copies[0][j].wait()
        if j == 1:
            page_copies(pages_ref, (shrink_ref, expand_ref), list_pos, sem_page, False)
            for c in w_copies:
                c.start()
        for b in range(part // 256):
            base = j * part + b * 256
            block = nt_dot(query, kv[0, base : base + 256, :])
            scores[:, base : base + 256] = block
            best = jnp.maximum(best, jnp.maximum(block[:, :128], block[:, 128:]))

    lanes = lax.broadcasted_iota(jnp.int32, (heads, span), 1)
    for j in range(n_sgrp):
        suf_copies[0][j].wait()
        for i in range(j * sgrp // 2, (j + 1) * sgrp // 2):
            keys = suf[0, 2 * i : 2 * i + 2].reshape(2 * span, head_dim)
            both = nt_dot(query[2 * heads * i : 2 * heads * (i + 1)], keys)
            for a in range(2):
                mine = both[a * heads : (a + 1) * heads, a * span : (a + 1) * span]
                row = 2 * i + a
                tail[row * heads : (row + 1) * heads, :] = jnp.where(lanes < len_ref[row], mine, -1.0e30)
    for b in range(span // 128):
        best = jnp.maximum(best, tail[:, b * 128 : (b + 1) * 128])
    peak[...] = jnp.broadcast_to(jnp.max(best, axis=1, keepdims=True), peak.shape)

    for j in range(n_part):
        kv_copies[1][j].wait()
    total[...] = jnp.zeros(total.shape, F32)
    acc[...] = jnp.zeros(acc.shape, F32)
    chunk = min(2048, tokens)

    @pl.loop(0, tokens // chunk)
    def _(i):
        base = pl.multiple_of(i * chunk, chunk)
        high = peak[...]
        summed = total[...]
        parts = []
        for b in range(chunk // 128):
            e = jnp.exp2((scores[:, pl.ds(base + b * 128, 128)] - high) * scale2)
            summed = summed + e
            parts.append(e.astype(BF16))
        total[...] = summed
        acc[...] += nn_dot(jnp.concatenate(parts, axis=1), kv[1, pl.ds(base, chunk), :])

    zeros = jnp.zeros((heads, span), F32)
    for i in range(rows // 2):
        if (2 * i) % sgrp == 0:
            suf_copies[1][2 * i // sgrp].wait()
        lo = 2 * heads * i
        high = jnp.concatenate([peak[lo : lo + 2 * heads, :]] * (span // 128), axis=1)
        e = jnp.exp2((tail[lo : lo + 2 * heads, :] - high) * scale2)
        part_sum = e[:, :128]
        for b in range(1, span // 128):
            part_sum = part_sum + e[:, b * 128 : (b + 1) * 128]
        total[lo : lo + 2 * heads, :] += part_sum
        diag = jnp.concatenate(
            [
                jnp.concatenate([e[:heads], zeros], axis=1),
                jnp.concatenate([zeros, e[heads:]], axis=1),
            ],
            axis=0,
        ).astype(BF16)
        vals = suf[1, 2 * i : 2 * i + 2].reshape(2 * span, head_dim)
        acc[lo : lo + 2 * heads, :] += nn_dot(diag, vals)

    norm = jnp.sum(total[...], axis=1, keepdims=True)
    rowbuf[...] = acc[...] / norm
    for h in range(heads):
        att_ref[:, h * head_dim : (h + 1) * head_dim] = rowbuf[pl.ds(h, rows, stride=heads), :].astype(BF16)
    page_copies(pages_ref, (shrink_ref, expand_ref), list_pos, sem_page, True)
    for c in w_copies:
        c.wait()


def attend(
    suffix_len, ids, pool_slot, queries, prefix_kv, suffix_kv, out_weight, pages, residual, n_tensor
):
    rows = queries.shape[0]
    n_z = n_tensor // 2
    width = out_weight.shape[1] // n_tensor
    tokens, head_dim = prefix_kv.shape[2:]
    n_q = rows * queries.shape[1] // head_dim
    span = suffix_kv.shape[3]
    out = pl.pallas_call(
        functools.partial(attend_kernel, n_z),
        out_shape=[
            pltpu.VMEM(queries.shape, BF16),
            pltpu.VMEM((DISTINCT,) + pages.shape[2:], BF16),
            pltpu.VMEM((DISTINCT,) + pages.shape[2:], BF16),
            pltpu.VMEM((rows, 128), jnp.int32),
            pltpu.VMEM((DISTINCT, 128), jnp.int32),
            pltpu.VMEM((rows, width), BF16),
        ]
        + [pltpu.VMEM((out_weight.shape[0], width), BF16)] * n_tensor,
        in_specs=[SMEM, SMEM, SMEM, VMEM, ANY, ANY, ANY, ANY, ANY],
        out_specs=[VMEM] * (6 + n_tensor),
        scratch_shapes=[
            pltpu.VMEM((2, tokens, head_dim), BF16),
            pltpu.VMEM((2, rows, span, head_dim), BF16),
            pltpu.VMEM((n_q, tokens), F32),
            pltpu.VMEM((n_q, span), F32),
            pltpu.VMEM((n_q, head_dim), F32),
            pltpu.VMEM((n_q, 128), F32),
            pltpu.VMEM((n_q, 128), F32),
            pltpu.VMEM((n_q, head_dim), F32),
        ]
        + list_scratch(pool_slot)
        + [
            pltpu.SemaphoreType.DMA((2, 4)),
            pltpu.SemaphoreType.DMA((2, 4)),
            pltpu.SemaphoreType.DMA((n_tensor + 1,)),
            pltpu.SemaphoreType.DMA((2, DISTINCT)),
        ],
        compiler_params=params(24),
        cost_estimate=pl.CostEstimate(
            flops=2 * 2 * n_q * tokens * head_dim,
            bytes_accessed=26 * MIB,
            transcendentals=n_q * tokens,
        ),
        name="attend",
    )(
        suffix_len,
        ids,
        pool_slot,
        queries,
        in_hbm(prefix_kv),
        in_hbm(suffix_kv),
        in_hbm(out_weight),
        in_hbm(pages),
        in_hbm(residual),
    )
    return out[:6], out[6 : 6 + n_z], out[6 + n_z :]


def small_call(kernel, name, out_shape, operands, flops=1 << 27):
    return pl.pallas_call(
        kernel,
        out_shape=out_shape,
        in_specs=[VMEM] * len(operands),
        out_specs=jax.tree.map(lambda _: VMEM, out_shape),
        compiler_params=params(8),
        cost_estimate=pl.CostEstimate(flops=flops, bytes_accessed=2 * MIB, transcendentals=0),
        name=name,
    )(*operands)


def collect_kernel(ids_ref, slot_ref, pages_ref, out_ref, seen, list_id, list_pos, sem):
    distinct_list(ids_ref, slot_ref, seen, list_id, list_pos)
    for wait in (False, True):
        page_copies(pages_ref, (out_ref.at[0], out_ref.at[1]), list_pos, sem, wait)


def collect_pages(ids, pool_slot, pages):
    return pl.pallas_call(
        collect_kernel,
        out_shape=pltpu.VMEM((2, DISTINCT) + pages.shape[2:], BF16),
        in_specs=[SMEM, SMEM, ANY],
        out_specs=VMEM,
        scratch_shapes=list_scratch(pool_slot) + [pltpu.SemaphoreType.DMA((2, DISTINCT))],
        compiler_params=params(4),
        cost_estimate=pl.CostEstimate(flops=0, bytes_accessed=2 * MIB, transcendentals=0),
        name="collect_pages",
    )(ids, pool_slot, in_hbm(pages))


def merged(own_ref, other, half, slot_mine):
    rank = own_ref.shape[1]
    tiles = []
    for j in range(DISTINCT):
        hit = jnp.broadcast_to(slot_mine[j : j + 1, :1], (rank, 1)) == 1
        tiles.append(jnp.where(hit, own_ref[j].astype(F32), other[half, j].astype(F32)).astype(BF16))
    return jnp.concatenate(tiles, axis=0)


def lane_place(shape, rank):
    return lax.broadcasted_iota(jnp.int32, shape, 1) // rank


def first_kernel(n, att_ref, row_slot_ref, slot_mine_ref, own_ref, other_ref, *rest):
    w_refs = rest[:n]
    out_ref, rank_ref = rest[n:]
    width = w_refs[0].shape[1]
    attended = att_ref[...]
    for k in range(n):
        out_ref[:, k * width : (k + 1) * width] = nn_dot(attended, w_refs[k][...]).astype(BF16)
    rank = own_ref.shape[1]
    per_tile = 128 // rank
    low = nt_dot(attended, merged(own_ref, other_ref, 0, slot_mine_ref[...]))
    row_slot = row_slot_ref[...]
    place = lane_place(row_slot.shape, rank)
    picked = jnp.zeros(row_slot.shape, F32)
    for tile in range(DISTINCT // per_tile):
        hit = row_slot == place + tile * per_tile
        picked = jnp.where(hit, low[:, tile * 128 : (tile + 1) * 128], picked)
    rank_ref[...] = picked
    out_ref[:, n * width :] = picked.astype(BF16)


def second_kernel(n, att_ref, *rest):
    w_refs = rest[:n]
    out_ref = rest[-1]
    width = w_refs[0].shape[1]
    attended = att_ref[...]
    for k in range(n):
        out_ref[:, k * width : (k + 1) * width] = nn_dot(attended, w_refs[k][...]).astype(BF16)


def add_kernel(spot, first_spot, att_ref, w_ref, from_ref, first_ref, rank_ref, out_ref):
    width = w_ref.shape[1]
    both = nn_dot(att_ref[...], w_ref[...]) + from_ref[:, spot * width : (spot + 1) * width].astype(F32)
    out_ref[:, :width] = both.astype(BF16)
    rank_both = rank_ref[...] + first_ref[:, first_spot * width :].astype(F32)
    out_ref[:, width:] = rank_both.astype(BF16)


def finish_kernel(n_z, spot, first_spot, *refs):
    att_ref, w_ref, row_slot_ref, slot_mine_ref, own_ref, other_ref = refs[:6]
    rank_ref, first_ref, from_ref, res_ref = refs[6:10]
    moved = refs[10 : 10 + n_z - 1]
    out_ref = refs[10 + n_z - 1]
    rank = own_ref.shape[1]
    per_tile = 128 // rank
    width = w_ref.shape[1]
    low = rank_ref[...] + first_ref[:, first_spot * width :].astype(F32)
    for ref in moved:
        low = low + ref[:, width:].astype(F32)
    row_slot = row_slot_ref[...]
    place = lane_place(row_slot.shape, rank)
    tiles = []
    for tile in range(DISTINCT // per_tile):
        tiles.append(jnp.where(row_slot == place + tile * per_tile, low, 0.0).astype(BF16))
    total = nn_dot(jnp.concatenate(tiles, axis=1), merged(own_ref, other_ref, 1, slot_mine_ref[...]))
    total = total + nn_dot(att_ref[...], w_ref[...])
    total = total + (res_ref[...].astype(F32) + from_ref[:, spot * width : (spot + 1) * width].astype(F32))
    for ref in moved:
        total = total + ref[:, :width].astype(F32)
    out_ref[...] = total.astype(BF16)


def place_kernel(n_z, *refs):
    blocks = refs[: 2 * n_z]
    out_ref = refs[2 * n_z]
    width = blocks[0].shape[1]
    me = lax.axis_index("tensor")
    z, y = me // 2, me % 2
    for k in range(n_z):
        for other in range(2):
            where = (z ^ k) * 2 + (y ^ other)
            out_ref[:, pl.ds(pl.multiple_of(where * width, width), width)] = blocks[2 * k + other][...]


def place(blocks, n_tensor):
    rows, width = blocks[0].shape
    return pl.pallas_call(
        functools.partial(place_kernel, n_tensor // 2),
        out_shape=jax.ShapeDtypeStruct((rows, width * n_tensor), BF16),
        in_specs=[VMEM] * n_tensor,
        out_specs=VMEM,
        compiler_params=params(4),
        cost_estimate=pl.CostEstimate(flops=0, bytes_accessed=1 * MIB, transcendentals=0),
        name="place",
    )(*blocks)


def body(
    n_tensor,
    queries,
    prefix_kv,
    suffix_kv,
    suffix_len,
    residual,
    out_weight,
    adapter_pages,
    adapter_ids,
    pool_slot,
):
    n_z = n_tensor // 2

    def along_y(x):
        return lax.ppermute(x, "tensor", [(t, t ^ 1) for t in range(n_tensor)])

    def along_z(x, k):
        return lax.ppermute(x, "tensor", [(t, t ^ (2 * k)) for t in range(n_tensor)])

    def across(x):
        return lax.ppermute(x, "req", [(0, 1), (1, 0)])

    rows = queries.shape[0]
    width = out_weight.shape[1] // n_tensor
    other_ids = across(adapter_ids)
    other_pages = across(collect_pages(other_ids, pool_slot, adapter_pages))
    (attended, own_shrink, own_expand, row_slot, slot_mine, res), own_w, far_w = attend(
        suffix_len,
        adapter_ids,
        pool_slot,
        queries,
        prefix_kv,
        suffix_kv,
        out_weight,
        adapter_pages,
        residual,
        n_tensor,
    )
    order = list(range(1, n_z)) + [0]
    first, second = order[: n_z // 2], order[n_z // 2 :]
    n_first, n_second = len(first), len(second)
    first_out, rank_own = small_call(
        functools.partial(first_kernel, n_first),
        "first_blocks",
        [pltpu.VMEM((rows, n_first * width + 128), BF16), pltpu.VMEM((rows, 128), F32)],
        [attended, row_slot, slot_mine, own_shrink, other_pages] + [far_w[k] for k in first],
    )
    from_first = along_y(first_out)
    second_out = small_call(
        functools.partial(second_kernel, n_second),
        "second_blocks",
        pltpu.VMEM((rows, n_second * width), BF16),
        [attended] + [far_w[k] for k in second] + [rank_own],
    )
    from_second = along_y(second_out)
    moved = []
    for k in range(1, n_z):
        source, spot = (from_first, first.index(k)) if k in first else (from_second, second.index(k))
        piece = small_call(
            functools.partial(add_kernel, spot, n_first),
            "add_block",
            pltpu.VMEM((rows, width + 128), BF16),
            [attended, own_w[k], source, from_first, rank_own],
        )
        moved.append(along_z(piece, k))
    result = small_call(
        functools.partial(finish_kernel, n_z, second.index(0), n_first),
        "finish",
        pltpu.VMEM((rows, width), BF16),
        [attended, own_w[0], row_slot, slot_mine, own_expand, other_pages, rank_own, from_first, from_second, res]
        + moved,
    )
    blocks = []
    held = [result] + [along_z(result, k) for k in range(1, n_z)]
    for k in range(n_z):
        blocks += [held[k], along_y(held[k])]
    return place(blocks, n_tensor)


def solution(mesh):
    return jax.shard_map(
        functools.partial(body, mesh.shape["tensor"]),
        mesh=mesh,
        in_specs=(
            P(("group", "req"), "tensor"),
            P(("group", "tensor"), None, None, None),
            P(("group", "req"), "tensor", None, None, None),
            P(("group", "req")),
            P(("group", "req"), None),
            P("tensor", None),
            P("req", None, None, "tensor"),
            P(("group", "req")),
            P(),
        ),
        out_specs=P(("group", "req"), None),
        check_vma=False,
    )
```

```python
import functools

import jax
import jax.numpy as jnp
from jax import lax
from jax.experimental import pallas as pl
from jax.experimental.pallas import tpu as pltpu
from jax.sharding import PartitionSpec as P

F32 = jnp.float32
BF16 = jnp.bfloat16
LOG2E = 1.4426950408889634
ANY = pl.BlockSpec(memory_space=pl.ANY)
VMEM = pl.BlockSpec(memory_space=pltpu.VMEM)
SMEM = pl.BlockSpec(memory_space=pltpu.SMEM)
MIB = 1 << 20
DISTINCT = 8


def in_hbm(x):
    return pltpu.with_memory_space_constraint(x, pltpu.HBM)


def params(mib):
    return pltpu.CompilerParams(vmem_limit_bytes=mib * MIB)


def nt_dot(a, b):
    return lax.dot_general(a, b, (((1,), (1,)), ((), ())), preferred_element_type=F32)


def nn_dot(a, b):
    return jnp.dot(a, b, preferred_element_type=F32)


def distinct_list(ids_ref, pool_slot_ref, seen, list_id, list_pos):
    rows = ids_ref.shape[0]
    for i in range(pool_slot_ref.shape[0]):
        seen[i] = 0
    for j in range(DISTINCT + 1):
        list_id[j] = -1
        list_pos[j] = 0
    found = jnp.int32(0)
    for r in range(rows):
        one = ids_ref[r]
        fresh = 1 - seen[one]
        seen[one] = 1
        spot = jnp.minimum(found, DISTINCT)
        list_id[spot] = jnp.where(fresh == 1, one, list_id[spot])
        list_pos[spot] = jnp.where(fresh == 1, pool_slot_ref[one], list_pos[spot])
        found = found + fresh


def list_scratch(pool_slot):
    return [
        pltpu.SMEM((pool_slot.shape[0],), jnp.int32),
        pltpu.SMEM((DISTINCT + 1,), jnp.int32),
        pltpu.SMEM((DISTINCT + 1,), jnp.int32),
    ]


def page_copies(pages_ref, outs, list_pos, sem, wait):
    pool = pages_ref.shape[0]
    me = lax.axis_index("req")
    for j in range(DISTINCT):
        pos = list_pos[j]

        @pl.when(pos // pool == me)
        def _():
            for i, out in enumerate(outs):
                copy = pltpu.make_async_copy(pages_ref.at[pos % pool, i], out.at[j], sem.at[i, j])
                if wait:
                    copy.wait()
                else:
                    copy.start()


def suffix_scores_kernel(
    len_ref, q_ref, prefix_ref, suffix_ref, query_ref, tail_ref, keys_ref, suf, rowbuf, sem, sem_suf
):
    rows = q_ref.shape[0]
    head_dim = prefix_ref.shape[3]
    heads = q_ref.shape[1] // head_dim
    span = suffix_ref.shape[3]
    groups = sem_suf.shape[0]
    size = rows // groups
    copies = [
        pltpu.make_async_copy(
            suffix_ref.at[pl.ds(j * size, size), 0, 0], suf.at[pl.ds(j * size, size)], sem_suf.at[j]
        )
        for j in range(groups)
    ]
    fetch = pltpu.make_async_copy(prefix_ref.at[0, 0], keys_ref, sem.at[0])
    for c in copies + [fetch]:
        c.start()
    for h in range(heads):
        rowbuf[pl.ds(h, rows, stride=heads), :] = q_ref[:, h * head_dim : (h + 1) * head_dim].astype(F32)
    query = rowbuf[...].astype(BF16)
    query_ref[...] = query
    lanes = lax.broadcasted_iota(jnp.int32, (heads, span), 1)
    for j in range(groups):
        copies[j].wait()
        for i in range(j * size // 2, (j + 1) * size // 2):
            keys = suf[2 * i : 2 * i + 2].reshape(2 * span, head_dim)
            both = nt_dot(query[2 * heads * i : 2 * heads * (i + 1)], keys)
            for a in range(2):
                mine = both[a * heads : (a + 1) * heads, a * span : (a + 1) * span]
                row = 2 * i + a
                tail_ref[row * heads : (row + 1) * heads, :] = jnp.where(lanes < len_ref[row], mine, -1.0e30)
    fetch.wait()


def weight_copies(weight_ref, outs, spots, sem):
    me = lax.axis_index("tensor")
    z, y = me // 2, me % 2
    copies = []
    for i, (side, k) in enumerate(spots):
        width = outs[i].shape[1]
        column = pl.multiple_of(((z ^ k) * 2 + (y ^ side)) * width, width)
        copies.append(pltpu.make_async_copy(weight_ref.at[:, pl.ds(column, width)], outs[i], sem.at[i]))
    return copies


def prefix_scores_kernel(spots, ids_ref, slot_ref, query_ref, tail_ref, keys_ref, prefix_ref, suffix_ref, *rest):
    pages_ref, weight_ref = rest[:2]
    scores_ref, peak_ref, out_pages_ref, vals_ref, suf_vals_ref = rest[2:7]
    w_refs = rest[7 : 7 + len(spots)]
    seen, list_id, list_pos, sem, sem_page, sem_w = rest[7 + len(spots) :]
    tokens = keys_ref.shape[0]
    fetch = [
        pltpu.make_async_copy(prefix_ref.at[0, 1], vals_ref, sem.at[0]),
        pltpu.make_async_copy(suffix_ref.at[:, 0, 1], suf_vals_ref, sem.at[1]),
    ] + weight_copies(weight_ref, w_refs, spots, sem_w)
    distinct_list(ids_ref, slot_ref, seen, list_id, list_pos)
    outs = (out_pages_ref.at[0], out_pages_ref.at[1])
    page_copies(pages_ref, outs, list_pos, sem_page, False)
    for c in fetch:
        c.start()
    query = query_ref[...]
    best = jnp.maximum(tail_ref[:, :128], tail_ref[:, 128:256])
    for b in range(2, tail_ref.shape[1] // 128):
        best = jnp.maximum(best, tail_ref[:, b * 128 : (b + 1) * 128])
    for base in range(0, tokens, 256):
        block = nt_dot(query, keys_ref[base : base + 256, :])
        scores_ref[:, base : base + 256] = block
        best = jnp.maximum(best, jnp.maximum(block[:, :128], block[:, 128:]))
    peak_ref[...] = jnp.broadcast_to(jnp.max(best, axis=1, keepdims=True), peak_ref.shape)
    page_copies(pages_ref, outs, list_pos, sem_page, True)
    for c in fetch:
        c.wait()


def values_kernel(spots, ids_ref, slot_ref, scores, tail, peak, vals_ref, suf_vals_ref, *rest):
    pages_ref, weight_ref, residual_ref = rest[:3]
    att_ref, shrink_ref, expand_ref, row_slot_ref, slot_mine_ref, res_ref = rest[3:9]
    w_refs = rest[9 : 9 + len(spots)]
    rowbuf, total, acc, seen, list_id, list_pos, sem, sem_page, sem_w = rest[9 + len(spots) :]
    rows, head_dim, span = suf_vals_ref.shape[0], vals_ref.shape[1], suf_vals_ref.shape[1]
    tokens = vals_ref.shape[0]
    heads = att_ref.shape[1] // head_dim
    width = res_ref.shape[1]
    me = lax.axis_index("tensor")
    scale2 = float(head_dim) ** -0.5 * LOG2E
    fetch = weight_copies(weight_ref, w_refs, spots, sem_w)
    fetch.append(
        pltpu.make_async_copy(
            residual_ref.at[:, pl.ds(pl.multiple_of(me * width, width), width)], res_ref, sem.at[0]
        )
    )
    for c in fetch:
        c.start()
    distinct_list(ids_ref, slot_ref, seen, list_id, list_pos)
    page_copies(pages_ref, (shrink_ref, expand_ref), list_pos, sem_page, False)
    row_index = lax.broadcasted_iota(jnp.int32, (rows, 128), 0)
    row_id = jnp.full((rows, 128), -2, jnp.int32)
    for r in range(rows):
        row_id = jnp.where(row_index == r, ids_ref[r], row_id)
    row_slot = jnp.full((rows, 128), -1, jnp.int32)
    slot_index = lax.broadcasted_iota(jnp.int32, (DISTINCT, 128), 0)
    slot_mine = jnp.zeros((DISTINCT, 128), jnp.int32)
    mine = lax.axis_index("req")
    for j in range(DISTINCT):
        row_slot = jnp.where(row_id == list_id[j], j, row_slot)
        owned = (list_pos[j] // pages_ref.shape[0] == mine).astype(jnp.int32)
        slot_mine = jnp.where(slot_index == j, owned, slot_mine)
    row_slot_ref[...] = row_slot
    slot_mine_ref[...] = slot_mine

    total[...] = jnp.zeros(total.shape, F32)
    acc[...] = jnp.zeros(acc.shape, F32)
    chunk = min(2048, tokens)

    @pl.loop(0, tokens // chunk)
    def _(i):
        base = pl.multiple_of(i * chunk, chunk)
        high = peak[...]
        summed = total[...]
        parts = []
        for b in range(chunk // 128):
            e = jnp.exp2((scores[:, pl.ds(base + b * 128, 128)] - high) * scale2)
            summed = summed + e
            parts.append(e.astype(BF16))
        total[...] = summed
        acc[...] += nn_dot(jnp.concatenate(parts, axis=1), vals_ref[pl.ds(base, chunk), :])

    zeros = jnp.zeros((heads, span), F32)
    for i in range(rows // 2):
        lo = 2 * heads * i
        high = jnp.concatenate([peak[lo : lo + 2 * heads, :]] * (span // 128), axis=1)
        e = jnp.exp2((tail[lo : lo + 2 * heads, :] - high) * scale2)
        part_sum = e[:, :128]
        for b in range(1, span // 128):
            part_sum = part_sum + e[:, b * 128 : (b + 1) * 128]
        total[lo : lo + 2 * heads, :] += part_sum
        diag = jnp.concatenate(
            [
                jnp.concatenate([e[:heads], zeros], axis=1),
                jnp.concatenate([zeros, e[heads:]], axis=1),
            ],
            axis=0,
        ).astype(BF16)
        vals = suf_vals_ref[2 * i : 2 * i + 2].reshape(2 * span, head_dim)
        acc[lo : lo + 2 * heads, :] += nn_dot(diag, vals)

    norm = jnp.sum(total[...], axis=1, keepdims=True)
    rowbuf[...] = acc[...] / norm
    for h in range(heads):
        att_ref[:, h * head_dim : (h + 1) * head_dim] = rowbuf[pl.ds(h, rows, stride=heads), :].astype(BF16)
    page_copies(pages_ref, (shrink_ref, expand_ref), list_pos, sem_page, True)
    for c in fetch:
        c.wait()


def kernel_call(kernel, name, out_shape, specs, scratch, operands, mib, flops, bytes_accessed):
    return pl.pallas_call(
        kernel,
        out_shape=out_shape,
        in_specs=specs,
        out_specs=[VMEM] * len(out_shape),
        scratch_shapes=scratch,
        compiler_params=params(mib),
        cost_estimate=pl.CostEstimate(flops=flops, bytes_accessed=bytes_accessed, transcendentals=0),
        name=name,
    )(*operands)


def attend(
    suffix_len, ids, other_ids, pool_slot, queries, prefix_kv, suffix_kv, out_weight, pages, residual, n_tensor, across
):
    rows = queries.shape[0]
    n_z = n_tensor // 2
    in_rows = out_weight.shape[0]
    width = out_weight.shape[1] // n_tensor
    tokens, head_dim = prefix_kv.shape[2:]
    n_q = rows * queries.shape[1] // head_dim
    span = suffix_kv.shape[3]
    prefix_kv, suffix_kv, out_weight = in_hbm(prefix_kv), in_hbm(suffix_kv), in_hbm(out_weight)
    pages, residual = in_hbm(pages), in_hbm(residual)
    query, tail, keys = kernel_call(
        suffix_scores_kernel,
        "suffix_scores",
        [pltpu.VMEM((n_q, head_dim), BF16), pltpu.VMEM((n_q, span), F32), pltpu.VMEM((tokens, head_dim), BF16)],
        [SMEM, VMEM, ANY, ANY],
        [
            pltpu.VMEM((rows, span, head_dim), BF16),
            pltpu.VMEM((n_q, head_dim), F32),
            pltpu.SemaphoreType.DMA((1,)),
            pltpu.SemaphoreType.DMA((4,)),
        ],
        [suffix_len, queries, prefix_kv, suffix_kv],
        6,
        1 << 30,
        6 * MIB,
    )
    far = list(range(n_z - 1, -1, -1))
    early = [(0, k) for k in far[: n_z // 2]]
    late = [(1, k) for k in far] + [(0, k) for k in far[n_z // 2 :]]
    scores, peak, out_pages, vals, suf_vals, *early_w = kernel_call(
        functools.partial(prefix_scores_kernel, early),
        "prefix_scores",
        [
            pltpu.VMEM((n_q, tokens), F32),
            pltpu.VMEM((n_q, 128), F32),
            pltpu.VMEM((2, DISTINCT) + pages.shape[2:], BF16),
            pltpu.VMEM((tokens, head_dim), BF16),
            pltpu.VMEM((rows, span, head_dim), BF16),
        ]
        + [pltpu.VMEM((in_rows, width), BF16)] * len(early),
        [SMEM, SMEM, VMEM, VMEM, VMEM, ANY, ANY, ANY, ANY],
        list_scratch(pool_slot)
        + [
            pltpu.SemaphoreType.DMA((2,)),
            pltpu.SemaphoreType.DMA((2, DISTINCT)),
            pltpu.SemaphoreType.DMA((len(early),)),
        ],
        [other_ids, pool_slot, query, tail, keys, prefix_kv, suffix_kv, pages, out_weight],
        4,
        2 * n_q * tokens * head_dim,
        9 * MIB,
    )
    other_pages = across(out_pages)
    attended, own_shrink, own_expand, row_slot, slot_mine, res, *late_w = kernel_call(
        functools.partial(values_kernel, late),
        "values",
        [
            pltpu.VMEM(queries.shape, BF16),
            pltpu.VMEM((DISTINCT,) + pages.shape[2:], BF16),
            pltpu.VMEM((DISTINCT,) + pages.shape[2:], BF16),
            pltpu.VMEM((rows, 128), jnp.int32),
            pltpu.VMEM((DISTINCT, 128), jnp.int32),
            pltpu.VMEM((rows, width), BF16),
        ]
        + [pltpu.VMEM((in_rows, width), BF16)] * len(late),
        [SMEM, SMEM, VMEM, VMEM, VMEM, VMEM, VMEM, ANY, ANY, ANY],
        [
            pltpu.VMEM((n_q, head_dim), F32),
            pltpu.VMEM((n_q, 128), F32),
            pltpu.VMEM((n_q, head_dim), F32),
        ]
        + list_scratch(pool_slot)
        + [
            pltpu.SemaphoreType.DMA((1,)),
            pltpu.SemaphoreType.DMA((2, DISTINCT)),
            pltpu.SemaphoreType.DMA((len(late),)),
        ],
        [ids, pool_slot, scores, tail, peak, vals, suf_vals, pages, out_weight, residual],
        6,
        2 * n_q * tokens * head_dim,
        14 * MIB,
    )
    weights = dict(zip(early + late, list(early_w) + list(late_w)))
    return attended, own_shrink, own_expand, other_pages, row_slot, slot_mine, res, weights


def small_call(kernel, name, out_shape, operands, flops=1 << 27):
    return pl.pallas_call(
        kernel,
        out_shape=out_shape,
        in_specs=[VMEM] * len(operands),
        out_specs=jax.tree.map(lambda _: VMEM, out_shape),
        compiler_params=params(8),
        cost_estimate=pl.CostEstimate(flops=flops, bytes_accessed=2 * MIB, transcendentals=0),
        name=name,
    )(*operands)


def merged(own_ref, other, half, slot_mine):
    rank = own_ref.shape[1]
    tiles = []
    for j in range(DISTINCT):
        hit = jnp.broadcast_to(slot_mine[j : j + 1, :1], (rank, 1)) == 1
        tiles.append(jnp.where(hit, own_ref[j].astype(F32), other[half, j].astype(F32)).astype(BF16))
    return jnp.concatenate(tiles, axis=0)


def lane_place(shape, rank):
    return lax.broadcasted_iota(jnp.int32, shape, 1) // rank


def far_kernel(n, att_ref, row_slot_ref, slot_mine_ref, own_ref, other_ref, *rest):
    w_refs = rest[:n]
    out_ref, rank_ref = rest[n:]
    width = w_refs[0].shape[1]
    attended = att_ref[...]
    for k in range(n):
        out_ref[:, k * width : (k + 1) * width] = nn_dot(attended, w_refs[k][...]).astype(BF16)
    rank = own_ref.shape[1]
    per_tile = 128 // rank
    low = nt_dot(attended, merged(own_ref, other_ref, 0, slot_mine_ref[...]))
    row_slot = row_slot_ref[...]
    place = lane_place(row_slot.shape, rank)
    picked = jnp.zeros(row_slot.shape, F32)
    for tile in range(DISTINCT // per_tile):
        hit = row_slot == place + tile * per_tile
        picked = jnp.where(hit, low[:, tile * 128 : (tile + 1) * 128], picked)
    rank_ref[...] = picked
    out_ref[:, n * width :] = picked.astype(BF16)


def near_kernel(att_ref, w_ref, cross_w_ref, rank_ref, out_ref, cross_ref):
    width = w_ref.shape[1]
    attended = att_ref[...]
    rank = rank_ref[...].astype(BF16)
    for w, out in ((w_ref, out_ref), (cross_w_ref, cross_ref)):
        out[:, :width] = nn_dot(attended, w[...]).astype(BF16)
        out[:, width:] = rank


def block_kernel(att_ref, w_ref, after_ref, out_ref):
    out_ref[...] = nn_dot(att_ref[...], w_ref[...]).astype(BF16)


def add_kernel(spot, att_ref, w_ref, from_ref, rank_ref, out_ref):
    width = w_ref.shape[1]
    both = nn_dot(att_ref[...], w_ref[...]) + from_ref[:, spot * width : (spot + 1) * width].astype(F32)
    out_ref[:, :width] = both.astype(BF16)
    rank_both = rank_ref[...] + from_ref[:, from_ref.shape[1] - 128 :].astype(F32)
    out_ref[:, width:] = rank_both.astype(BF16)


def finish_kernel(*refs):
    att_ref, w_ref, row_slot_ref, slot_mine_ref, own_ref, other_ref = refs[:6]
    rank_ref, far_ref, from_ref, res_ref = refs[6:10]
    moved, out_ref = refs[10:-1], refs[-1]
    rank = own_ref.shape[1]
    per_tile = 128 // rank
    width = w_ref.shape[1]
    low = rank_ref[...] + far_ref[:, far_ref.shape[1] - 128 :].astype(F32)
    for ref in moved:
        low = low + ref[:, width:].astype(F32)
    row_slot = row_slot_ref[...]
    place = lane_place(row_slot.shape, rank)
    tiles = []
    for tile in range(DISTINCT // per_tile):
        tiles.append(jnp.where(row_slot == place + tile * per_tile, low, 0.0).astype(BF16))
    total = nn_dot(jnp.concatenate(tiles, axis=1), merged(own_ref, other_ref, 1, slot_mine_ref[...]))
    total = total + nn_dot(att_ref[...], w_ref[...])
    total = total + (res_ref[...].astype(F32) + from_ref[...].astype(F32))
    for ref in moved:
        total = total + ref[:, :width].astype(F32)
    out_ref[...] = total.astype(BF16)


def place_kernel(n_z, *refs):
    blocks = refs[: 2 * n_z]
    out_ref = refs[2 * n_z]
    width = blocks[0].shape[1]
    me = lax.axis_index("tensor")
    z, y = me // 2, me % 2
    for k in range(n_z):
        for other in range(2):
            where = (z ^ k) * 2 + (y ^ other)
            out_ref[:, pl.ds(pl.multiple_of(where * width, width), width)] = blocks[2 * k + other][...]


def place(blocks, n_tensor):
    rows, width = blocks[0].shape
    return pl.pallas_call(
        functools.partial(place_kernel, n_tensor // 2),
        out_shape=jax.ShapeDtypeStruct((rows, width * n_tensor), BF16),
        in_specs=[VMEM] * n_tensor,
        out_specs=VMEM,
        compiler_params=params(4),
        cost_estimate=pl.CostEstimate(flops=0, bytes_accessed=1 * MIB, transcendentals=0),
        name="place",
    )(*blocks)


def body(
    n_tensor,
    queries,
    prefix_kv,
    suffix_kv,
    suffix_len,
    residual,
    out_weight,
    adapter_pages,
    adapter_ids,
    pool_slot,
):
    n_z = n_tensor // 2

    def along_y(x):
        return lax.ppermute(x, "tensor", [(t, t ^ 1) for t in range(n_tensor)])

    def along_z(x, k):
        return lax.ppermute(x, "tensor", [(t, t ^ (2 * k)) for t in range(n_tensor)])

    def along_both(x, k):
        return lax.ppermute(x, "tensor", [(t, t ^ (2 * k) ^ 1) for t in range(n_tensor)])

    def across(x):
        return lax.ppermute(x, "req", [(0, 1), (1, 0)])

    rows = queries.shape[0]
    width = out_weight.shape[1] // n_tensor
    attended, own_shrink, own_expand, other_pages, row_slot, slot_mine, res, weights = attend(
        suffix_len,
        adapter_ids,
        across(adapter_ids),
        pool_slot,
        queries,
        prefix_kv,
        suffix_kv,
        out_weight,
        adapter_pages,
        residual,
        n_tensor,
        across,
    )
    far = list(range(n_z - 1, 1, -1))
    piece_shape = pltpu.VMEM((rows, width + 128), BF16)
    far_out, rank_own = small_call(
        functools.partial(far_kernel, len(far)),
        "far_blocks",
        [pltpu.VMEM((rows, len(far) * width + 128), BF16), pltpu.VMEM((rows, 128), F32)],
        [attended, row_slot, slot_mine, own_shrink, other_pages] + [weights[1, k] for k in far],
    )
    from_far = along_y(far_out)
    straight, cross = small_call(
        near_kernel,
        "near_blocks",
        [piece_shape, piece_shape],
        [attended, weights[0, 1], weights[1, 1], rank_own],
    )
    moved = [along_z(straight, 1), along_both(cross, 1)]
    for spot, k in enumerate(far):
        piece = small_call(
            functools.partial(add_kernel, spot),
            "add_block",
            piece_shape,
            [attended, weights[0, k], from_far, rank_own],
        )
        moved.append(along_z(piece, k))
    own_far = small_call(
        block_kernel, "own_far_block", pltpu.VMEM((rows, width), BF16), [attended, weights[1, 0], piece]
    )
    from_own = along_y(own_far)
    result = small_call(
        finish_kernel,
        "finish",
        pltpu.VMEM((rows, width), BF16),
        [attended, weights[0, 0], row_slot, slot_mine, own_expand, other_pages, rank_own, from_far, from_own, res]
        + moved,
    )
    held = [result] + [along_z(result, k) for k in range(1, n_z)]
    blocks = []
    for k in range(n_z):
        blocks += [held[k], along_both(result, k) if k < 2 else along_y(held[k])]
    return place(blocks, n_tensor)


def solution(mesh):
    return jax.shard_map(
        functools.partial(body, mesh.shape["tensor"]),
        mesh=mesh,
        in_specs=(
            P(("group", "req"), "tensor"),
            P(("group", "tensor"), None, None, None),
            P(("group", "req"), "tensor", None, None, None),
            P(("group", "req")),
            P(("group", "req"), None),
            P("tensor", None),
            P("req", None, None, "tensor"),
            P(("group", "req")),
            P(),
        ),
        out_specs=P(("group", "req"), None),
        check_vma=False,
    )
```

```python
import functools

import jax
import jax.numpy as jnp
from jax import lax
from jax.experimental import pallas as pl
from jax.experimental.pallas import tpu as pltpu
from jax.sharding import PartitionSpec as P

F32 = jnp.float32
BF16 = jnp.bfloat16
LOG2E = 1.4426950408889634
ANY = pl.BlockSpec(memory_space=pl.ANY)
VMEM = pl.BlockSpec(memory_space=pltpu.VMEM)
SMEM = pl.BlockSpec(memory_space=pltpu.SMEM)
MIB = 1 << 20
DISTINCT = 8


def in_hbm(x):
    return pltpu.with_memory_space_constraint(x, pltpu.HBM)


def params(mib):
    return pltpu.CompilerParams(vmem_limit_bytes=mib * MIB)


def nt_dot(a, b):
    return lax.dot_general(a, b, (((1,), (1,)), ((), ())), preferred_element_type=F32)


def nn_dot(a, b):
    return jnp.dot(a, b, preferred_element_type=F32)


def distinct_list(ids_ref, pool_slot_ref, seen, list_id, list_pos):
    rows = ids_ref.shape[0]
    for i in range(pool_slot_ref.shape[0]):
        seen[i] = 0
    for j in range(DISTINCT + 1):
        list_id[j] = -1
        list_pos[j] = 0
    found = jnp.int32(0)
    for r in range(rows):
        one = ids_ref[r]
        fresh = 1 - seen[one]
        seen[one] = 1
        spot = jnp.minimum(found, DISTINCT)
        list_id[spot] = jnp.where(fresh == 1, one, list_id[spot])
        list_pos[spot] = jnp.where(fresh == 1, pool_slot_ref[one], list_pos[spot])
        found = found + fresh


def list_scratch(pool_slot):
    return [
        pltpu.SMEM((pool_slot.shape[0],), jnp.int32),
        pltpu.SMEM((DISTINCT + 1,), jnp.int32),
        pltpu.SMEM((DISTINCT + 1,), jnp.int32),
    ]


def page_copies(pages_ref, outs, list_pos, sem, wait):
    pool = pages_ref.shape[0]
    me = lax.axis_index("req")
    for j in range(DISTINCT):
        pos = list_pos[j]

        @pl.when(pos // pool == me)
        def _():
            for i, out in enumerate(outs):
                copy = pltpu.make_async_copy(pages_ref.at[pos % pool, i], out.at[j], sem.at[i, j])
                if wait:
                    copy.wait()
                else:
                    copy.start()


def prefix_scores_kernel(
    q_ref, prefix_ref, suffix_ref, query_ref, scores_ref, peak_ref, vals_ref, suf_keys_ref, qbuf, keys, rowbuf, sem, sem_keys
):
    rows = q_ref.shape[0]
    tokens, head_dim = keys.shape
    heads = q_ref.shape[1] // head_dim
    parts = sem_keys.shape[0]
    size = tokens // parts
    key_copies = [
        pltpu.make_async_copy(
            prefix_ref.at[0, 0, pl.ds(j * size, size)], keys.at[pl.ds(j * size, size)], sem_keys.at[j]
        )
        for j in range(parts)
    ]
    fetch_q = pltpu.make_async_copy(q_ref, qbuf, sem.at[0])
    fetch = [
        pltpu.make_async_copy(suffix_ref.at[:, 0, 0], suf_keys_ref, sem.at[1]),
        pltpu.make_async_copy(prefix_ref.at[0, 1], vals_ref, sem.at[2]),
    ]
    for c in [fetch_q] + key_copies + fetch:
        c.start()
    fetch_q.wait()
    for h in range(heads):
        rowbuf[pl.ds(h, rows, stride=heads), :] = qbuf[:, h * head_dim : (h + 1) * head_dim].astype(F32)
    query = rowbuf[...].astype(BF16)
    query_ref[...] = query
    best = jnp.full(peak_ref.shape, -3.0e38, F32)
    step = min(512, size)
    for j in range(parts):
        key_copies[j].wait()
        for base in range(j * size, (j + 1) * size, step):
            block = nt_dot(keys[base : base + step, :], query)
            scores_ref[base : base + step, :] = block
            best = jnp.maximum(best, jnp.max(block.reshape(step // 8, 8, block.shape[1]), axis=0))
    peak_ref[...] = best
    for c in fetch:
        c.wait()


def weight_copies(weight_ref, outs, spots, sem):
    me = lax.axis_index("tensor")
    z, y = me // 2, me % 2
    copies = []
    for i, (side, k) in enumerate(spots):
        width = outs[i].shape[1]
        column = pl.multiple_of(((z ^ k) * 2 + (y ^ side)) * width, width)
        copies.append(pltpu.make_async_copy(weight_ref.at[:, pl.ds(column, width)], outs[i], sem.at[i]))
    return copies


def suffix_scores_kernel(spots, ids_ref, slot_ref, query_ref, suf_keys_ref, vals_ref, peak_ref, *rest):
    len_ref, suffix_ref, pages_ref, weight_ref = rest[:4]
    tail_ref, high_ref, high_row_ref, vals_t_ref, out_pages_ref, suf_vals_ref = rest[4:10]
    w_refs = rest[10 : 10 + len(spots)]
    lens, seen, list_id, list_pos, sem, sem_page, sem_w = rest[10 + len(spots) :]
    rows, span, head_dim = suf_keys_ref.shape
    tokens = vals_ref.shape[0]
    heads = query_ref.shape[0] // rows
    fetch_len = pltpu.make_async_copy(len_ref, lens, sem.at[1])
    fetch_len.start()
    fetch = [pltpu.make_async_copy(suffix_ref.at[:, 0, 1], suf_vals_ref, sem.at[0])]
    fetch += weight_copies(weight_ref, w_refs, spots, sem_w)
    distinct_list(ids_ref, slot_ref, seen, list_id, list_pos)
    outs = (out_pages_ref.at[0], out_pages_ref.at[1])
    page_copies(pages_ref, outs, list_pos, sem_page, False)
    for c in fetch:
        c.start()
    query = query_ref[...]
    lanes = lax.broadcasted_iota(jnp.int32, (heads, span), 1)
    fetch_len.wait()
    for i in range(rows // 2):
        keys = suf_keys_ref[2 * i : 2 * i + 2].reshape(2 * span, head_dim)
        both = nt_dot(query[2 * heads * i : 2 * heads * (i + 1)], keys)
        for a in range(2):
            mine = both[a * heads : (a + 1) * heads, a * span : (a + 1) * span]
            row = 2 * i + a
            tail_ref[row * heads : (row + 1) * heads, :] = jnp.where(lanes < lens[row], mine, -1.0e30)
    step = min(1024, tokens)
    for base in range(0, tokens, step):
        vals_t_ref[:, base : base + step] = vals_ref[base : base + step, :].astype(F32).T.astype(BF16)
    best = jnp.maximum(tail_ref[:, :128], tail_ref[:, 128:256])
    for b in range(2, span // 128):
        best = jnp.maximum(best, tail_ref[:, b * 128 : (b + 1) * 128])
    across_rows = jnp.broadcast_to(jnp.max(peak_ref[...], axis=0, keepdims=True), (128, peak_ref.shape[1]))
    high = jnp.maximum(across_rows.T, jnp.max(best, axis=1, keepdims=True))
    high_ref[...] = high
    high_row_ref[...] = high.T[:8]
    page_copies(pages_ref, outs, list_pos, sem_page, True)
    for c in fetch:
        c.wait()


def values_kernel(spots, ids_ref, slot_ref, scores, tail, peak, peak_row, vals_t_ref, suf_vals_ref, *rest):
    pages_ref, weight_ref, residual_ref = rest[:3]
    att_ref, shrink_ref, expand_ref, row_slot_ref, slot_mine_ref, res_ref = rest[3:9]
    w_refs = rest[9 : 9 + len(spots)]
    rowbuf, total, acc, total_row, acc_t, seen, list_id, list_pos, sem, sem_page, sem_w = rest[9 + len(spots) :]
    rows, span, head_dim = suf_vals_ref.shape
    tokens = vals_t_ref.shape[1]
    heads = att_ref.shape[1] // head_dim
    width = res_ref.shape[1]
    me = lax.axis_index("tensor")
    scale2 = float(head_dim) ** -0.5 * LOG2E
    fetch = weight_copies(weight_ref, w_refs, spots, sem_w)
    fetch.append(
        pltpu.make_async_copy(
            residual_ref.at[:, pl.ds(pl.multiple_of(me * width, width), width)], res_ref, sem.at[0]
        )
    )
    for c in fetch:
        c.start()
    distinct_list(ids_ref, slot_ref, seen, list_id, list_pos)
    page_copies(pages_ref, (shrink_ref, expand_ref), list_pos, sem_page, False)
    row_index = lax.broadcasted_iota(jnp.int32, (rows, 128), 0)
    row_id = jnp.full((rows, 128), -2, jnp.int32)
    for r in range(rows):
        row_id = jnp.where(row_index == r, ids_ref[r], row_id)
    row_slot = jnp.full((rows, 128), -1, jnp.int32)
    slot_index = lax.broadcasted_iota(jnp.int32, (DISTINCT, 128), 0)
    slot_mine = jnp.zeros((DISTINCT, 128), jnp.int32)
    mine = lax.axis_index("req")
    for j in range(DISTINCT):
        row_slot = jnp.where(row_id == list_id[j], j, row_slot)
        owned = (list_pos[j] // pages_ref.shape[0] == mine).astype(jnp.int32)
        slot_mine = jnp.where(slot_index == j, owned, slot_mine)
    row_slot_ref[...] = row_slot
    slot_mine_ref[...] = slot_mine

    total_row[...] = jnp.zeros(total_row.shape, F32)
    acc_t[...] = jnp.zeros(acc_t.shape, F32)
    n_q = acc_t.shape[1]
    chunk = min(2048, tokens)

    @pl.loop(0, tokens // chunk)
    def _(i):
        base = pl.multiple_of(i * chunk, chunk)
        high_row = peak_row[...]
        block = scores[pl.ds(base, chunk), :].reshape(chunk // 8, 8, n_q)
        e = jnp.exp2((block - high_row[None]) * scale2)
        total_row[...] += jnp.sum(e, axis=0)
        weights = e.reshape(chunk, n_q).astype(BF16)
        acc_t[...] += nn_dot(vals_t_ref[:, pl.ds(base, chunk)], weights)

    across_rows = jnp.broadcast_to(jnp.sum(total_row[...], axis=0, keepdims=True), (128, n_q))
    acc[...] = acc_t[...].T
    zeros = jnp.zeros((heads, span), F32)
    for i in range(rows // 2):
        lo = 2 * heads * i
        high = jnp.concatenate([peak[lo : lo + 2 * heads, :]] * (span // 128), axis=1)
        e = jnp.exp2((tail[lo : lo + 2 * heads, :] - high) * scale2)
        part_sum = e[:, :128]
        for b in range(1, span // 128):
            part_sum = part_sum + e[:, b * 128 : (b + 1) * 128]
        total[lo : lo + 2 * heads, :] = part_sum
        diag = jnp.concatenate(
            [
                jnp.concatenate([e[:heads], zeros], axis=1),
                jnp.concatenate([zeros, e[heads:]], axis=1),
            ],
            axis=0,
        ).astype(BF16)
        vals = suf_vals_ref[2 * i : 2 * i + 2].reshape(2 * span, head_dim)
        acc[lo : lo + 2 * heads, :] += nn_dot(diag, vals)

    norm = across_rows.T + jnp.sum(total[...], axis=1, keepdims=True)
    rowbuf[...] = acc[...] / norm
    for h in range(heads):
        att_ref[:, h * head_dim : (h + 1) * head_dim] = rowbuf[pl.ds(h, rows, stride=heads), :].astype(BF16)
    page_copies(pages_ref, (shrink_ref, expand_ref), list_pos, sem_page, True)
    for c in fetch:
        c.wait()


def kernel_call(kernel, name, out_shape, specs, scratch, operands, mib, flops, bytes_accessed):
    return pl.pallas_call(
        kernel,
        out_shape=out_shape,
        in_specs=specs,
        out_specs=[VMEM] * len(out_shape),
        scratch_shapes=scratch,
        compiler_params=params(mib),
        cost_estimate=pl.CostEstimate(flops=flops, bytes_accessed=bytes_accessed, transcendentals=0),
        name=name,
    )(*operands)


def attend(
    suffix_len, ids, other_ids, pool_slot, queries, prefix_kv, suffix_kv, out_weight, pages, residual, n_tensor, across
):
    rows = queries.shape[0]
    n_z = n_tensor // 2
    in_rows = out_weight.shape[0]
    width = out_weight.shape[1] // n_tensor
    tokens, head_dim = prefix_kv.shape[2:]
    n_q = rows * queries.shape[1] // head_dim
    span = suffix_kv.shape[3]
    prefix_kv, suffix_kv, out_weight = in_hbm(prefix_kv), in_hbm(suffix_kv), in_hbm(out_weight)
    pages, residual = in_hbm(pages), in_hbm(residual)
    query, scores, peak, vals, suf_keys = kernel_call(
        prefix_scores_kernel,
        "prefix_scores",
        [
            pltpu.VMEM((n_q, head_dim), BF16),
            pltpu.VMEM((tokens, n_q), F32),
            pltpu.VMEM((8, n_q), F32),
            pltpu.VMEM((tokens, head_dim), BF16),
            pltpu.VMEM((rows, span, head_dim), BF16),
        ],
        [ANY, ANY, ANY],
        [
            pltpu.VMEM(queries.shape, BF16),
            pltpu.VMEM((tokens, head_dim), BF16),
            pltpu.VMEM((n_q, head_dim), F32),
            pltpu.SemaphoreType.DMA((3,)),
            pltpu.SemaphoreType.DMA((4,)),
        ],
        [in_hbm(queries), prefix_kv, suffix_kv],
        8,
        2 * n_q * tokens * head_dim,
        6 * MIB,
    )
    far = list(range(n_z - 1, -1, -1))
    early = [(0, k) for k in far[: n_z // 2]]
    late = [(1, k) for k in far] + [(0, k) for k in far[n_z // 2 :]]
    tail, high, high_row, vals_t, out_pages, suf_vals, *early_w = kernel_call(
        functools.partial(suffix_scores_kernel, early),
        "suffix_scores",
        [
            pltpu.VMEM((n_q, span), F32),
            pltpu.VMEM((n_q, 128), F32),
            pltpu.VMEM((8, n_q), F32),
            pltpu.VMEM((head_dim, tokens), BF16),
            pltpu.VMEM((2, DISTINCT) + pages.shape[2:], BF16),
            pltpu.VMEM((rows, span, head_dim), BF16),
        ]
        + [pltpu.VMEM((in_rows, width), BF16)] * len(early),
        [SMEM, SMEM, VMEM, VMEM, VMEM, VMEM, ANY, ANY, ANY, ANY],
        [pltpu.SMEM((rows,), jnp.int32)]
        + list_scratch(pool_slot)
        + [
            pltpu.SemaphoreType.DMA((2,)),
            pltpu.SemaphoreType.DMA((2, DISTINCT)),
            pltpu.SemaphoreType.DMA((len(early),)),
        ],
        [other_ids, pool_slot, query, suf_keys, vals, peak, in_hbm(suffix_len), suffix_kv, pages, out_weight],
        8,
        1 << 29,
        7 * MIB,
    )
    other_pages = across(out_pages)
    attended, own_shrink, own_expand, row_slot, slot_mine, res, *late_w = kernel_call(
        functools.partial(values_kernel, late),
        "values",
        [
            pltpu.VMEM(queries.shape, BF16),
            pltpu.VMEM((DISTINCT,) + pages.shape[2:], BF16),
            pltpu.VMEM((DISTINCT,) + pages.shape[2:], BF16),
            pltpu.VMEM((rows, 128), jnp.int32),
            pltpu.VMEM((DISTINCT, 128), jnp.int32),
            pltpu.VMEM((rows, width), BF16),
        ]
        + [pltpu.VMEM((in_rows, width), BF16)] * len(late),
        [SMEM, SMEM, VMEM, VMEM, VMEM, VMEM, VMEM, VMEM, ANY, ANY, ANY],
        [
            pltpu.VMEM((n_q, head_dim), F32),
            pltpu.VMEM((n_q, 128), F32),
            pltpu.VMEM((n_q, head_dim), F32),
            pltpu.VMEM((8, n_q), F32),
            pltpu.VMEM((head_dim, n_q), F32),
        ]
        + list_scratch(pool_slot)
        + [
            pltpu.SemaphoreType.DMA((1,)),
            pltpu.SemaphoreType.DMA((2, DISTINCT)),
            pltpu.SemaphoreType.DMA((len(late),)),
        ],
        [ids, pool_slot, scores, tail, high, high_row, vals_t, suf_vals, pages, out_weight, residual],
        8,
        2 * n_q * tokens * head_dim,
        14 * MIB,
    )
    weights = dict(zip(early + late, list(early_w) + list(late_w)))
    return attended, own_shrink, own_expand, other_pages, row_slot, slot_mine, res, weights


def small_call(kernel, name, out_shape, operands, flops=1 << 27):
    return pl.pallas_call(
        kernel,
        out_shape=out_shape,
        in_specs=[VMEM] * len(operands),
        out_specs=jax.tree.map(lambda _: VMEM, out_shape),
        compiler_params=params(8),
        cost_estimate=pl.CostEstimate(flops=flops, bytes_accessed=2 * MIB, transcendentals=0),
        name=name,
    )(*operands)


def merged(own_ref, other, half, slot_mine):
    rank = own_ref.shape[1]
    tiles = []
    for j in range(DISTINCT):
        hit = jnp.broadcast_to(slot_mine[j : j + 1, :1], (rank, 1)) == 1
        tiles.append(jnp.where(hit, own_ref[j].astype(F32), other[half, j].astype(F32)).astype(BF16))
    return jnp.concatenate(tiles, axis=0)


def lane_place(shape, rank):
    return lax.broadcasted_iota(jnp.int32, shape, 1) // rank


def far_kernel(n, att_ref, row_slot_ref, slot_mine_ref, own_ref, other_ref, *rest):
    w_refs = rest[:n]
    out_ref, rank_ref = rest[n:]
    width = w_refs[0].shape[1]
    attended = att_ref[...]
    for k in range(n):
        out_ref[:, k * width : (k + 1) * width] = nn_dot(attended, w_refs[k][...]).astype(BF16)
    rank = own_ref.shape[1]
    per_tile = 128 // rank
    low = nt_dot(attended, merged(own_ref, other_ref, 0, slot_mine_ref[...]))
    row_slot = row_slot_ref[...]
    place = lane_place(row_slot.shape, rank)
    picked = jnp.zeros(row_slot.shape, F32)
    for tile in range(DISTINCT // per_tile):
        hit = row_slot == place + tile * per_tile
        picked = jnp.where(hit, low[:, tile * 128 : (tile + 1) * 128], picked)
    rank_ref[...] = picked
    out_ref[:, n * width :] = picked.astype(BF16)


def near_kernel(att_ref, w_ref, cross_w_ref, rank_ref, out_ref, cross_ref):
    width = w_ref.shape[1]
    attended = att_ref[...]
    rank = rank_ref[...].astype(BF16)
    for w, out in ((w_ref, out_ref), (cross_w_ref, cross_ref)):
        out[:, :width] = nn_dot(attended, w[...]).astype(BF16)
        out[:, width:] = rank


def block_kernel(att_ref, w_ref, after_ref, out_ref):
    out_ref[...] = nn_dot(att_ref[...], w_ref[...]).astype(BF16)


def add_kernel(spot, att_ref, w_ref, from_ref, rank_ref, out_ref):
    width = w_ref.shape[1]
    both = nn_dot(att_ref[...], w_ref[...]) + from_ref[:, spot * width : (spot + 1) * width].astype(F32)
    out_ref[:, :width] = both.astype(BF16)
    rank_both = rank_ref[...] + from_ref[:, from_ref.shape[1] - 128 :].astype(F32)
    out_ref[:, width:] = rank_both.astype(BF16)


def finish_kernel(*refs):
    att_ref, w_ref, row_slot_ref, slot_mine_ref, own_ref, other_ref = refs[:6]
    rank_ref, far_ref, from_ref, res_ref = refs[6:10]
    moved, out_ref = refs[10:-1], refs[-1]
    rank = own_ref.shape[1]
    per_tile = 128 // rank
    width = w_ref.shape[1]
    low = rank_ref[...] + far_ref[:, far_ref.shape[1] - 128 :].astype(F32)
    for ref in moved:
        low = low + ref[:, width:].astype(F32)
    row_slot = row_slot_ref[...]
    place = lane_place(row_slot.shape, rank)
    tiles = []
    for tile in range(DISTINCT // per_tile):
        tiles.append(jnp.where(row_slot == place + tile * per_tile, low, 0.0).astype(BF16))
    total = nn_dot(jnp.concatenate(tiles, axis=1), merged(own_ref, other_ref, 1, slot_mine_ref[...]))
    total = total + nn_dot(att_ref[...], w_ref[...])
    total = total + (res_ref[...].astype(F32) + from_ref[...].astype(F32))
    for ref in moved:
        total = total + ref[:, :width].astype(F32)
    out_ref[...] = total.astype(BF16)


def place_kernel(n_z, *refs):
    blocks = refs[: 2 * n_z]
    out_ref = refs[2 * n_z]
    width = blocks[0].shape[1]
    me = lax.axis_index("tensor")
    z, y = me // 2, me % 2
    for k in range(n_z):
        for other in range(2):
            where = (z ^ k) * 2 + (y ^ other)
            out_ref[:, pl.ds(pl.multiple_of(where * width, width), width)] = blocks[2 * k + other][...]


def place(blocks, n_tensor):
    rows, width = blocks[0].shape
    return pl.pallas_call(
        functools.partial(place_kernel, n_tensor // 2),
        out_shape=jax.ShapeDtypeStruct((rows, width * n_tensor), BF16),
        in_specs=[VMEM] * n_tensor,
        out_specs=VMEM,
        compiler_params=params(4),
        cost_estimate=pl.CostEstimate(flops=0, bytes_accessed=1 * MIB, transcendentals=0),
        name="place",
    )(*blocks)


def body(
    n_tensor,
    queries,
    prefix_kv,
    suffix_kv,
    suffix_len,
    residual,
    out_weight,
    adapter_pages,
    adapter_ids,
    pool_slot,
):
    n_z = n_tensor // 2

    def along_y(x):
        return lax.ppermute(x, "tensor", [(t, t ^ 1) for t in range(n_tensor)])

    def along_z(x, k):
        return lax.ppermute(x, "tensor", [(t, t ^ (2 * k)) for t in range(n_tensor)])

    def along_both(x, k):
        return lax.ppermute(x, "tensor", [(t, t ^ (2 * k) ^ 1) for t in range(n_tensor)])

    def across(x):
        return lax.ppermute(x, "req", [(0, 1), (1, 0)])

    rows = queries.shape[0]
    width = out_weight.shape[1] // n_tensor
    attended, own_shrink, own_expand, other_pages, row_slot, slot_mine, res, weights = attend(
        suffix_len,
        adapter_ids,
        across(adapter_ids),
        pool_slot,
        queries,
        prefix_kv,
        suffix_kv,
        out_weight,
        adapter_pages,
        residual,
        n_tensor,
        across,
    )
    far = list(range(n_z - 1, 1, -1))
    piece_shape = pltpu.VMEM((rows, width + 128), BF16)
    far_out, rank_own = small_call(
        functools.partial(far_kernel, len(far)),
        "far_blocks",
        [pltpu.VMEM((rows, len(far) * width + 128), BF16), pltpu.VMEM((rows, 128), F32)],
        [attended, row_slot, slot_mine, own_shrink, other_pages] + [weights[1, k] for k in far],
    )
    from_far = along_y(far_out)
    straight, cross = small_call(
        near_kernel,
        "near_blocks",
        [piece_shape, piece_shape],
        [attended, weights[0, 1], weights[1, 1], rank_own],
    )
    moved = [along_z(straight, 1), along_both(cross, 1)]
    for spot, k in enumerate(far):
        piece = small_call(
            functools.partial(add_kernel, spot),
            "add_block",
            piece_shape,
            [attended, weights[0, k], from_far, rank_own],
        )
        moved.append(along_z(piece, k))
    own_far = small_call(
        block_kernel, "own_far_block", pltpu.VMEM((rows, width), BF16), [attended, weights[1, 0], piece]
    )
    from_own = along_y(own_far)
    result = small_call(
        finish_kernel,
        "finish",
        pltpu.VMEM((rows, width), BF16),
        [attended, weights[0, 0], row_slot, slot_mine, own_expand, other_pages, rank_own, from_far, from_own, res]
        + moved,
    )
    held = [result] + [along_z(result, k) for k in range(1, n_z)]
    blocks = []
    for k in range(n_z):
        blocks += [held[k], along_both(result, k) if k < 2 else along_y(held[k])]
    return place(blocks, n_tensor)


def solution(mesh):
    return jax.shard_map(
        functools.partial(body, mesh.shape["tensor"]),
        mesh=mesh,
        in_specs=(
            P(("group", "req"), "tensor"),
            P(("group", "tensor"), None, None, None),
            P(("group", "req"), "tensor", None, None, None),
            P(("group", "req")),
            P(("group", "req"), None),
            P("tensor", None),
            P("req", None, None, "tensor"),
            P(("group", "req")),
            P(),
        ),
        out_specs=P(("group", "req"), None),
        check_vma=False,
    )
```

```python
import functools

import jax
import jax.numpy as jnp
from jax import lax
from jax.experimental import pallas as pl
from jax.experimental.pallas import tpu as pltpu
from jax.sharding import PartitionSpec as P

F32 = jnp.float32
BF16 = jnp.bfloat16
LOG2E = 1.4426950408889634
ANY = pl.BlockSpec(memory_space=pl.ANY)
VMEM = pl.BlockSpec(memory_space=pltpu.VMEM)
SMEM = pl.BlockSpec(memory_space=pltpu.SMEM)
MIB = 1 << 20
DISTINCT = 8


def in_hbm(x):
    return pltpu.with_memory_space_constraint(x, pltpu.HBM)


def params(mib):
    return pltpu.CompilerParams(vmem_limit_bytes=mib * MIB)


def nt_dot(a, b):
    return lax.dot_general(a, b, (((1,), (1,)), ((), ())), preferred_element_type=F32)


def nn_dot(a, b):
    return jnp.dot(a, b, preferred_element_type=F32)


def distinct_list(ids_ref, pool_slot_ref, seen, list_id, list_pos):
    rows = ids_ref.shape[0]
    for i in range(pool_slot_ref.shape[0]):
        seen[i] = 0
    for j in range(DISTINCT + 1):
        list_id[j] = -1
        list_pos[j] = 0
    found = jnp.int32(0)
    for r in range(rows):
        one = ids_ref[r]
        fresh = 1 - seen[one]
        seen[one] = 1
        spot = jnp.minimum(found, DISTINCT)
        list_id[spot] = jnp.where(fresh == 1, one, list_id[spot])
        list_pos[spot] = jnp.where(fresh == 1, pool_slot_ref[one], list_pos[spot])
        found = found + fresh


def list_scratch(pool_slot):
    return [
        pltpu.SMEM((pool_slot.shape[0],), jnp.int32),
        pltpu.SMEM((DISTINCT + 1,), jnp.int32),
        pltpu.SMEM((DISTINCT + 1,), jnp.int32),
    ]


def page_copies(pages_ref, outs, list_pos, sem, wait):
    pool = pages_ref.shape[0]
    me = lax.axis_index("req")
    for j in range(DISTINCT):
        pos = list_pos[j]

        @pl.when(pos // pool == me)
        def _():
            for i, out in enumerate(outs):
                copy = pltpu.make_async_copy(pages_ref.at[pos % pool, i], out.at[j], sem.at[i, j])
                if wait:
                    copy.wait()
                else:
                    copy.start()


def prefix_scores_kernel(
    q_ref, prefix_ref, suffix_ref, query_ref, scores_ref, peak_ref, vals_ref, suf_keys_ref, qbuf, keys, rowbuf, sem, sem_keys
):
    rows = q_ref.shape[0]
    tokens, head_dim = keys.shape
    heads = q_ref.shape[1] // head_dim
    parts = sem_keys.shape[0]
    size = tokens // parts
    key_copies = [
        pltpu.make_async_copy(
            prefix_ref.at[0, 0, pl.ds(j * size, size)], keys.at[pl.ds(j * size, size)], sem_keys.at[j]
        )
        for j in range(parts)
    ]
    fetch_q = pltpu.make_async_copy(q_ref, qbuf, sem.at[0])
    fetch = [
        pltpu.make_async_copy(suffix_ref.at[:, 0, 0], suf_keys_ref, sem.at[1]),
        pltpu.make_async_copy(prefix_ref.at[0, 1], vals_ref, sem.at[2]),
    ]
    for c in [fetch_q] + key_copies + fetch:
        c.start()
    fetch_q.wait()
    for h in range(heads):
        rowbuf[pl.ds(h, rows, stride=heads), :] = qbuf[:, h * head_dim : (h + 1) * head_dim].astype(F32)
    query = rowbuf[...].astype(BF16)
    query_ref[...] = query
    best = jnp.full(peak_ref.shape, -3.0e38, F32)
    step = min(512, size)
    for j in range(parts):
        key_copies[j].wait()
        for base in range(j * size, (j + 1) * size, step):
            block = nt_dot(keys[base : base + step, :], query)
            scores_ref[base : base + step, :] = block
            best = jnp.maximum(best, jnp.max(block.reshape(step // 8, 8, block.shape[1]), axis=0))
    peak_ref[...] = best
    for c in fetch:
        c.wait()


def weight_copies(weight_ref, outs, spots, sem):
    me = lax.axis_index("tensor")
    z, y = me // 2, me % 2
    copies = []
    for i, (side, k) in enumerate(spots):
        width = outs[i].shape[1]
        column = pl.multiple_of(((z ^ k) * 2 + (y ^ side)) * width, width)
        copies.append(pltpu.make_async_copy(weight_ref.at[:, pl.ds(column, width)], outs[i], sem.at[i]))
    return copies


def suffix_scores_kernel(spots, ids_ref, slot_ref, query_ref, suf_keys_ref, peak_ref, *rest):
    len_ref, suffix_ref, pages_ref, weight_ref = rest[:4]
    tail_ref, high_ref, high_row_ref, out_pages_ref, suf_vals_ref = rest[4:9]
    w_refs = rest[9 : 9 + len(spots)]
    lens, seen, list_id, list_pos, sem, sem_page, sem_w = rest[9 + len(spots) :]
    rows, span, head_dim = suf_keys_ref.shape
    heads = query_ref.shape[0] // rows
    fetch_len = pltpu.make_async_copy(len_ref, lens, sem.at[1])
    fetch_len.start()
    fetch = [pltpu.make_async_copy(suffix_ref.at[:, 0, 1], suf_vals_ref, sem.at[0])]
    fetch += weight_copies(weight_ref, w_refs, spots, sem_w)
    for c in fetch:
        c.start()
    distinct_list(ids_ref, slot_ref, seen, list_id, list_pos)
    outs = (out_pages_ref.at[0], out_pages_ref.at[1])
    page_copies(pages_ref, outs, list_pos, sem_page, False)
    query = query_ref[...]
    lanes = lax.broadcasted_iota(jnp.int32, (heads, span), 1)
    fetch_len.wait()
    for i in range(rows // 2):
        keys = suf_keys_ref[2 * i : 2 * i + 2].reshape(2 * span, head_dim)
        both = nt_dot(query[2 * heads * i : 2 * heads * (i + 1)], keys)
        for a in range(2):
            mine = both[a * heads : (a + 1) * heads, a * span : (a + 1) * span]
            row = 2 * i + a
            tail_ref[row * heads : (row + 1) * heads, :] = jnp.where(lanes < lens[row], mine, -1.0e30)
    best = jnp.maximum(tail_ref[:, :128], tail_ref[:, 128:256])
    for b in range(2, span // 128):
        best = jnp.maximum(best, tail_ref[:, b * 128 : (b + 1) * 128])
    across_rows = jnp.broadcast_to(jnp.max(peak_ref[...], axis=0, keepdims=True), (128, peak_ref.shape[1]))
    high = jnp.maximum(across_rows.T, jnp.max(best, axis=1, keepdims=True))
    high_ref[...] = high
    high_row_ref[...] = high.T[:8]
    page_copies(pages_ref, outs, list_pos, sem_page, True)
    for c in fetch:
        c.wait()


def values_kernel(spots, ids_ref, slot_ref, scores, tail, peak, peak_row, vals_ref, suf_vals_ref, *rest):
    pages_ref, weight_ref, residual_ref = rest[:3]
    att_ref, shrink_ref, expand_ref, row_slot_ref, slot_mine_ref, res_ref = rest[3:9]
    w_refs = rest[9 : 9 + len(spots)]
    rowbuf, total, acc, seen, list_id, list_pos, sem, sem_page, sem_w = rest[9 + len(spots) :]
    rows, span, head_dim = suf_vals_ref.shape
    tokens = vals_ref.shape[0]
    heads = att_ref.shape[1] // head_dim
    width = res_ref.shape[1]
    me = lax.axis_index("tensor")
    scale2 = float(head_dim) ** -0.5 * LOG2E
    fetch = weight_copies(weight_ref, w_refs, spots, sem_w)
    fetch.append(
        pltpu.make_async_copy(
            residual_ref.at[:, pl.ds(pl.multiple_of(me * width, width), width)], res_ref, sem.at[0]
        )
    )
    for c in fetch:
        c.start()
    distinct_list(ids_ref, slot_ref, seen, list_id, list_pos)
    page_copies(pages_ref, (shrink_ref, expand_ref), list_pos, sem_page, False)
    row_index = lax.broadcasted_iota(jnp.int32, (rows, 128), 0)
    row_id = jnp.full((rows, 128), -2, jnp.int32)
    for r in range(rows):
        row_id = jnp.where(row_index == r, ids_ref[r], row_id)
    row_slot = jnp.full((rows, 128), -1, jnp.int32)
    slot_index = lax.broadcasted_iota(jnp.int32, (DISTINCT, 128), 0)
    slot_mine = jnp.zeros((DISTINCT, 128), jnp.int32)
    mine = lax.axis_index("req")
    for j in range(DISTINCT):
        row_slot = jnp.where(row_id == list_id[j], j, row_slot)
        owned = (list_pos[j] // pages_ref.shape[0] == mine).astype(jnp.int32)
        slot_mine = jnp.where(slot_index == j, owned, slot_mine)
    row_slot_ref[...] = row_slot
    slot_mine_ref[...] = slot_mine

    n_q = acc.shape[0]
    chunk = min(1024, tokens)
    high_row = peak_row[...]
    total_row = jnp.zeros((8, n_q), F32)
    acc_t = jnp.zeros((head_dim, n_q), F32)
    for base in range(0, tokens, chunk):
        block = scores[base : base + chunk, :].reshape(chunk // 8, 8, n_q)
        e = jnp.exp2((block - high_row[None]) * scale2)
        total_row = total_row + jnp.sum(e, axis=0)
        weights = e.reshape(chunk, n_q).astype(BF16)
        acc_t = acc_t + nn_dot(vals_ref[base : base + chunk, :].T, weights)
    across_rows = jnp.broadcast_to(jnp.sum(total_row, axis=0, keepdims=True), (128, n_q))
    acc[...] = acc_t.T
    zeros = jnp.zeros((heads, span), F32)
    for i in range(rows // 2):
        lo = 2 * heads * i
        high = jnp.concatenate([peak[lo : lo + 2 * heads, :]] * (span // 128), axis=1)
        e = jnp.exp2((tail[lo : lo + 2 * heads, :] - high) * scale2)
        part_sum = e[:, :128]
        for b in range(1, span // 128):
            part_sum = part_sum + e[:, b * 128 : (b + 1) * 128]
        total[lo : lo + 2 * heads, :] = part_sum
        diag = jnp.concatenate(
            [
                jnp.concatenate([e[:heads], zeros], axis=1),
                jnp.concatenate([zeros, e[heads:]], axis=1),
            ],
            axis=0,
        ).astype(BF16)
        vals = suf_vals_ref[2 * i : 2 * i + 2].reshape(2 * span, head_dim)
        acc[lo : lo + 2 * heads, :] += nn_dot(diag, vals)

    norm = across_rows.T + jnp.sum(total[...], axis=1, keepdims=True)
    rowbuf[...] = acc[...] / norm
    for h in range(heads):
        att_ref[:, h * head_dim : (h + 1) * head_dim] = rowbuf[pl.ds(h, rows, stride=heads), :].astype(BF16)
    page_copies(pages_ref, (shrink_ref, expand_ref), list_pos, sem_page, True)
    for c in fetch:
        c.wait()


def kernel_call(kernel, name, out_shape, specs, scratch, operands, mib, flops, bytes_accessed):
    return pl.pallas_call(
        kernel,
        out_shape=out_shape,
        in_specs=specs,
        out_specs=[VMEM] * len(out_shape),
        scratch_shapes=scratch,
        compiler_params=params(mib),
        cost_estimate=pl.CostEstimate(flops=flops, bytes_accessed=bytes_accessed, transcendentals=0),
        name=name,
    )(*operands)


def attend(
    suffix_len, ids, other_ids, pool_slot, queries, prefix_kv, suffix_kv, out_weight, pages, residual, n_tensor, across
):
    rows = queries.shape[0]
    n_z = n_tensor // 2
    in_rows = out_weight.shape[0]
    width = out_weight.shape[1] // n_tensor
    tokens, head_dim = prefix_kv.shape[2:]
    n_q = rows * queries.shape[1] // head_dim
    span = suffix_kv.shape[3]
    prefix_kv, suffix_kv, out_weight = in_hbm(prefix_kv), in_hbm(suffix_kv), in_hbm(out_weight)
    pages, residual = in_hbm(pages), in_hbm(residual)
    query, scores, peak, vals, suf_keys = kernel_call(
        prefix_scores_kernel,
        "prefix_scores",
        [
            pltpu.VMEM((n_q, head_dim), BF16),
            pltpu.VMEM((tokens, n_q), F32),
            pltpu.VMEM((8, n_q), F32),
            pltpu.VMEM((tokens, head_dim), BF16),
            pltpu.VMEM((rows, span, head_dim), BF16),
        ],
        [ANY, ANY, ANY],
        [
            pltpu.VMEM(queries.shape, BF16),
            pltpu.VMEM((tokens, head_dim), BF16),
            pltpu.VMEM((n_q, head_dim), F32),
            pltpu.SemaphoreType.DMA((3,)),
            pltpu.SemaphoreType.DMA((4,)),
        ],
        [in_hbm(queries), prefix_kv, suffix_kv],
        8,
        2 * n_q * tokens * head_dim,
        6 * MIB,
    )
    far = list(range(n_z - 1, -1, -1))
    early = [(0, k) for k in far[: n_z // 2]]
    late = [(1, k) for k in far] + [(0, k) for k in far[n_z // 2 :]]
    tail, high, high_row, out_pages, suf_vals, *early_w = kernel_call(
        functools.partial(suffix_scores_kernel, early),
        "suffix_scores",
        [
            pltpu.VMEM((n_q, span), F32),
            pltpu.VMEM((n_q, 128), F32),
            pltpu.VMEM((8, n_q), F32),
            pltpu.VMEM((2, DISTINCT) + pages.shape[2:], BF16),
            pltpu.VMEM((rows, span, head_dim), BF16),
        ]
        + [pltpu.VMEM((in_rows, width), BF16)] * len(early),
        [SMEM, SMEM, VMEM, VMEM, VMEM, ANY, ANY, ANY, ANY],
        [pltpu.SMEM((rows,), jnp.int32)]
        + list_scratch(pool_slot)
        + [
            pltpu.SemaphoreType.DMA((2,)),
            pltpu.SemaphoreType.DMA((2, DISTINCT)),
            pltpu.SemaphoreType.DMA((len(early),)),
        ],
        [other_ids, pool_slot, query, suf_keys, peak, in_hbm(suffix_len), suffix_kv, pages, out_weight],
        8,
        1 << 29,
        7 * MIB,
    )
    other_pages = across(out_pages)
    attended, own_shrink, own_expand, row_slot, slot_mine, res, *late_w = kernel_call(
        functools.partial(values_kernel, late),
        "values",
        [
            pltpu.VMEM(queries.shape, BF16),
            pltpu.VMEM((DISTINCT,) + pages.shape[2:], BF16),
            pltpu.VMEM((DISTINCT,) + pages.shape[2:], BF16),
            pltpu.VMEM((rows, 128), jnp.int32),
            pltpu.VMEM((DISTINCT, 128), jnp.int32),
            pltpu.VMEM((rows, width), BF16),
        ]
        + [pltpu.VMEM((in_rows, width), BF16)] * len(late),
        [SMEM, SMEM, VMEM, VMEM, VMEM, VMEM, VMEM, VMEM, ANY, ANY, ANY],
        [
            pltpu.VMEM((n_q, head_dim), F32),
            pltpu.VMEM((n_q, 128), F32),
            pltpu.VMEM((n_q, head_dim), F32),
        ]
        + list_scratch(pool_slot)
        + [
            pltpu.SemaphoreType.DMA((1,)),
            pltpu.SemaphoreType.DMA((2, DISTINCT)),
            pltpu.SemaphoreType.DMA((len(late),)),
        ],
        [ids, pool_slot, scores, tail, high, high_row, vals, suf_vals, pages, out_weight, residual],
        8,
        2 * n_q * tokens * head_dim,
        14 * MIB,
    )
    weights = dict(zip(early + late, list(early_w) + list(late_w)))
    return attended, own_shrink, own_expand, other_pages, row_slot, slot_mine, res, weights


def small_call(kernel, name, out_shape, operands, flops=1 << 27):
    return pl.pallas_call(
        kernel,
        out_shape=out_shape,
        in_specs=[VMEM] * len(operands),
        out_specs=jax.tree.map(lambda _: VMEM, out_shape),
        compiler_params=params(8),
        cost_estimate=pl.CostEstimate(flops=flops, bytes_accessed=2 * MIB, transcendentals=0),
        name=name,
    )(*operands)


def merged(own_ref, other, half, slot_mine):
    rank = own_ref.shape[1]
    tiles = []
    for j in range(DISTINCT):
        hit = jnp.broadcast_to(slot_mine[j : j + 1, :1], (rank, 1)) == 1
        tiles.append(jnp.where(hit, own_ref[j].astype(F32), other[half, j].astype(F32)).astype(BF16))
    return jnp.concatenate(tiles, axis=0)


def lane_place(shape, rank):
    return lax.broadcasted_iota(jnp.int32, shape, 1) // rank


def far_kernel(n, att_ref, row_slot_ref, slot_mine_ref, own_ref, other_ref, *rest):
    w_refs = rest[:n]
    out_ref, rank_ref = rest[n:]
    width = w_refs[0].shape[1]
    attended = att_ref[...]
    for k in range(n):
        out_ref[:, k * width : (k + 1) * width] = nn_dot(attended, w_refs[k][...]).astype(BF16)
    rank = own_ref.shape[1]
    per_tile = 128 // rank
    low = nt_dot(attended, merged(own_ref, other_ref, 0, slot_mine_ref[...]))
    row_slot = row_slot_ref[...]
    place = lane_place(row_slot.shape, rank)
    picked = jnp.zeros(row_slot.shape, F32)
    for tile in range(DISTINCT // per_tile):
        hit = row_slot == place + tile * per_tile
        picked = jnp.where(hit, low[:, tile * 128 : (tile + 1) * 128], picked)
    rank_ref[...] = picked
    out_ref[:, n * width :] = picked.astype(BF16)


def near_kernel(att_ref, w_ref, cross_w_ref, rank_ref, out_ref, cross_ref):
    width = w_ref.shape[1]
    attended = att_ref[...]
    rank = rank_ref[...].astype(BF16)
    for w, out in ((w_ref, out_ref), (cross_w_ref, cross_ref)):
        out[:, :width] = nn_dot(attended, w[...]).astype(BF16)
        out[:, width:] = rank


def block_kernel(att_ref, w_ref, after_ref, out_ref):
    out_ref[...] = nn_dot(att_ref[...], w_ref[...]).astype(BF16)


def add_kernel(spot, n_near, att_ref, w_ref, from_ref, rank_ref, *rest):
    near_refs, out_ref = rest[:n_near], rest[-1]
    width = w_ref.shape[1]
    both = nn_dot(att_ref[...], w_ref[...]) + from_ref[:, spot * width : (spot + 1) * width].astype(F32)
    out_ref[:, :width] = both.astype(BF16)
    if near_refs:
        low = rank_ref[...] + from_ref[:, from_ref.shape[1] - 128 :].astype(F32)
        for ref in near_refs:
            low = low + ref[:, width:].astype(F32)
        out_ref[:, width:] = low.astype(BF16)


def finish_kernel(*refs):
    att_ref, w_ref, row_slot_ref, slot_mine_ref, own_ref, other_ref = refs[:6]
    rank_ref, far_ref, from_ref, res_ref = refs[6:10]
    moved, out_ref = refs[10:-1], refs[-1]
    rank = own_ref.shape[1]
    per_tile = 128 // rank
    width = w_ref.shape[1]
    low = rank_ref[...] + far_ref[:, far_ref.shape[1] - 128 :].astype(F32)
    for ref in moved:
        if ref.shape[1] > width:
            low = low + ref[:, width:].astype(F32)
    row_slot = row_slot_ref[...]
    place = lane_place(row_slot.shape, rank)
    tiles = []
    for tile in range(DISTINCT // per_tile):
        tiles.append(jnp.where(row_slot == place + tile * per_tile, low, 0.0).astype(BF16))
    total = nn_dot(jnp.concatenate(tiles, axis=1), merged(own_ref, other_ref, 1, slot_mine_ref[...]))
    total = total + nn_dot(att_ref[...], w_ref[...])
    total = total + (res_ref[...].astype(F32) + from_ref[...].astype(F32))
    for ref in moved:
        total = total + ref[:, :width].astype(F32)
    out_ref[...] = total.astype(BF16)


def place_kernel(spots, *refs):
    blocks, out_ref = refs[:-1], refs[-1]
    width = blocks[0].shape[1]
    me = lax.axis_index("tensor")
    z, y = me // 2, me % 2
    for block, (k, side) in zip(blocks, spots):
        where = (z ^ k) * 2 + (y ^ side)
        out_ref[:, pl.ds(pl.multiple_of(where * width, width), width)] = block[...]


def place(blocks, spots, n_tensor):
    rows, width = blocks[0].shape
    return pl.pallas_call(
        functools.partial(place_kernel, spots),
        out_shape=jax.ShapeDtypeStruct((rows, width * n_tensor), BF16),
        in_specs=[VMEM] * n_tensor,
        out_specs=VMEM,
        compiler_params=params(4),
        cost_estimate=pl.CostEstimate(flops=0, bytes_accessed=1 * MIB, transcendentals=0),
        name="place",
    )(*blocks)


def body(
    n_tensor,
    queries,
    prefix_kv,
    suffix_kv,
    suffix_len,
    residual,
    out_weight,
    adapter_pages,
    adapter_ids,
    pool_slot,
):
    n_z = n_tensor // 2

    def along_y(x):
        return lax.ppermute(x, "tensor", [(t, t ^ 1) for t in range(n_tensor)])

    def along_z(x, k):
        return lax.ppermute(x, "tensor", [(t, t ^ (2 * k)) for t in range(n_tensor)])

    def along_both(x, k):
        return lax.ppermute(x, "tensor", [(t, t ^ (2 * k) ^ 1) for t in range(n_tensor)])

    def across(x):
        return lax.ppermute(x, "req", [(0, 1), (1, 0)])

    rows = queries.shape[0]
    width = out_weight.shape[1] // n_tensor
    attended, own_shrink, own_expand, other_pages, row_slot, slot_mine, res, weights = attend(
        suffix_len,
        adapter_ids,
        across(adapter_ids),
        pool_slot,
        queries,
        prefix_kv,
        suffix_kv,
        out_weight,
        adapter_pages,
        residual,
        n_tensor,
        across,
    )
    far = list(range(n_z - 1, 1, -1))
    piece_shape = pltpu.VMEM((rows, width + 128), BF16)
    far_out, rank_own = small_call(
        functools.partial(far_kernel, len(far)),
        "far_blocks",
        [pltpu.VMEM((rows, len(far) * width + 128), BF16), pltpu.VMEM((rows, 128), F32)],
        [attended, row_slot, slot_mine, own_shrink, other_pages] + [weights[1, k] for k in far],
    )
    from_far = along_y(far_out)
    straight, cross = small_call(
        near_kernel,
        "near_blocks",
        [piece_shape, piece_shape],
        [attended, weights[0, 1], weights[1, 1], rank_own],
    )
    moved = [along_z(straight, 1), along_both(cross, 1)]
    near = list(moved)
    after = []
    for spot, k in enumerate(far):
        beside = near if k % 2 else []
        piece = small_call(
            functools.partial(add_kernel, spot, len(beside)),
            "add_block",
            piece_shape if k % 2 else pltpu.VMEM((rows, width), BF16),
            [attended, weights[0, k], from_far, rank_own] + beside + after,
        )
        moved.append(along_z(piece, k))
        after = [piece]
    own_far = small_call(
        block_kernel, "own_far_block", pltpu.VMEM((rows, width), BF16), [attended, weights[1, 0], piece]
    )
    from_own = along_y(own_far)
    result = small_call(
        finish_kernel,
        "finish",
        pltpu.VMEM((rows, width), BF16),
        [attended, weights[0, 0], row_slot, slot_mine, own_expand, other_pages, rank_own, from_far, from_own, res]
        + moved,
    )
    held = [result] + [along_z(result, k) for k in range(1, n_z)]
    crossed = [along_both(result, k) if k < 3 else along_y(held[k]) for k in range(n_z)]
    spots = [(0, 0)] + [(k, side) for k in range(1, n_z) for side in (0, 1)]
    spots.insert(len(spots) - 2, (0, 1))
    return place([(crossed if side else held)[k] for k, side in spots], spots, n_tensor)


def solution(mesh):
    return jax.shard_map(
        functools.partial(body, mesh.shape["tensor"]),
        mesh=mesh,
        in_specs=(
            P(("group", "req"), "tensor"),
            P(("group", "tensor"), None, None, None),
            P(("group", "req"), "tensor", None, None, None),
            P(("group", "req")),
            P(("group", "req"), None),
            P("tensor", None),
            P("req", None, None, "tensor"),
            P(("group", "req")),
            P(),
        ),
        out_specs=P(("group", "req"), None),
        check_vma=False,
    )
```

```python
import functools

import jax
import jax.numpy as jnp
from jax import lax
from jax.experimental import pallas as pl
from jax.experimental.pallas import tpu as pltpu
from jax.sharding import PartitionSpec as P

F32 = jnp.float32
BF16 = jnp.bfloat16
LOG2E = 1.4426950408889634
ANY = pl.BlockSpec(memory_space=pl.ANY)
VMEM = pl.BlockSpec(memory_space=pltpu.VMEM)
SMEM = pl.BlockSpec(memory_space=pltpu.SMEM)
MIB = 1 << 20
DISTINCT = 8


def in_hbm(x):
    return pltpu.with_memory_space_constraint(x, pltpu.HBM)


def params(mib):
    return pltpu.CompilerParams(vmem_limit_bytes=mib * MIB)


def nt_dot(a, b):
    return lax.dot_general(a, b, (((1,), (1,)), ((), ())), preferred_element_type=F32)


def nn_dot(a, b):
    return jnp.dot(a, b, preferred_element_type=F32)


def distinct_list(ids_ref, pool_slot_ref, seen, list_id, list_pos):
    rows = ids_ref.shape[0]
    for i in range(pool_slot_ref.shape[0]):
        seen[i] = 0
    for j in range(DISTINCT + 1):
        list_id[j] = -1
        list_pos[j] = 0
    found = jnp.int32(0)
    for r in range(rows):
        one = ids_ref[r]
        fresh = 1 - seen[one]
        seen[one] = 1
        spot = jnp.minimum(found, DISTINCT)
        list_id[spot] = jnp.where(fresh == 1, one, list_id[spot])
        list_pos[spot] = jnp.where(fresh == 1, pool_slot_ref[one], list_pos[spot])
        found = found + fresh


def list_scratch(pool_slot):
    return [
        pltpu.SMEM((pool_slot.shape[0],), jnp.int32),
        pltpu.SMEM((DISTINCT + 1,), jnp.int32),
        pltpu.SMEM((DISTINCT + 1,), jnp.int32),
    ]


def page_copies(pages_ref, outs, list_pos, sem, wait):
    pool = pages_ref.shape[0]
    me = lax.axis_index("req")
    for j in range(DISTINCT):
        pos = list_pos[j]

        @pl.when(pos // pool == me)
        def _():
            for i, out in enumerate(outs):
                copy = pltpu.make_async_copy(pages_ref.at[pos % pool, i], out.at[j], sem.at[i, j])
                if wait:
                    copy.wait()
                else:
                    copy.start()


def prefix_scores_kernel(
    q_ref, prefix_ref, suffix_ref, query_ref, scores_ref, peak_ref, vals_ref, suf_keys_ref, qbuf, keys, rowbuf, sem, sem_keys
):
    rows = q_ref.shape[0]
    tokens, head_dim = keys.shape
    heads = q_ref.shape[1] // head_dim
    parts = sem_keys.shape[0]
    size = tokens // parts
    key_copies = [
        pltpu.make_async_copy(
            prefix_ref.at[0, 0, pl.ds(j * size, size)], keys.at[pl.ds(j * size, size)], sem_keys.at[j]
        )
        for j in range(parts)
    ]
    fetch_q = pltpu.make_async_copy(q_ref, qbuf, sem.at[0])
    fetch = [
        pltpu.make_async_copy(suffix_ref.at[:, 0, 0], suf_keys_ref, sem.at[1]),
        pltpu.make_async_copy(prefix_ref.at[0, 1], vals_ref, sem.at[2]),
    ]
    for c in [fetch_q] + key_copies + fetch:
        c.start()
    fetch_q.wait()
    for h in range(heads):
        rowbuf[pl.ds(h, rows, stride=heads), :] = qbuf[:, h * head_dim : (h + 1) * head_dim].astype(F32)
    query = rowbuf[...].astype(BF16)
    query_ref[...] = query
    best = jnp.full(peak_ref.shape, -3.0e38, F32)
    step = min(512, size)
    for j in range(parts):
        key_copies[j].wait()
        for base in range(j * size, (j + 1) * size, step):
            block = nt_dot(keys[base : base + step, :], query)
            scores_ref[base : base + step, :] = block
            best = jnp.maximum(best, jnp.max(block.reshape(step // 8, 8, block.shape[1]), axis=0))
    peak_ref[...] = best
    for c in fetch:
        c.wait()


def weight_copies(weight_ref, outs, spots, sem):
    me = lax.axis_index("tensor")
    z, y = me // 2, me % 2
    copies = []
    for i, (side, k) in enumerate(spots):
        width = outs[i].shape[1]
        column = pl.multiple_of(((z ^ k) * 2 + (y ^ side)) * width, width)
        copies.append(pltpu.make_async_copy(weight_ref.at[:, pl.ds(column, width)], outs[i], sem.at[i]))
    return copies


def suffix_scores_kernel(spots, ids_ref, slot_ref, query_ref, suf_keys_ref, vals_ref, peak_ref, *rest):
    len_ref, suffix_ref, pages_ref, weight_ref = rest[:4]
    tail_ref, high_ref, high_row_ref, vals_t_ref, out_pages_ref, suf_vals_ref = rest[4:10]
    w_refs = rest[10 : 10 + len(spots)]
    lens, seen, list_id, list_pos, sem, sem_page, sem_w = rest[10 + len(spots) :]
    rows, span, head_dim = suf_keys_ref.shape
    tokens = vals_ref.shape[0]
    heads = query_ref.shape[0] // rows
    fetch_len = pltpu.make_async_copy(len_ref, lens, sem.at[1])
    fetch_len.start()
    fetch = [pltpu.make_async_copy(suffix_ref.at[:, 0, 1], suf_vals_ref, sem.at[0])]
    fetch += weight_copies(weight_ref, w_refs, spots, sem_w)
    distinct_list(ids_ref, slot_ref, seen, list_id, list_pos)
    outs = (out_pages_ref.at[0], out_pages_ref.at[1])
    page_copies(pages_ref, outs, list_pos, sem_page, False)
    for c in fetch:
        c.start()
    query = query_ref[...]
    lanes = lax.broadcasted_iota(jnp.int32, (heads, span), 1)
    fetch_len.wait()
    for i in range(rows // 2):
        keys = suf_keys_ref[2 * i : 2 * i + 2].reshape(2 * span, head_dim)
        both = nt_dot(query[2 * heads * i : 2 * heads * (i + 1)], keys)
        for a in range(2):
            mine = both[a * heads : (a + 1) * heads, a * span : (a + 1) * span]
            row = 2 * i + a
            tail_ref[row * heads : (row + 1) * heads, :] = jnp.where(lanes < lens[row], mine, -1.0e30)
    step = min(1024, tokens)
    for base in range(0, tokens, step):
        vals_t_ref[:, base : base + step] = vals_ref[base : base + step, :].astype(F32).T.astype(BF16)
    best = jnp.maximum(tail_ref[:, :128], tail_ref[:, 128:256])
    for b in range(2, span // 128):
        best = jnp.maximum(best, tail_ref[:, b * 128 : (b + 1) * 128])
    across_rows = jnp.broadcast_to(jnp.max(peak_ref[...], axis=0, keepdims=True), (128, peak_ref.shape[1]))
    high = jnp.maximum(across_rows.T, jnp.max(best, axis=1, keepdims=True))
    high_ref[...] = high
    high_row_ref[...] = high.T[:8]
    page_copies(pages_ref, outs, list_pos, sem_page, True)
    for c in fetch:
        c.wait()


def values_kernel(spots, ids_ref, slot_ref, scores, tail, peak, peak_row, vals_t_ref, suf_vals_ref, *rest):
    pages_ref, weight_ref, residual_ref = rest[:3]
    att_ref, shrink_ref, expand_ref, row_slot_ref, slot_mine_ref, res_ref = rest[3:9]
    w_refs = rest[9 : 9 + len(spots)]
    rowbuf, total, acc, total_row, acc_t, seen, list_id, list_pos, sem, sem_page, sem_w = rest[9 + len(spots) :]
    rows, span, head_dim = suf_vals_ref.shape
    tokens = vals_t_ref.shape[1]
    heads = att_ref.shape[1] // head_dim
    width = res_ref.shape[1]
    me = lax.axis_index("tensor")
    scale2 = float(head_dim) ** -0.5 * LOG2E
    fetch = weight_copies(weight_ref, w_refs, spots, sem_w)
    fetch.append(
        pltpu.make_async_copy(
            residual_ref.at[:, pl.ds(pl.multiple_of(me * width, width), width)], res_ref, sem.at[0]
        )
    )
    for c in fetch:
        c.start()
    distinct_list(ids_ref, slot_ref, seen, list_id, list_pos)
    page_copies(pages_ref, (shrink_ref, expand_ref), list_pos, sem_page, False)
    row_index = lax.broadcasted_iota(jnp.int32, (rows, 128), 0)
    row_id = jnp.full((rows, 128), -2, jnp.int32)
    for r in range(rows):
        row_id = jnp.where(row_index == r, ids_ref[r], row_id)
    row_slot = jnp.full((rows, 128), -1, jnp.int32)
    slot_index = lax.broadcasted_iota(jnp.int32, (DISTINCT, 128), 0)
    slot_mine = jnp.zeros((DISTINCT, 128), jnp.int32)
    mine = lax.axis_index("req")
    for j in range(DISTINCT):
        row_slot = jnp.where(row_id == list_id[j], j, row_slot)
        owned = (list_pos[j] // pages_ref.shape[0] == mine).astype(jnp.int32)
        slot_mine = jnp.where(slot_index == j, owned, slot_mine)
    row_slot_ref[...] = row_slot
    slot_mine_ref[...] = slot_mine

    total_row[...] = jnp.zeros(total_row.shape, F32)
    acc_t[...] = jnp.zeros(acc_t.shape, F32)
    n_q = acc_t.shape[1]
    chunk = min(2048, tokens)

    @pl.loop(0, tokens // chunk)
    def _(i):
        base = pl.multiple_of(i * chunk, chunk)
        high_row = peak_row[...]
        block = scores[pl.ds(base, chunk), :].reshape(chunk // 8, 8, n_q)
        e = jnp.exp2((block - high_row[None]) * scale2)
        total_row[...] += jnp.sum(e, axis=0)
        weights = e.reshape(chunk, n_q).astype(BF16)
        acc_t[...] += nn_dot(vals_t_ref[:, pl.ds(base, chunk)], weights)

    across_rows = jnp.broadcast_to(jnp.sum(total_row[...], axis=0, keepdims=True), (128, n_q))
    acc[...] = acc_t[...].T
    zeros = jnp.zeros((heads, span), F32)
    for i in range(rows // 2):
        lo = 2 * heads * i
        high = jnp.concatenate([peak[lo : lo + 2 * heads, :]] * (span // 128), axis=1)
        e = jnp.exp2((tail[lo : lo + 2 * heads, :] - high) * scale2)
        part_sum = e[:, :128]
        for b in range(1, span // 128):
            part_sum = part_sum + e[:, b * 128 : (b + 1) * 128]
        total[lo : lo + 2 * heads, :] = part_sum
        diag = jnp.concatenate(
            [
                jnp.concatenate([e[:heads], zeros], axis=1),
                jnp.concatenate([zeros, e[heads:]], axis=1),
            ],
            axis=0,
        ).astype(BF16)
        vals = suf_vals_ref[2 * i : 2 * i + 2].reshape(2 * span, head_dim)
        acc[lo : lo + 2 * heads, :] += nn_dot(diag, vals)

    norm = across_rows.T + jnp.sum(total[...], axis=1, keepdims=True)
    rowbuf[...] = acc[...] / norm
    for h in range(heads):
        att_ref[:, h * head_dim : (h + 1) * head_dim] = rowbuf[pl.ds(h, rows, stride=heads), :].astype(BF16)
    page_copies(pages_ref, (shrink_ref, expand_ref), list_pos, sem_page, True)
    for c in fetch:
        c.wait()


def kernel_call(kernel, name, out_shape, specs, scratch, operands, mib, flops, bytes_accessed):
    return pl.pallas_call(
        kernel,
        out_shape=out_shape,
        in_specs=specs,
        out_specs=[VMEM] * len(out_shape),
        scratch_shapes=scratch,
        compiler_params=params(mib),
        cost_estimate=pl.CostEstimate(flops=flops, bytes_accessed=bytes_accessed, transcendentals=0),
        name=name,
    )(*operands)


def attend(
    suffix_len, ids, other_ids, pool_slot, queries, prefix_kv, suffix_kv, out_weight, pages, residual, n_tensor, across
):
    rows = queries.shape[0]
    n_z = n_tensor // 2
    in_rows = out_weight.shape[0]
    width = out_weight.shape[1] // n_tensor
    tokens, head_dim = prefix_kv.shape[2:]
    n_q = rows * queries.shape[1] // head_dim
    span = suffix_kv.shape[3]
    prefix_kv, suffix_kv, out_weight = in_hbm(prefix_kv), in_hbm(suffix_kv), in_hbm(out_weight)
    pages, residual = in_hbm(pages), in_hbm(residual)
    query, scores, peak, vals, suf_keys = kernel_call(
        prefix_scores_kernel,
        "prefix_scores",
        [
            pltpu.VMEM((n_q, head_dim), BF16),
            pltpu.VMEM((tokens, n_q), F32),
            pltpu.VMEM((8, n_q), F32),
            pltpu.VMEM((tokens, head_dim), BF16),
            pltpu.VMEM((rows, span, head_dim), BF16),
        ],
        [ANY, ANY, ANY],
        [
            pltpu.VMEM(queries.shape, BF16),
            pltpu.VMEM((tokens, head_dim), BF16),
            pltpu.VMEM((n_q, head_dim), F32),
            pltpu.SemaphoreType.DMA((3,)),
            pltpu.SemaphoreType.DMA((4,)),
        ],
        [in_hbm(queries), prefix_kv, suffix_kv],
        8,
        2 * n_q * tokens * head_dim,
        6 * MIB,
    )
    far = list(range(n_z - 1, -1, -1))
    early = [(0, k) for k in far[: n_z // 2]]
    late = [(1, k) for k in far if k] + [(0, k) for k in far[n_z // 2 :] if k]
    tail, high, high_row, vals_t, out_pages, suf_vals, *early_w = kernel_call(
        functools.partial(suffix_scores_kernel, early),
        "suffix_scores",
        [
            pltpu.VMEM((n_q, span), F32),
            pltpu.VMEM((n_q, 128), F32),
            pltpu.VMEM((8, n_q), F32),
            pltpu.VMEM((head_dim, tokens), BF16),
            pltpu.VMEM((2, DISTINCT) + pages.shape[2:], BF16),
            pltpu.VMEM((rows, span, head_dim), BF16),
        ]
        + [pltpu.VMEM((in_rows, width), BF16)] * len(early),
        [SMEM, SMEM, VMEM, VMEM, VMEM, VMEM, ANY, ANY, ANY, ANY],
        [pltpu.SMEM((rows,), jnp.int32)]
        + list_scratch(pool_slot)
        + [
            pltpu.SemaphoreType.DMA((2,)),
            pltpu.SemaphoreType.DMA((2, DISTINCT)),
            pltpu.SemaphoreType.DMA((len(early),)),
        ],
        [other_ids, pool_slot, query, suf_keys, vals, peak, in_hbm(suffix_len), suffix_kv, pages, out_weight],
        8,
        1 << 29,
        7 * MIB,
    )
    other_pages = across(out_pages)
    attended, own_shrink, own_expand, row_slot, slot_mine, res, *late_w = kernel_call(
        functools.partial(values_kernel, late),
        "values",
        [
            pltpu.VMEM(queries.shape, BF16),
            pltpu.VMEM((DISTINCT,) + pages.shape[2:], BF16),
            pltpu.VMEM((DISTINCT,) + pages.shape[2:], BF16),
            pltpu.VMEM((rows, 128), jnp.int32),
            pltpu.VMEM((DISTINCT, 128), jnp.int32),
            pltpu.VMEM((rows, width), BF16),
        ]
        + [pltpu.VMEM((in_rows, width), BF16)] * len(late),
        [SMEM, SMEM, VMEM, VMEM, VMEM, VMEM, VMEM, VMEM, ANY, ANY, ANY],
        [
            pltpu.VMEM((n_q, head_dim), F32),
            pltpu.VMEM((n_q, 128), F32),
            pltpu.VMEM((n_q, head_dim), F32),
            pltpu.VMEM((8, n_q), F32),
            pltpu.VMEM((head_dim, n_q), F32),
        ]
        + list_scratch(pool_slot)
        + [
            pltpu.SemaphoreType.DMA((1,)),
            pltpu.SemaphoreType.DMA((2, DISTINCT)),
            pltpu.SemaphoreType.DMA((len(late),)),
        ],
        [ids, pool_slot, scores, tail, high, high_row, vals_t, suf_vals, pages, out_weight, residual],
        8,
        2 * n_q * tokens * head_dim,
        14 * MIB,
    )
    weights = dict(zip(early + late, list(early_w) + list(late_w)))
    return attended, own_shrink, own_expand, other_pages, row_slot, slot_mine, res, weights


def small_call(kernel, name, out_shape, operands, flops=1 << 27):
    return pl.pallas_call(
        kernel,
        out_shape=out_shape,
        in_specs=[VMEM] * len(operands),
        out_specs=jax.tree.map(lambda _: VMEM, out_shape),
        compiler_params=params(8),
        cost_estimate=pl.CostEstimate(flops=flops, bytes_accessed=2 * MIB, transcendentals=0),
        name=name,
    )(*operands)


def merged(own_ref, other, half, slot_mine):
    rank = own_ref.shape[1]
    tiles = []
    for j in range(DISTINCT):
        hit = jnp.broadcast_to(slot_mine[j : j + 1, :1], (rank, 1)) == 1
        tiles.append(jnp.where(hit, own_ref[j].astype(F32), other[half, j].astype(F32)).astype(BF16))
    return jnp.concatenate(tiles, axis=0)


def lane_place(shape, rank):
    return lax.broadcasted_iota(jnp.int32, shape, 1) // rank


def far_kernel(n, att_ref, row_slot_ref, slot_mine_ref, own_ref, other_ref, *rest):
    w_refs = rest[:n]
    out_ref, rank_ref = rest[n:]
    width = w_refs[0].shape[1]
    attended = att_ref[...]
    for k in range(n):
        out_ref[:, k * width : (k + 1) * width] = nn_dot(attended, w_refs[k][...]).astype(BF16)
    rank = own_ref.shape[1]
    per_tile = 128 // rank
    low = nt_dot(attended, merged(own_ref, other_ref, 0, slot_mine_ref[...]))
    row_slot = row_slot_ref[...]
    place = lane_place(row_slot.shape, rank)
    picked = jnp.zeros(row_slot.shape, F32)
    for tile in range(DISTINCT // per_tile):
        hit = row_slot == place + tile * per_tile
        picked = jnp.where(hit, low[:, tile * 128 : (tile + 1) * 128], picked)
    rank_ref[...] = picked
    out_ref[:, n * width :] = picked.astype(BF16)


def near_kernel(att_ref, w_ref, rank_ref, *rest):
    out_ref = rest[-1]
    width = w_ref.shape[1]
    out_ref[:, :width] = nn_dot(att_ref[...], w_ref[...]).astype(BF16)
    out_ref[:, width:] = rank_ref[...].astype(BF16)


def load_kernel(spots, weight_ref, after_ref, out_ref, sem):
    (copy,) = weight_copies(weight_ref, [out_ref], spots, sem)
    copy.start()
    copy.wait()


def load_block(weight, spot, after, n_tensor):
    return kernel_call(
        functools.partial(load_kernel, [spot]),
        "load_block",
        [pltpu.VMEM((weight.shape[0], weight.shape[1] // n_tensor), BF16)],
        [ANY, VMEM],
        [pltpu.SemaphoreType.DMA((1,))],
        [in_hbm(weight), after],
        2,
        0,
        2 * MIB,
    )[0]


def block_kernel(att_ref, w_ref, after_ref, out_ref):
    out_ref[...] = nn_dot(att_ref[...], w_ref[...]).astype(BF16)


def add_kernel(spot, att_ref, w_ref, from_ref, rank_ref, *rest):
    out_ref = rest[-1]
    width = w_ref.shape[1]
    both = nn_dot(att_ref[...], w_ref[...]) + from_ref[:, spot * width : (spot + 1) * width].astype(F32)
    out_ref[:, :width] = both.astype(BF16)
    rank_both = rank_ref[...] + from_ref[:, from_ref.shape[1] - 128 :].astype(F32)
    out_ref[:, width:] = rank_both.astype(BF16)


def finish_kernel(*refs):
    att_ref, w_ref, row_slot_ref, slot_mine_ref, own_ref, other_ref = refs[:6]
    rank_ref, far_ref, from_ref, res_ref = refs[6:10]
    moved, out_ref = refs[10:-1], refs[-1]
    rank = own_ref.shape[1]
    per_tile = 128 // rank
    width = w_ref.shape[1]
    low = rank_ref[...] + far_ref[:, far_ref.shape[1] - 128 :].astype(F32)
    for ref in moved:
        low = low + ref[:, width:].astype(F32)
    row_slot = row_slot_ref[...]
    place = lane_place(row_slot.shape, rank)
    tiles = []
    for tile in range(DISTINCT // per_tile):
        tiles.append(jnp.where(row_slot == place + tile * per_tile, low, 0.0).astype(BF16))
    total = nn_dot(jnp.concatenate(tiles, axis=1), merged(own_ref, other_ref, 1, slot_mine_ref[...]))
    total = total + nn_dot(att_ref[...], w_ref[...])
    total = total + (res_ref[...].astype(F32) + from_ref[...].astype(F32))
    for ref in moved:
        total = total + ref[:, :width].astype(F32)
    out_ref[...] = total.astype(BF16)


def place_kernel(spots, *refs):
    blocks, out_ref = refs[:-1], refs[-1]
    width = blocks[0].shape[1]
    me = lax.axis_index("tensor")
    z, y = me // 2, me % 2
    for block, (k, side) in zip(blocks, spots):
        where = (z ^ k) * 2 + (y ^ side)
        out_ref[:, pl.ds(pl.multiple_of(where * width, width), width)] = block[...]


def place(blocks, spots, n_tensor):
    rows, width = blocks[0].shape
    return pl.pallas_call(
        functools.partial(place_kernel, spots),
        out_shape=jax.ShapeDtypeStruct((rows, width * n_tensor), BF16),
        in_specs=[VMEM] * n_tensor,
        out_specs=VMEM,
        compiler_params=params(4),
        cost_estimate=pl.CostEstimate(flops=0, bytes_accessed=1 * MIB, transcendentals=0),
        name="place",
    )(*blocks)


def body(
    n_tensor,
    queries,
    prefix_kv,
    suffix_kv,
    suffix_len,
    residual,
    out_weight,
    adapter_pages,
    adapter_ids,
    pool_slot,
):
    n_z = n_tensor // 2

    def along_y(x):
        return lax.ppermute(x, "tensor", [(t, t ^ 1) for t in range(n_tensor)])

    def along_z(x, k):
        return lax.ppermute(x, "tensor", [(t, t ^ (2 * k)) for t in range(n_tensor)])

    def along_both(x, k):
        return lax.ppermute(x, "tensor", [(t, t ^ (2 * k) ^ 1) for t in range(n_tensor)])

    def across(x):
        return lax.ppermute(x, "req", [(0, 1), (1, 0)])

    rows = queries.shape[0]
    width = out_weight.shape[1] // n_tensor
    attended, own_shrink, own_expand, other_pages, row_slot, slot_mine, res, weights = attend(
        suffix_len,
        adapter_ids,
        across(adapter_ids),
        pool_slot,
        queries,
        prefix_kv,
        suffix_kv,
        out_weight,
        adapter_pages,
        residual,
        n_tensor,
        across,
    )
    far = list(range(n_z - 1, 1, -1))
    piece_shape = pltpu.VMEM((rows, width + 128), BF16)
    far_out, rank_own = small_call(
        functools.partial(far_kernel, len(far)),
        "far_blocks",
        [pltpu.VMEM((rows, len(far) * width + 128), BF16), pltpu.VMEM((rows, 128), F32)],
        [attended, row_slot, slot_mine, own_shrink, other_pages] + [weights[1, k] for k in far],
    )
    from_far = along_y(far_out)
    straight = small_call(near_kernel, "near_block", piece_shape, [attended, weights[0, 1], rank_own])
    weights[1, 0] = load_block(out_weight, (1, 0), straight, n_tensor)
    moved = [along_z(straight, 1)]
    after = []
    for spot, k in enumerate(far):
        piece = small_call(
            functools.partial(add_kernel, spot),
            "add_block",
            piece_shape,
            [attended, weights[0, k], from_far, rank_own] + after,
        )
        moved.append(along_z(piece, k))
        after = [piece]
    cross = small_call(near_kernel, "cross_block", piece_shape, [attended, weights[1, 1], rank_own, piece])
    moved.append(along_both(cross, 1))
    own_far = small_call(
        block_kernel, "own_far_block", pltpu.VMEM((rows, width), BF16), [attended, weights[1, 0], cross]
    )
    from_own = along_y(own_far)
    weights[0, 0] = load_block(out_weight, (0, 0), own_far, n_tensor)
    result = small_call(
        finish_kernel,
        "finish",
        pltpu.VMEM((rows, width), BF16),
        [attended, weights[0, 0], row_slot, slot_mine, own_expand, other_pages, rank_own, from_far, from_own, res]
        + moved,
    )
    held = [result] + [along_z(result, k) for k in range(1, n_z)]
    crossed = [along_both(result, k) if k < 2 else along_y(held[k]) for k in range(n_z)]
    spots = [(0, 0), (1, 1), (1, 0)] + [(k, side) for k in range(2, n_z) for side in (0, 1)]
    spots.insert(len(spots) - 2, (0, 1))
    return place([(crossed if side else held)[k] for k, side in spots], spots, n_tensor)


def solution(mesh):
    return jax.shard_map(
        functools.partial(body, mesh.shape["tensor"]),
        mesh=mesh,
        in_specs=(
            P(("group", "req"), "tensor"),
            P(("group", "tensor"), None, None, None),
            P(("group", "req"), "tensor", None, None, None),
            P(("group", "req")),
            P(("group", "req"), None),
            P("tensor", None),
            P("req", None, None, "tensor"),
            P(("group", "req")),
            P(),
        ),
        out_specs=P(("group", "req"), None),
        check_vma=False,
    )
```

```python
import functools

import jax
import jax.numpy as jnp
from jax import lax
from jax.experimental import pallas as pl
from jax.experimental.pallas import tpu as pltpu
from jax.sharding import PartitionSpec as P

F32 = jnp.float32
BF16 = jnp.bfloat16
LOG2E = 1.4426950408889634
ANY = pl.BlockSpec(memory_space=pl.ANY)
VMEM = pl.BlockSpec(memory_space=pltpu.VMEM)
SMEM = pl.BlockSpec(memory_space=pltpu.SMEM)
MIB = 1 << 20
DISTINCT = 8


def in_hbm(x):
    return pltpu.with_memory_space_constraint(x, pltpu.HBM)


def params(mib):
    return pltpu.CompilerParams(vmem_limit_bytes=mib * MIB)


def nt_dot(a, b):
    return lax.dot_general(a, b, (((1,), (1,)), ((), ())), preferred_element_type=F32)


def nn_dot(a, b):
    return jnp.dot(a, b, preferred_element_type=F32)


def distinct_list(ids_ref, pool_slot_ref, seen, list_id, list_pos):
    rows = ids_ref.shape[0]
    for i in range(pool_slot_ref.shape[0]):
        seen[i] = 0
    for j in range(DISTINCT + 1):
        list_id[j] = -1
        list_pos[j] = 0
    found = jnp.int32(0)
    for r in range(rows):
        one = ids_ref[r]
        fresh = 1 - seen[one]
        seen[one] = 1
        spot = jnp.minimum(found, DISTINCT)
        list_id[spot] = jnp.where(fresh == 1, one, list_id[spot])
        list_pos[spot] = jnp.where(fresh == 1, pool_slot_ref[one], list_pos[spot])
        found = found + fresh


def list_scratch(pool_slot):
    return [
        pltpu.SMEM((pool_slot.shape[0],), jnp.int32),
        pltpu.SMEM((DISTINCT + 1,), jnp.int32),
        pltpu.SMEM((DISTINCT + 1,), jnp.int32),
    ]


def page_copies(pages_ref, outs, list_pos, sem, wait):
    pool = pages_ref.shape[0]
    me = lax.axis_index("req")
    for j in range(DISTINCT):
        pos = list_pos[j]

        @pl.when(pos // pool == me)
        def _():
            for i, out in enumerate(outs):
                copy = pltpu.make_async_copy(pages_ref.at[pos % pool, i], out.at[j], sem.at[i, j])
                if wait:
                    copy.wait()
                else:
                    copy.start()


def prefix_scores_kernel(
    q_ref, prefix_ref, suffix_ref, query_ref, scores_ref, peak_ref, vals_ref, suf_keys_ref, qbuf, keys, rowbuf, sem, sem_keys
):
    rows = q_ref.shape[0]
    tokens, head_dim = keys.shape
    heads = q_ref.shape[1] // head_dim
    parts = sem_keys.shape[0]
    size = tokens // parts
    key_copies = [
        pltpu.make_async_copy(
            prefix_ref.at[0, 0, pl.ds(j * size, size)], keys.at[pl.ds(j * size, size)], sem_keys.at[j]
        )
        for j in range(parts)
    ]
    fetch_q = pltpu.make_async_copy(q_ref, qbuf, sem.at[0])
    fetch = [
        pltpu.make_async_copy(suffix_ref.at[:, 0, 0], suf_keys_ref, sem.at[1]),
        pltpu.make_async_copy(prefix_ref.at[0, 1], vals_ref, sem.at[2]),
    ]
    for c in [fetch_q] + key_copies + fetch:
        c.start()
    fetch_q.wait()
    for h in range(heads):
        rowbuf[pl.ds(h, rows, stride=heads), :] = qbuf[:, h * head_dim : (h + 1) * head_dim].astype(F32)
    query = rowbuf[...].astype(BF16)
    query_ref[...] = query
    best = jnp.full(peak_ref.shape, -3.0e38, F32)
    step = min(512, size)
    for j in range(parts):
        key_copies[j].wait()
        for base in range(j * size, (j + 1) * size, step):
            block = nt_dot(keys[base : base + step, :], query)
            scores_ref[base : base + step, :] = block
            best = jnp.maximum(best, jnp.max(block.reshape(step // 8, 8, block.shape[1]), axis=0))
    peak_ref[...] = best
    for c in fetch:
        c.wait()


def weight_copies(weight_ref, outs, spots, sem):
    me = lax.axis_index("tensor")
    z, y = me // 2, me % 2
    copies = []
    for i, (side, k) in enumerate(spots):
        width = outs[i].shape[1]
        column = pl.multiple_of(((z ^ k) * 2 + (y ^ side)) * width, width)
        copies.append(pltpu.make_async_copy(weight_ref.at[:, pl.ds(column, width)], outs[i], sem.at[i]))
    return copies


def suffix_scores_kernel(spots, ids_ref, slot_ref, query_ref, suf_keys_ref, vals_ref, peak_ref, *rest):
    len_ref, suffix_ref, pages_ref, weight_ref = rest[:4]
    tail_ref, high_ref, high_row_ref, vals_t_ref, out_pages_ref, suf_vals_ref = rest[4:10]
    w_refs = rest[10 : 10 + len(spots)]
    lens, seen, list_id, list_pos, sem, sem_page, sem_w = rest[10 + len(spots) :]
    rows, span, head_dim = suf_keys_ref.shape
    tokens = vals_ref.shape[0]
    heads = query_ref.shape[0] // rows
    fetch_len = pltpu.make_async_copy(len_ref, lens, sem.at[1])
    fetch_len.start()
    fetch = [pltpu.make_async_copy(suffix_ref.at[:, 0, 1], suf_vals_ref, sem.at[0])]
    fetch += weight_copies(weight_ref, w_refs, spots, sem_w)
    distinct_list(ids_ref, slot_ref, seen, list_id, list_pos)
    outs = (out_pages_ref.at[0], out_pages_ref.at[1])
    page_copies(pages_ref, outs, list_pos, sem_page, False)
    for c in fetch:
        c.start()
    query = query_ref[...]
    lanes = lax.broadcasted_iota(jnp.int32, (heads, span), 1)
    fetch_len.wait()
    for i in range(rows // 2):
        keys = suf_keys_ref[2 * i : 2 * i + 2].reshape(2 * span, head_dim)
        both = nt_dot(query[2 * heads * i : 2 * heads * (i + 1)], keys)
        for a in range(2):
            mine = both[a * heads : (a + 1) * heads, a * span : (a + 1) * span]
            row = 2 * i + a
            tail_ref[row * heads : (row + 1) * heads, :] = jnp.where(lanes < lens[row], mine, -1.0e30)
    step = min(1024, tokens)
    for base in range(0, tokens, step):
        vals_t_ref[:, base : base + step] = vals_ref[base : base + step, :].astype(F32).T.astype(BF16)
    best = jnp.maximum(tail_ref[:, :128], tail_ref[:, 128:256])
    for b in range(2, span // 128):
        best = jnp.maximum(best, tail_ref[:, b * 128 : (b + 1) * 128])
    across_rows = jnp.broadcast_to(jnp.max(peak_ref[...], axis=0, keepdims=True), (128, peak_ref.shape[1]))
    high = jnp.maximum(across_rows.T, jnp.max(best, axis=1, keepdims=True))
    high_ref[...] = high
    high_row_ref[...] = high.T[:8]
    page_copies(pages_ref, outs, list_pos, sem_page, True)
    for c in fetch:
        c.wait()


def values_kernel(spots, ids_ref, slot_ref, scores, tail, peak, peak_row, vals_t_ref, suf_vals_ref, *rest):
    pages_ref, weight_ref, residual_ref = rest[:3]
    att_ref, shrink_ref, expand_ref, row_slot_ref, slot_mine_ref, res_ref = rest[3:9]
    w_refs = rest[9 : 9 + len(spots)]
    rowbuf, total, acc, total_row, acc_t, seen, list_id, list_pos, sem, sem_page, sem_w = rest[9 + len(spots) :]
    rows, span, head_dim = suf_vals_ref.shape
    tokens = vals_t_ref.shape[1]
    heads = att_ref.shape[1] // head_dim
    width = res_ref.shape[1]
    me = lax.axis_index("tensor")
    scale2 = float(head_dim) ** -0.5 * LOG2E
    fetch = weight_copies(weight_ref, w_refs, spots, sem_w)
    fetch.append(
        pltpu.make_async_copy(
            residual_ref.at[:, pl.ds(pl.multiple_of(me * width, width), width)], res_ref, sem.at[0]
        )
    )
    for c in fetch:
        c.start()
    distinct_list(ids_ref, slot_ref, seen, list_id, list_pos)
    page_copies(pages_ref, (shrink_ref, expand_ref), list_pos, sem_page, False)
    row_index = lax.broadcasted_iota(jnp.int32, (rows, 128), 0)
    row_id = jnp.full((rows, 128), -2, jnp.int32)
    for r in range(rows):
        row_id = jnp.where(row_index == r, ids_ref[r], row_id)
    row_slot = jnp.full((rows, 128), -1, jnp.int32)
    slot_index = lax.broadcasted_iota(jnp.int32, (DISTINCT, 128), 0)
    slot_mine = jnp.zeros((DISTINCT, 128), jnp.int32)
    mine = lax.axis_index("req")
    for j in range(DISTINCT):
        row_slot = jnp.where(row_id == list_id[j], j, row_slot)
        owned = (list_pos[j] // pages_ref.shape[0] == mine).astype(jnp.int32)
        slot_mine = jnp.where(slot_index == j, owned, slot_mine)
    row_slot_ref[...] = row_slot
    slot_mine_ref[...] = slot_mine

    total_row[...] = jnp.zeros(total_row.shape, F32)
    acc_t[...] = jnp.zeros(acc_t.shape, F32)
    n_q = acc_t.shape[1]
    chunk = min(2048, tokens)

    @pl.loop(0, tokens // chunk)
    def _(i):
        base = pl.multiple_of(i * chunk, chunk)
        high_row = peak_row[...]
        block = scores[pl.ds(base, chunk), :].reshape(chunk // 8, 8, n_q)
        e = jnp.exp2((block - high_row[None]) * scale2)
        total_row[...] += jnp.sum(e, axis=0)
        weights = e.reshape(chunk, n_q).astype(BF16)
        acc_t[...] += nn_dot(vals_t_ref[:, pl.ds(base, chunk)], weights)

    across_rows = jnp.broadcast_to(jnp.sum(total_row[...], axis=0, keepdims=True), (128, n_q))
    acc[...] = acc_t[...].T
    zeros = jnp.zeros((heads, span), F32)
    for i in range(rows // 2):
        lo = 2 * heads * i
        high = jnp.concatenate([peak[lo : lo + 2 * heads, :]] * (span // 128), axis=1)
        e = jnp.exp2((tail[lo : lo + 2 * heads, :] - high) * scale2)
        part_sum = e[:, :128]
        for b in range(1, span // 128):
            part_sum = part_sum + e[:, b * 128 : (b + 1) * 128]
        total[lo : lo + 2 * heads, :] = part_sum
        diag = jnp.concatenate(
            [
                jnp.concatenate([e[:heads], zeros], axis=1),
                jnp.concatenate([zeros, e[heads:]], axis=1),
            ],
            axis=0,
        ).astype(BF16)
        vals = suf_vals_ref[2 * i : 2 * i + 2].reshape(2 * span, head_dim)
        acc[lo : lo + 2 * heads, :] += nn_dot(diag, vals)

    norm = across_rows.T + jnp.sum(total[...], axis=1, keepdims=True)
    rowbuf[...] = acc[...] / norm
    for h in range(heads):
        att_ref[:, h * head_dim : (h + 1) * head_dim] = rowbuf[pl.ds(h, rows, stride=heads), :].astype(BF16)
    page_copies(pages_ref, (shrink_ref, expand_ref), list_pos, sem_page, True)
    for c in fetch:
        c.wait()


def kernel_call(kernel, name, out_shape, specs, scratch, operands, mib, flops, bytes_accessed):
    return pl.pallas_call(
        kernel,
        out_shape=out_shape,
        in_specs=specs,
        out_specs=[VMEM] * len(out_shape),
        scratch_shapes=scratch,
        compiler_params=params(mib),
        cost_estimate=pl.CostEstimate(flops=flops, bytes_accessed=bytes_accessed, transcendentals=0),
        name=name,
    )(*operands)


def attend(
    suffix_len, ids, other_ids, pool_slot, queries, prefix_kv, suffix_kv, out_weight, pages, residual, n_tensor, across
):
    rows = queries.shape[0]
    n_z = n_tensor // 2
    in_rows = out_weight.shape[0]
    width = out_weight.shape[1] // n_tensor
    tokens, head_dim = prefix_kv.shape[2:]
    n_q = rows * queries.shape[1] // head_dim
    span = suffix_kv.shape[3]
    prefix_kv, suffix_kv, out_weight = in_hbm(prefix_kv), in_hbm(suffix_kv), in_hbm(out_weight)
    pages, residual = in_hbm(pages), in_hbm(residual)
    query, scores, peak, vals, suf_keys = kernel_call(
        prefix_scores_kernel,
        "prefix_scores",
        [
            pltpu.VMEM((n_q, head_dim), BF16),
            pltpu.VMEM((tokens, n_q), F32),
            pltpu.VMEM((8, n_q), F32),
            pltpu.VMEM((tokens, head_dim), BF16),
            pltpu.VMEM((rows, span, head_dim), BF16),
        ],
        [ANY, ANY, ANY],
        [
            pltpu.VMEM(queries.shape, BF16),
            pltpu.VMEM((tokens, head_dim), BF16),
            pltpu.VMEM((n_q, head_dim), F32),
            pltpu.SemaphoreType.DMA((3,)),
            pltpu.SemaphoreType.DMA((4,)),
        ],
        [in_hbm(queries), prefix_kv, suffix_kv],
        8,
        2 * n_q * tokens * head_dim,
        6 * MIB,
    )
    far = list(range(n_z - 1, -1, -1))
    early = [(0, k) for k in far[: n_z // 2]]
    late = [(1, k) for k in far] + [(0, k) for k in far[n_z // 2 :] if k]
    tail, high, high_row, vals_t, out_pages, suf_vals, *early_w = kernel_call(
        functools.partial(suffix_scores_kernel, early),
        "suffix_scores",
        [
            pltpu.VMEM((n_q, span), F32),
            pltpu.VMEM((n_q, 128), F32),
            pltpu.VMEM((8, n_q), F32),
            pltpu.VMEM((head_dim, tokens), BF16),
            pltpu.VMEM((2, DISTINCT) + pages.shape[2:], BF16),
            pltpu.VMEM((rows, span, head_dim), BF16),
        ]
        + [pltpu.VMEM((in_rows, width), BF16)] * len(early),
        [SMEM, SMEM, VMEM, VMEM, VMEM, VMEM, ANY, ANY, ANY, ANY],
        [pltpu.SMEM((rows,), jnp.int32)]
        + list_scratch(pool_slot)
        + [
            pltpu.SemaphoreType.DMA((2,)),
            pltpu.SemaphoreType.DMA((2, DISTINCT)),
            pltpu.SemaphoreType.DMA((len(early),)),
        ],
        [other_ids, pool_slot, query, suf_keys, vals, peak, in_hbm(suffix_len), suffix_kv, pages, out_weight],
        8,
        1 << 29,
        7 * MIB,
    )
    other_pages = across(out_pages)
    attended, own_shrink, own_expand, row_slot, slot_mine, res, *late_w = kernel_call(
        functools.partial(values_kernel, late),
        "values",
        [
            pltpu.VMEM(queries.shape, BF16),
            pltpu.VMEM((DISTINCT,) + pages.shape[2:], BF16),
            pltpu.VMEM((DISTINCT,) + pages.shape[2:], BF16),
            pltpu.VMEM((rows, 128), jnp.int32),
            pltpu.VMEM((DISTINCT, 128), jnp.int32),
            pltpu.VMEM((rows, width), BF16),
        ]
        + [pltpu.VMEM((in_rows, width), BF16)] * len(late),
        [SMEM, SMEM, VMEM, VMEM, VMEM, VMEM, VMEM, VMEM, ANY, ANY, ANY],
        [
            pltpu.VMEM((n_q, head_dim), F32),
            pltpu.VMEM((n_q, 128), F32),
            pltpu.VMEM((n_q, head_dim), F32),
            pltpu.VMEM((8, n_q), F32),
            pltpu.VMEM((head_dim, n_q), F32),
        ]
        + list_scratch(pool_slot)
        + [
            pltpu.SemaphoreType.DMA((1,)),
            pltpu.SemaphoreType.DMA((2, DISTINCT)),
            pltpu.SemaphoreType.DMA((len(late),)),
        ],
        [ids, pool_slot, scores, tail, high, high_row, vals_t, suf_vals, pages, out_weight, residual],
        8,
        2 * n_q * tokens * head_dim,
        14 * MIB,
    )
    weights = dict(zip(early + late, list(early_w) + list(late_w)))
    return attended, own_shrink, own_expand, other_pages, row_slot, slot_mine, res, weights


def small_call(kernel, name, out_shape, operands, flops=1 << 27):
    return pl.pallas_call(
        kernel,
        out_shape=out_shape,
        in_specs=[VMEM] * len(operands),
        out_specs=jax.tree.map(lambda _: VMEM, out_shape),
        compiler_params=params(8),
        cost_estimate=pl.CostEstimate(flops=flops, bytes_accessed=2 * MIB, transcendentals=0),
        name=name,
    )(*operands)


def merged(own_ref, other, half, slot_mine):
    rank = own_ref.shape[1]
    tiles = []
    for j in range(DISTINCT):
        hit = jnp.broadcast_to(slot_mine[j : j + 1, :1], (rank, 1)) == 1
        tiles.append(jnp.where(hit, own_ref[j].astype(F32), other[half, j].astype(F32)).astype(BF16))
    return jnp.concatenate(tiles, axis=0)


def lane_place(shape, rank):
    return lax.broadcasted_iota(jnp.int32, shape, 1) // rank


def far_kernel(n, att_ref, row_slot_ref, slot_mine_ref, own_ref, other_ref, *rest):
    w_refs = rest[:n]
    out_ref, rank_ref = rest[n:]
    width = w_refs[0].shape[1]
    attended = att_ref[...]
    for k in range(n):
        out_ref[:, k * width : (k + 1) * width] = nn_dot(attended, w_refs[k][...]).astype(BF16)
    rank = own_ref.shape[1]
    per_tile = 128 // rank
    low = nt_dot(attended, merged(own_ref, other_ref, 0, slot_mine_ref[...]))
    row_slot = row_slot_ref[...]
    place = lane_place(row_slot.shape, rank)
    picked = jnp.zeros(row_slot.shape, F32)
    for tile in range(DISTINCT // per_tile):
        hit = row_slot == place + tile * per_tile
        picked = jnp.where(hit, low[:, tile * 128 : (tile + 1) * 128], picked)
    rank_ref[...] = picked
    out_ref[:, n * width :] = picked.astype(BF16)


def near_kernel(att_ref, w_ref, rank_ref, *rest):
    out_ref = rest[-1]
    width = w_ref.shape[1]
    out_ref[:, :width] = nn_dot(att_ref[...], w_ref[...]).astype(BF16)
    out_ref[:, width:] = rank_ref[...].astype(BF16)


def pair_kernel(att_ref, w_ref, cross_w_ref, rank_ref, out_ref, cross_ref):
    near_kernel(att_ref, w_ref, rank_ref, out_ref)
    near_kernel(att_ref, cross_w_ref, rank_ref, cross_ref)


def load_kernel(spots, weight_ref, after_ref, out_ref, sem):
    (copy,) = weight_copies(weight_ref, [out_ref], spots, sem)
    copy.start()
    copy.wait()


def load_block(weight, spot, after, n_tensor):
    return kernel_call(
        functools.partial(load_kernel, [spot]),
        "load_block",
        [pltpu.VMEM((weight.shape[0], weight.shape[1] // n_tensor), BF16)],
        [ANY, VMEM],
        [pltpu.SemaphoreType.DMA((1,))],
        [in_hbm(weight), after],
        2,
        0,
        2 * MIB,
    )[0]


def block_kernel(att_ref, w_ref, after_ref, out_ref):
    out_ref[...] = nn_dot(att_ref[...], w_ref[...]).astype(BF16)


def add_kernel(spot, att_ref, w_ref, from_ref, rank_ref, *rest):
    out_ref = rest[-1]
    width = w_ref.shape[1]
    both = nn_dot(att_ref[...], w_ref[...]) + from_ref[:, spot * width : (spot + 1) * width].astype(F32)
    out_ref[:, :width] = both.astype(BF16)
    rank_both = rank_ref[...] + from_ref[:, from_ref.shape[1] - 128 :].astype(F32)
    out_ref[:, width:] = rank_both.astype(BF16)


def finish_kernel(*refs):
    att_ref, w_ref, row_slot_ref, slot_mine_ref, own_ref, other_ref = refs[:6]
    rank_ref, far_ref, from_ref, res_ref = refs[6:10]
    moved, out_ref = refs[10:-1], refs[-1]
    rank = own_ref.shape[1]
    per_tile = 128 // rank
    width = w_ref.shape[1]
    low = rank_ref[...] + far_ref[:, far_ref.shape[1] - 128 :].astype(F32)
    for ref in moved:
        low = low + ref[:, width:].astype(F32)
    row_slot = row_slot_ref[...]
    place = lane_place(row_slot.shape, rank)
    tiles = []
    for tile in range(DISTINCT // per_tile):
        tiles.append(jnp.where(row_slot == place + tile * per_tile, low, 0.0).astype(BF16))
    total = nn_dot(jnp.concatenate(tiles, axis=1), merged(own_ref, other_ref, 1, slot_mine_ref[...]))
    total = total + nn_dot(att_ref[...], w_ref[...])
    total = total + (res_ref[...].astype(F32) + from_ref[...].astype(F32))
    for ref in moved:
        total = total + ref[:, :width].astype(F32)
    out_ref[...] = total.astype(BF16)


def place_kernel(spots, *refs):
    blocks, out_ref = refs[:-1], refs[-1]
    width = blocks[0].shape[1]
    me = lax.axis_index("tensor")
    z, y = me // 2, me % 2
    for block, (k, side) in zip(blocks, spots):
        where = (z ^ k) * 2 + (y ^ side)
        out_ref[:, pl.ds(pl.multiple_of(where * width, width), width)] = block[...]


def place(blocks, spots, n_tensor):
    rows, width = blocks[0].shape
    return pl.pallas_call(
        functools.partial(place_kernel, spots),
        out_shape=jax.ShapeDtypeStruct((rows, width * n_tensor), BF16),
        in_specs=[VMEM] * n_tensor,
        out_specs=VMEM,
        compiler_params=params(4),
        cost_estimate=pl.CostEstimate(flops=0, bytes_accessed=1 * MIB, transcendentals=0),
        name="place",
    )(*blocks)


def body(
    n_tensor,
    queries,
    prefix_kv,
    suffix_kv,
    suffix_len,
    residual,
    out_weight,
    adapter_pages,
    adapter_ids,
    pool_slot,
):
    n_z = n_tensor // 2

    def along_y(x):
        return lax.ppermute(x, "tensor", [(t, t ^ 1) for t in range(n_tensor)])

    def along_z(x, k):
        return lax.ppermute(x, "tensor", [(t, t ^ (2 * k)) for t in range(n_tensor)])

    def along_both(x, k):
        return lax.ppermute(x, "tensor", [(t, t ^ (2 * k) ^ 1) for t in range(n_tensor)])

    def across(x):
        return lax.ppermute(x, "req", [(0, 1), (1, 0)])

    rows = queries.shape[0]
    width = out_weight.shape[1] // n_tensor
    attended, own_shrink, own_expand, other_pages, row_slot, slot_mine, res, weights = attend(
        suffix_len,
        adapter_ids,
        across(adapter_ids),
        pool_slot,
        queries,
        prefix_kv,
        suffix_kv,
        out_weight,
        adapter_pages,
        residual,
        n_tensor,
        across,
    )
    via_y = list(range(n_z - 2, 0, -2))
    direct = list(range(n_z - 1, 1, -2))
    piece_shape = pltpu.VMEM((rows, width + 128), BF16)
    far_out, rank_own = small_call(
        functools.partial(far_kernel, len(via_y)),
        "far_blocks",
        [pltpu.VMEM((rows, len(via_y) * width + 128), BF16), pltpu.VMEM((rows, 128), F32)],
        [attended, row_slot, slot_mine, own_shrink, other_pages] + [weights[1, k] for k in via_y],
    )
    from_far = along_y(far_out)
    moved = []
    for k in direct:
        straight, cross = small_call(
            pair_kernel,
            "pair_blocks",
            [piece_shape, piece_shape],
            [attended, weights[0, k], weights[1, k], rank_own],
        )
        moved += [along_z(straight, k), along_both(cross, k)]
    near = small_call(near_kernel, "near_block", piece_shape, [attended, weights[0, 1], rank_own, cross])
    moved.append(along_z(near, 1))
    after = [near]
    for spot, k in enumerate(via_y):
        piece = small_call(
            functools.partial(add_kernel, spot),
            "add_block",
            piece_shape,
            [attended, weights[0, k], from_far, rank_own] + after,
        )
        moved.append(along_z(piece, k))
        after = [piece]
    cross = small_call(near_kernel, "cross_block", piece_shape, [attended, weights[1, 1], rank_own, piece])
    moved.append(along_both(cross, 1))
    own_far = small_call(
        block_kernel, "own_far_block", pltpu.VMEM((rows, width), BF16), [attended, weights[1, 0], cross]
    )
    from_own = along_y(own_far)
    weights[0, 0] = load_block(out_weight, (0, 0), own_far, n_tensor)
    result = small_call(
        finish_kernel,
        "finish",
        pltpu.VMEM((rows, width), BF16),
        [attended, weights[0, 0], row_slot, slot_mine, own_expand, other_pages, rank_own, from_far, from_own, res]
        + moved,
    )
    held = [result] + [along_z(result, k) for k in range(1, n_z)]
    crossed = [along_both(result, k) if k < 2 else along_y(held[k]) for k in range(n_z)]
    spots = [(0, 0), (1, 1), (1, 0)] + [(k, side) for k in range(2, n_z) for side in (0, 1)]
    spots.insert(len(spots) - 2, (0, 1))
    return place([(crossed if side else held)[k] for k, side in spots], spots, n_tensor)


def solution(mesh):
    return jax.shard_map(
        functools.partial(body, mesh.shape["tensor"]),
        mesh=mesh,
        in_specs=(
            P(("group", "req"), "tensor"),
            P(("group", "tensor"), None, None, None),
            P(("group", "req"), "tensor", None, None, None),
            P(("group", "req")),
            P(("group", "req"), None),
            P("tensor", None),
            P("req", None, None, "tensor"),
            P(("group", "req")),
            P(),
        ),
        out_specs=P(("group", "req"), None),
        check_vma=False,
    )
```

```python
import functools

import jax
import jax.numpy as jnp
from jax import lax
from jax.experimental import pallas as pl
from jax.experimental.pallas import tpu as pltpu
from jax.sharding import PartitionSpec as P

F32 = jnp.float32
BF16 = jnp.bfloat16
LOG2E = 1.4426950408889634
ANY = pl.BlockSpec(memory_space=pl.ANY)
VMEM = pl.BlockSpec(memory_space=pltpu.VMEM)
SMEM = pl.BlockSpec(memory_space=pltpu.SMEM)
MIB = 1 << 20
DISTINCT = 8


def in_hbm(x):
    return pltpu.with_memory_space_constraint(x, pltpu.HBM)


def params(mib):
    return pltpu.CompilerParams(vmem_limit_bytes=mib * MIB)


def nt_dot(a, b):
    return lax.dot_general(a, b, (((1,), (1,)), ((), ())), preferred_element_type=F32)


def nn_dot(a, b):
    return jnp.dot(a, b, preferred_element_type=F32)


def distinct_list(ids_ref, pool_slot_ref, seen, list_id, list_pos):
    rows = ids_ref.shape[0]
    for i in range(pool_slot_ref.shape[0]):
        seen[i] = 0
    for j in range(DISTINCT + 1):
        list_id[j] = -1
        list_pos[j] = 0
    found = jnp.int32(0)
    for r in range(rows):
        one = ids_ref[r]
        fresh = 1 - seen[one]
        seen[one] = 1
        spot = jnp.minimum(found, DISTINCT)
        list_id[spot] = jnp.where(fresh == 1, one, list_id[spot])
        list_pos[spot] = jnp.where(fresh == 1, pool_slot_ref[one], list_pos[spot])
        found = found + fresh


def list_scratch(pool_slot):
    return [
        pltpu.SMEM((pool_slot.shape[0],), jnp.int32),
        pltpu.SMEM((DISTINCT + 1,), jnp.int32),
        pltpu.SMEM((DISTINCT + 1,), jnp.int32),
    ]


def page_copies(pages_ref, outs, list_pos, sem, wait):
    pool = pages_ref.shape[0]
    me = lax.axis_index("req")
    for j in range(DISTINCT):
        pos = list_pos[j]

        @pl.when(pos // pool == me)
        def _():
            for i, out in enumerate(outs):
                copy = pltpu.make_async_copy(pages_ref.at[pos % pool, i], out.at[j], sem.at[i, j])
                if wait:
                    copy.wait()
                else:
                    copy.start()


def prefix_scores_kernel(
    q_ref, prefix_ref, suffix_ref, query_ref, scores_ref, peak_ref, vals_ref, suf_keys_ref, qbuf, keys, rowbuf, sem, sem_keys
):
    rows = q_ref.shape[0]
    tokens, head_dim = keys.shape
    heads = q_ref.shape[1] // head_dim
    parts = sem_keys.shape[0]
    size = tokens // parts
    key_copies = [
        pltpu.make_async_copy(
            prefix_ref.at[0, 0, pl.ds(j * size, size)], keys.at[pl.ds(j * size, size)], sem_keys.at[j]
        )
        for j in range(parts)
    ]
    fetch_q = pltpu.make_async_copy(q_ref, qbuf, sem.at[0])
    fetch = [
        pltpu.make_async_copy(suffix_ref.at[:, 0, 0], suf_keys_ref, sem.at[1]),
        pltpu.make_async_copy(prefix_ref.at[0, 1], vals_ref, sem.at[2]),
    ]
    for c in [fetch_q] + key_copies + fetch:
        c.start()
    fetch_q.wait()
    for h in range(heads):
        rowbuf[pl.ds(h, rows, stride=heads), :] = qbuf[:, h * head_dim : (h + 1) * head_dim].astype(F32)
    query = rowbuf[...].astype(BF16)
    query_ref[...] = query
    best = jnp.full(peak_ref.shape, -3.0e38, F32)
    step = min(512, size)
    for j in range(parts):
        key_copies[j].wait()
        for base in range(j * size, (j + 1) * size, step):
            block = nt_dot(keys[base : base + step, :], query)
            scores_ref[base : base + step, :] = block
            best = jnp.maximum(best, jnp.max(block.reshape(step // 8, 8, block.shape[1]), axis=0))
    peak_ref[...] = best
    for c in fetch:
        c.wait()


def weight_copies(weight_ref, outs, spots, sem):
    me = lax.axis_index("tensor")
    z, y = me // 2, me % 2
    copies = []
    for i, (side, k) in enumerate(spots):
        width = outs[i].shape[1]
        column = pl.multiple_of(((z ^ k) * 2 + (y ^ side)) * width, width)
        copies.append(pltpu.make_async_copy(weight_ref.at[:, pl.ds(column, width)], outs[i], sem.at[i]))
    return copies


def suffix_scores_kernel(spots, ids_ref, slot_ref, query_ref, suf_keys_ref, vals_ref, peak_ref, *rest):
    len_ref, suffix_ref, pages_ref, weight_ref = rest[:4]
    tail_ref, high_ref, high_row_ref, vals_t_ref, out_pages_ref, suf_vals_ref = rest[4:10]
    w_refs = rest[10 : 10 + len(spots)]
    lens, seen, list_id, list_pos, sem, sem_page, sem_w = rest[10 + len(spots) :]
    rows, span, head_dim = suf_keys_ref.shape
    tokens = vals_ref.shape[0]
    heads = query_ref.shape[0] // rows
    fetch_len = pltpu.make_async_copy(len_ref, lens, sem.at[1])
    fetch_len.start()
    fetch = [pltpu.make_async_copy(suffix_ref.at[:, 0, 1], suf_vals_ref, sem.at[0])]
    fetch += weight_copies(weight_ref, w_refs, spots, sem_w)
    distinct_list(ids_ref, slot_ref, seen, list_id, list_pos)
    outs = (out_pages_ref.at[0], out_pages_ref.at[1])
    page_copies(pages_ref, outs, list_pos, sem_page, False)
    for c in fetch:
        c.start()
    query = query_ref[...]
    lanes = lax.broadcasted_iota(jnp.int32, (heads, span), 1)
    fetch_len.wait()
    for i in range(rows // 2):
        keys = suf_keys_ref[2 * i : 2 * i + 2].reshape(2 * span, head_dim)
        both = nt_dot(query[2 * heads * i : 2 * heads * (i + 1)], keys)
        for a in range(2):
            mine = both[a * heads : (a + 1) * heads, a * span : (a + 1) * span]
            row = 2 * i + a
            tail_ref[row * heads : (row + 1) * heads, :] = jnp.where(lanes < lens[row], mine, -1.0e30)
    step = min(1024, tokens)
    for base in range(0, tokens, step):
        vals_t_ref[:, base : base + step] = vals_ref[base : base + step, :].astype(F32).T.astype(BF16)
    best = jnp.maximum(tail_ref[:, :128], tail_ref[:, 128:256])
    for b in range(2, span // 128):
        best = jnp.maximum(best, tail_ref[:, b * 128 : (b + 1) * 128])
    across_rows = jnp.broadcast_to(jnp.max(peak_ref[...], axis=0, keepdims=True), (128, peak_ref.shape[1]))
    high = jnp.maximum(across_rows.T, jnp.max(best, axis=1, keepdims=True))
    high_ref[...] = high
    high_row_ref[...] = high.T[:8]
    page_copies(pages_ref, outs, list_pos, sem_page, True)
    for c in fetch:
        c.wait()


def values_kernel(spots, ids_ref, slot_ref, scores, tail, peak, peak_row, vals_t_ref, suf_vals_ref, *rest):
    pages_ref, weight_ref, residual_ref = rest[:3]
    att_ref, shrink_ref, expand_ref, row_slot_ref, slot_mine_ref, res_ref = rest[3:9]
    w_refs = rest[9 : 9 + len(spots)]
    rowbuf, total, acc, total_row, acc_t, seen, list_id, list_pos, sem, sem_page, sem_w = rest[9 + len(spots) :]
    rows, span, head_dim = suf_vals_ref.shape
    tokens = vals_t_ref.shape[1]
    heads = att_ref.shape[1] // head_dim
    width = res_ref.shape[1]
    me = lax.axis_index("tensor")
    scale2 = float(head_dim) ** -0.5 * LOG2E
    fetch = weight_copies(weight_ref, w_refs, spots, sem_w)
    fetch.append(
        pltpu.make_async_copy(
            residual_ref.at[:, pl.ds(pl.multiple_of(me * width, width), width)], res_ref, sem.at[0]
        )
    )
    for c in fetch:
        c.start()
    distinct_list(ids_ref, slot_ref, seen, list_id, list_pos)
    page_copies(pages_ref, (shrink_ref, expand_ref), list_pos, sem_page, False)
    row_index = lax.broadcasted_iota(jnp.int32, (rows, 128), 0)
    row_id = jnp.full((rows, 128), -2, jnp.int32)
    for r in range(rows):
        row_id = jnp.where(row_index == r, ids_ref[r], row_id)
    row_slot = jnp.full((rows, 128), -1, jnp.int32)
    slot_index = lax.broadcasted_iota(jnp.int32, (DISTINCT, 128), 0)
    slot_mine = jnp.zeros((DISTINCT, 128), jnp.int32)
    mine = lax.axis_index("req")
    for j in range(DISTINCT):
        row_slot = jnp.where(row_id == list_id[j], j, row_slot)
        owned = (list_pos[j] // pages_ref.shape[0] == mine).astype(jnp.int32)
        slot_mine = jnp.where(slot_index == j, owned, slot_mine)
    row_slot_ref[...] = row_slot
    slot_mine_ref[...] = slot_mine

    total_row[...] = jnp.zeros(total_row.shape, F32)
    acc_t[...] = jnp.zeros(acc_t.shape, F32)
    n_q = acc_t.shape[1]
    chunk = min(2048, tokens)

    @pl.loop(0, tokens // chunk)
    def _(i):
        base = pl.multiple_of(i * chunk, chunk)
        high_row = peak_row[...]
        block = scores[pl.ds(base, chunk), :].reshape(chunk // 8, 8, n_q)
        e = jnp.exp2((block - high_row[None]) * scale2)
        total_row[...] += jnp.sum(e, axis=0)
        weights = e.reshape(chunk, n_q).astype(BF16)
        acc_t[...] += nn_dot(vals_t_ref[:, pl.ds(base, chunk)], weights)

    across_rows = jnp.broadcast_to(jnp.sum(total_row[...], axis=0, keepdims=True), (128, n_q))
    acc[...] = acc_t[...].T
    zeros = jnp.zeros((heads, span), F32)
    for i in range(rows // 2):
        lo = 2 * heads * i
        high = jnp.concatenate([peak[lo : lo + 2 * heads, :]] * (span // 128), axis=1)
        e = jnp.exp2((tail[lo : lo + 2 * heads, :] - high) * scale2)
        part_sum = e[:, :128]
        for b in range(1, span // 128):
            part_sum = part_sum + e[:, b * 128 : (b + 1) * 128]
        total[lo : lo + 2 * heads, :] = part_sum
        diag = jnp.concatenate(
            [
                jnp.concatenate([e[:heads], zeros], axis=1),
                jnp.concatenate([zeros, e[heads:]], axis=1),
            ],
            axis=0,
        ).astype(BF16)
        vals = suf_vals_ref[2 * i : 2 * i + 2].reshape(2 * span, head_dim)
        acc[lo : lo + 2 * heads, :] += nn_dot(diag, vals)

    norm = across_rows.T + jnp.sum(total[...], axis=1, keepdims=True)
    rowbuf[...] = acc[...] / norm
    for h in range(heads):
        att_ref[:, h * head_dim : (h + 1) * head_dim] = rowbuf[pl.ds(h, rows, stride=heads), :].astype(BF16)
    page_copies(pages_ref, (shrink_ref, expand_ref), list_pos, sem_page, True)
    for c in fetch:
        c.wait()


def kernel_call(kernel, name, out_shape, specs, scratch, operands, mib, flops, bytes_accessed):
    return pl.pallas_call(
        kernel,
        out_shape=out_shape,
        in_specs=specs,
        out_specs=[VMEM] * len(out_shape),
        scratch_shapes=scratch,
        compiler_params=params(mib),
        cost_estimate=pl.CostEstimate(flops=flops, bytes_accessed=bytes_accessed, transcendentals=0),
        name=name,
    )(*operands)


def attend(
    suffix_len, ids, other_ids, pool_slot, queries, prefix_kv, suffix_kv, out_weight, pages, residual, n_tensor, across
):
    rows = queries.shape[0]
    n_z = n_tensor // 2
    in_rows = out_weight.shape[0]
    width = out_weight.shape[1] // n_tensor
    tokens, head_dim = prefix_kv.shape[2:]
    n_q = rows * queries.shape[1] // head_dim
    span = suffix_kv.shape[3]
    prefix_kv, suffix_kv, out_weight = in_hbm(prefix_kv), in_hbm(suffix_kv), in_hbm(out_weight)
    pages, residual = in_hbm(pages), in_hbm(residual)
    query, scores, peak, vals, suf_keys = kernel_call(
        prefix_scores_kernel,
        "prefix_scores",
        [
            pltpu.VMEM((n_q, head_dim), BF16),
            pltpu.VMEM((tokens, n_q), F32),
            pltpu.VMEM((8, n_q), F32),
            pltpu.VMEM((tokens, head_dim), BF16),
            pltpu.VMEM((rows, span, head_dim), BF16),
        ],
        [ANY, ANY, ANY],
        [
            pltpu.VMEM(queries.shape, BF16),
            pltpu.VMEM((tokens, head_dim), BF16),
            pltpu.VMEM((n_q, head_dim), F32),
            pltpu.SemaphoreType.DMA((3,)),
            pltpu.SemaphoreType.DMA((4,)),
        ],
        [in_hbm(queries), prefix_kv, suffix_kv],
        8,
        2 * n_q * tokens * head_dim,
        6 * MIB,
    )
    far = list(range(n_z - 1, -1, -1))
    early = [(0, k) for k in far[: n_z // 4]]
    late = [(1, k) for k in far if k > 1] + [(0, k) for k in far[n_z // 4 :] if k > 1]
    tail, high, high_row, vals_t, out_pages, suf_vals, *early_w = kernel_call(
        functools.partial(suffix_scores_kernel, early),
        "suffix_scores",
        [
            pltpu.VMEM((n_q, span), F32),
            pltpu.VMEM((n_q, 128), F32),
            pltpu.VMEM((8, n_q), F32),
            pltpu.VMEM((head_dim, tokens), BF16),
            pltpu.VMEM((2, DISTINCT) + pages.shape[2:], BF16),
            pltpu.VMEM((rows, span, head_dim), BF16),
        ]
        + [pltpu.VMEM((in_rows, width), BF16)] * len(early),
        [SMEM, SMEM, VMEM, VMEM, VMEM, VMEM, ANY, ANY, ANY, ANY],
        [pltpu.SMEM((rows,), jnp.int32)]
        + list_scratch(pool_slot)
        + [
            pltpu.SemaphoreType.DMA((2,)),
            pltpu.SemaphoreType.DMA((2, DISTINCT)),
            pltpu.SemaphoreType.DMA((len(early),)),
        ],
        [other_ids, pool_slot, query, suf_keys, vals, peak, in_hbm(suffix_len), suffix_kv, pages, out_weight],
        8,
        1 << 29,
        7 * MIB,
    )
    other_pages = across(out_pages)
    attended, own_shrink, own_expand, row_slot, slot_mine, res, *late_w = kernel_call(
        functools.partial(values_kernel, late),
        "values",
        [
            pltpu.VMEM(queries.shape, BF16),
            pltpu.VMEM((DISTINCT,) + pages.shape[2:], BF16),
            pltpu.VMEM((DISTINCT,) + pages.shape[2:], BF16),
            pltpu.VMEM((rows, 128), jnp.int32),
            pltpu.VMEM((DISTINCT, 128), jnp.int32),
            pltpu.VMEM((rows, width), BF16),
        ]
        + [pltpu.VMEM((in_rows, width), BF16)] * len(late),
        [SMEM, SMEM, VMEM, VMEM, VMEM, VMEM, VMEM, VMEM, ANY, ANY, ANY],
        [
            pltpu.VMEM((n_q, head_dim), F32),
            pltpu.VMEM((n_q, 128), F32),
            pltpu.VMEM((n_q, head_dim), F32),
            pltpu.VMEM((8, n_q), F32),
            pltpu.VMEM((head_dim, n_q), F32),
        ]
        + list_scratch(pool_slot)
        + [
            pltpu.SemaphoreType.DMA((1,)),
            pltpu.SemaphoreType.DMA((2, DISTINCT)),
            pltpu.SemaphoreType.DMA((len(late),)),
        ],
        [ids, pool_slot, scores, tail, high, high_row, vals_t, suf_vals, pages, out_weight, residual],
        8,
        2 * n_q * tokens * head_dim,
        14 * MIB,
    )
    weights = dict(zip(early + late, list(early_w) + list(late_w)))
    return attended, own_shrink, own_expand, other_pages, row_slot, slot_mine, res, weights


def small_call(kernel, name, out_shape, operands, flops=1 << 27):
    return pl.pallas_call(
        kernel,
        out_shape=out_shape,
        in_specs=[VMEM] * len(operands),
        out_specs=jax.tree.map(lambda _: VMEM, out_shape),
        compiler_params=params(8),
        cost_estimate=pl.CostEstimate(flops=flops, bytes_accessed=2 * MIB, transcendentals=0),
        name=name,
    )(*operands)


def merged(own_ref, other, half, slot_mine):
    rank = own_ref.shape[1]
    tiles = []
    for j in range(DISTINCT):
        hit = jnp.broadcast_to(slot_mine[j : j + 1, :1], (rank, 1)) == 1
        tiles.append(jnp.where(hit, own_ref[j].astype(F32), other[half, j].astype(F32)).astype(BF16))
    return jnp.concatenate(tiles, axis=0)


def lane_place(shape, rank):
    return lax.broadcasted_iota(jnp.int32, shape, 1) // rank


def far_kernel(n, att_ref, row_slot_ref, slot_mine_ref, own_ref, other_ref, *rest):
    w_refs = rest[:n]
    out_ref, rank_ref = rest[n:]
    width = w_refs[0].shape[1]
    attended = att_ref[...]
    for k in range(n):
        out_ref[:, k * width : (k + 1) * width] = nn_dot(attended, w_refs[k][...]).astype(BF16)
    rank = own_ref.shape[1]
    per_tile = 128 // rank
    low = nt_dot(attended, merged(own_ref, other_ref, 0, slot_mine_ref[...]))
    row_slot = row_slot_ref[...]
    place = lane_place(row_slot.shape, rank)
    picked = jnp.zeros(row_slot.shape, F32)
    for tile in range(DISTINCT // per_tile):
        hit = row_slot == place + tile * per_tile
        picked = jnp.where(hit, low[:, tile * 128 : (tile + 1) * 128], picked)
    rank_ref[...] = picked
    out_ref[:, n * width :] = picked.astype(BF16)


def near_kernel(spots, att_ref, rank_ref, weight_ref, *rest):
    outs, (wbuf, sem) = rest[: len(spots)], rest[len(spots) :]
    width = wbuf.shape[2]
    copies = weight_copies(weight_ref, [wbuf.at[i] for i in range(len(spots))], spots, sem)
    for c in copies:
        c.start()
    attended = att_ref[...]
    rank = rank_ref[...].astype(BF16)
    for i, out in enumerate(outs):
        copies[i].wait()
        out[:, :width] = nn_dot(attended, wbuf[i]).astype(BF16)
        if out.shape[1] > width:
            out[:, width:] = rank


def near_blocks(spots, columns, attended, rank_own, weight, after, n_tensor):
    rows = attended.shape[0]
    width = weight.shape[1] // n_tensor

    def kernel(att_ref, rank_ref, weight_ref, *rest):
        near_kernel(spots, att_ref, rank_ref, weight_ref, *rest[len(after) :])

    return kernel_call(
        kernel,
        "near_blocks",
        [pltpu.VMEM((rows, columns), BF16)] * len(spots),
        [VMEM, VMEM, ANY] + [VMEM] * len(after),
        [pltpu.VMEM((len(spots), weight.shape[0], width), BF16), pltpu.SemaphoreType.DMA((len(spots),))],
        [attended, rank_own, in_hbm(weight)] + after,
        8,
        1 << 27,
        2 * len(spots) * MIB,
    )


def load_kernel(spots, weight_ref, after_ref, out_ref, sem):
    (copy,) = weight_copies(weight_ref, [out_ref], spots, sem)
    copy.start()
    copy.wait()


def load_block(weight, spot, after, n_tensor):
    return kernel_call(
        functools.partial(load_kernel, [spot]),
        "load_block",
        [pltpu.VMEM((weight.shape[0], weight.shape[1] // n_tensor), BF16)],
        [ANY, VMEM],
        [pltpu.SemaphoreType.DMA((1,))],
        [in_hbm(weight), after],
        2,
        0,
        2 * MIB,
    )[0]


def add_kernel(spot, att_ref, w_ref, from_ref, rank_ref, *rest):
    out_ref = rest[-1]
    width = w_ref.shape[1]
    both = nn_dot(att_ref[...], w_ref[...]) + from_ref[:, spot * width : (spot + 1) * width].astype(F32)
    out_ref[:, :width] = both.astype(BF16)
    rank_both = rank_ref[...] + from_ref[:, from_ref.shape[1] - 128 :].astype(F32)
    out_ref[:, width:] = rank_both.astype(BF16)


def finish_kernel(*refs):
    att_ref, w_ref, row_slot_ref, slot_mine_ref, own_ref, other_ref = refs[:6]
    rank_ref, far_ref, from_ref, res_ref = refs[6:10]
    moved, out_ref = refs[10:-1], refs[-1]
    rank = own_ref.shape[1]
    per_tile = 128 // rank
    width = w_ref.shape[1]
    low = rank_ref[...] + far_ref[:, far_ref.shape[1] - 128 :].astype(F32)
    for ref in moved:
        low = low + ref[:, width:].astype(F32)
    row_slot = row_slot_ref[...]
    place = lane_place(row_slot.shape, rank)
    tiles = []
    for tile in range(DISTINCT // per_tile):
        tiles.append(jnp.where(row_slot == place + tile * per_tile, low, 0.0).astype(BF16))
    total = nn_dot(jnp.concatenate(tiles, axis=1), merged(own_ref, other_ref, 1, slot_mine_ref[...]))
    total = total + nn_dot(att_ref[...], w_ref[...])
    total = total + (res_ref[...].astype(F32) + from_ref[...].astype(F32))
    for ref in moved:
        total = total + ref[:, :width].astype(F32)
    out_ref[...] = total.astype(BF16)


def place_kernel(spots, *refs):
    blocks, out_ref = refs[:-1], refs[-1]
    width = blocks[0].shape[1]
    me = lax.axis_index("tensor")
    z, y = me // 2, me % 2
    for block, (k, side) in zip(blocks, spots):
        where = (z ^ k) * 2 + (y ^ side)
        out_ref[:, pl.ds(pl.multiple_of(where * width, width), width)] = block[...]


def place(blocks, spots, n_tensor):
    rows, width = blocks[0].shape
    return pl.pallas_call(
        functools.partial(place_kernel, spots),
        out_shape=jax.ShapeDtypeStruct((rows, width * n_tensor), BF16),
        in_specs=[VMEM] * n_tensor,
        out_specs=VMEM,
        compiler_params=params(4),
        cost_estimate=pl.CostEstimate(flops=0, bytes_accessed=1 * MIB, transcendentals=0),
        name="place",
    )(*blocks)


def body(
    n_tensor,
    queries,
    prefix_kv,
    suffix_kv,
    suffix_len,
    residual,
    out_weight,
    adapter_pages,
    adapter_ids,
    pool_slot,
):
    n_z = n_tensor // 2

    def along_y(x):
        return lax.ppermute(x, "tensor", [(t, t ^ 1) for t in range(n_tensor)])

    def along_z(x, k):
        return lax.ppermute(x, "tensor", [(t, t ^ (2 * k)) for t in range(n_tensor)])

    def along_both(x, k):
        return lax.ppermute(x, "tensor", [(t, t ^ (2 * k) ^ 1) for t in range(n_tensor)])

    def across(x):
        return lax.ppermute(x, "req", [(0, 1), (1, 0)])

    rows = queries.shape[0]
    width = out_weight.shape[1] // n_tensor
    attended, own_shrink, own_expand, other_pages, row_slot, slot_mine, res, weights = attend(
        suffix_len,
        adapter_ids,
        across(adapter_ids),
        pool_slot,
        queries,
        prefix_kv,
        suffix_kv,
        out_weight,
        adapter_pages,
        residual,
        n_tensor,
        across,
    )
    far = list(range(n_z - 1, 1, -1))
    piece_shape = pltpu.VMEM((rows, width + 128), BF16)
    far_out, rank_own = small_call(
        functools.partial(far_kernel, len(far)),
        "far_blocks",
        [pltpu.VMEM((rows, len(far) * width + 128), BF16), pltpu.VMEM((rows, 128), F32)],
        [attended, row_slot, slot_mine, own_shrink, other_pages] + [weights[1, k] for k in far],
    )
    from_far = along_y(far_out)
    straight, cross = near_blocks(
        [(0, 1), (1, 1)], width + 128, attended, rank_own, out_weight, [], n_tensor
    )
    moved = [along_z(straight, 1), along_both(cross, 1)]
    after = []
    for spot, k in enumerate(far):
        piece = small_call(
            functools.partial(add_kernel, spot),
            "add_block",
            piece_shape,
            [attended, weights[0, k], from_far, rank_own] + after,
        )
        moved.append(along_z(piece, k))
        after = [piece]
    (own_far,) = near_blocks([(1, 0)], width, attended, rank_own, out_weight, [piece], n_tensor)
    from_own = along_y(own_far)
    weights[0, 0] = load_block(out_weight, (0, 0), own_far, n_tensor)
    result = small_call(
        finish_kernel,
        "finish",
        pltpu.VMEM((rows, width), BF16),
        [attended, weights[0, 0], row_slot, slot_mine, own_expand, other_pages, rank_own, from_far, from_own, res]
        + moved,
    )
    held = [result] + [along_z(result, k) for k in range(1, n_z)]
    crossed = [along_both(result, k) if k < 2 else along_y(held[k]) for k in range(n_z)]
    spots = [(0, 0), (1, 1), (1, 0)] + [(k, side) for k in range(2, n_z) for side in (0, 1)]
    spots.insert(len(spots) - 2, (0, 1))
    return place([(crossed if side else held)[k] for k, side in spots], spots, n_tensor)


def solution(mesh):
    return jax.shard_map(
        functools.partial(body, mesh.shape["tensor"]),
        mesh=mesh,
        in_specs=(
            P(("group", "req"), "tensor"),
            P(("group", "tensor"), None, None, None),
            P(("group", "req"), "tensor", None, None, None),
            P(("group", "req")),
            P(("group", "req"), None),
            P("tensor", None),
            P("req", None, None, "tensor"),
            P(("group", "req")),
            P(),
        ),
        out_specs=P(("group", "req"), None),
        check_vma=False,
    )
```

```python
import functools

import jax
import jax.numpy as jnp
from jax import lax
from jax.experimental import pallas as pl
from jax.experimental.pallas import tpu as pltpu
from jax.sharding import PartitionSpec as P

F32 = jnp.float32
BF16 = jnp.bfloat16
LOG2E = 1.4426950408889634
ANY = pl.BlockSpec(memory_space=pl.ANY)
VMEM = pl.BlockSpec(memory_space=pltpu.VMEM)
SMEM = pl.BlockSpec(memory_space=pltpu.SMEM)
MIB = 1 << 20
DISTINCT = 8


def in_hbm(x):
    return pltpu.with_memory_space_constraint(x, pltpu.HBM)


def params(mib):
    return pltpu.CompilerParams(vmem_limit_bytes=mib * MIB)


def nt_dot(a, b):
    return lax.dot_general(a, b, (((1,), (1,)), ((), ())), preferred_element_type=F32)


def nn_dot(a, b):
    return jnp.dot(a, b, preferred_element_type=F32)


def distinct_list(ids_ref, pool_slot_ref, seen, list_id, list_pos):
    rows = ids_ref.shape[0]
    for i in range(pool_slot_ref.shape[0]):
        seen[i] = 0
    for j in range(DISTINCT + 1):
        list_id[j] = -1
        list_pos[j] = 0
    found = jnp.int32(0)
    for r in range(rows):
        one = ids_ref[r]
        fresh = 1 - seen[one]
        seen[one] = 1
        spot = jnp.minimum(found, DISTINCT)
        list_id[spot] = jnp.where(fresh == 1, one, list_id[spot])
        list_pos[spot] = jnp.where(fresh == 1, pool_slot_ref[one], list_pos[spot])
        found = found + fresh


def list_scratch(pool_slot):
    return [
        pltpu.SMEM((pool_slot.shape[0],), jnp.int32),
        pltpu.SMEM((DISTINCT + 1,), jnp.int32),
        pltpu.SMEM((DISTINCT + 1,), jnp.int32),
    ]


def page_copies(pages_ref, outs, list_pos, sem, wait):
    pool = pages_ref.shape[0]
    me = lax.axis_index("req")
    for j in range(DISTINCT):
        pos = list_pos[j]

        @pl.when(pos // pool == me)
        def _():
            for i, out in enumerate(outs):
                copy = pltpu.make_async_copy(pages_ref.at[pos % pool, i], out.at[j], sem.at[i, j])
                if wait:
                    copy.wait()
                else:
                    copy.start()


def prefix_scores_kernel(
    q_ref, prefix_ref, suffix_ref, query_ref, scores_ref, peak_ref, suf_keys_ref, qbuf, keys, rowbuf, sem, sem_keys
):
    rows = q_ref.shape[0]
    tokens, head_dim = keys.shape
    heads = q_ref.shape[1] // head_dim
    parts = sem_keys.shape[0]
    size = tokens // parts
    key_copies = [
        pltpu.make_async_copy(
            prefix_ref.at[0, 0, pl.ds(j * size, size)], keys.at[pl.ds(j * size, size)], sem_keys.at[j]
        )
        for j in range(parts)
    ]
    fetch_q = pltpu.make_async_copy(q_ref, qbuf, sem.at[0])
    fetch = [pltpu.make_async_copy(suffix_ref.at[:, 0, 0], suf_keys_ref, sem.at[1])]
    for c in [fetch_q] + key_copies + fetch:
        c.start()
    fetch_q.wait()
    for h in range(heads):
        rowbuf[pl.ds(h, rows, stride=heads), :] = qbuf[:, h * head_dim : (h + 1) * head_dim].astype(F32)
    query = rowbuf[...].astype(BF16)
    query_ref[...] = query
    best = jnp.full(peak_ref.shape, -3.0e38, F32)
    step = min(512, size)
    for j in range(parts):
        key_copies[j].wait()
        for base in range(j * size, (j + 1) * size, step):
            block = nt_dot(keys[base : base + step, :], query)
            scores_ref[base : base + step, :] = block
            best = jnp.maximum(best, jnp.max(block.reshape(step // 8, 8, block.shape[1]), axis=0))
    peak_ref[...] = best
    for c in fetch:
        c.wait()


def weight_copies(weight_ref, outs, spots, sem):
    me = lax.axis_index("tensor")
    z, y = me // 2, me % 2
    copies = []
    for i, (side, k) in enumerate(spots):
        width = outs[i].shape[1]
        column = pl.multiple_of(((z ^ k) * 2 + (y ^ side)) * width, width)
        copies.append(pltpu.make_async_copy(weight_ref.at[:, pl.ds(column, width)], outs[i], sem.at[i]))
    return copies


def suffix_scores_kernel(spots, ids_ref, slot_ref, query_ref, suf_keys_ref, peak_ref, *rest):
    len_ref, prefix_ref, pages_ref, weight_ref = rest[:4]
    tail_ref, high_ref, high_row_ref, vals_t_ref, out_pages_ref = rest[4:9]
    w_refs = rest[9 : 9 + len(spots)]
    lens, vals_ref, seen, list_id, list_pos, sem, sem_page, sem_w = rest[9 + len(spots) :]
    rows, span, head_dim = suf_keys_ref.shape
    tokens = vals_ref.shape[0]
    parts = sem.shape[0] - 1
    size = tokens // parts
    heads = query_ref.shape[0] // rows
    fetch_len = pltpu.make_async_copy(len_ref, lens, sem.at[parts])
    fetch_len.start()
    val_copies = [
        pltpu.make_async_copy(
            prefix_ref.at[0, 1, pl.ds(j * size, size)], vals_ref.at[pl.ds(j * size, size)], sem.at[j]
        )
        for j in range(parts)
    ]
    for c in val_copies:
        c.start()
    fetch = weight_copies(weight_ref, w_refs, spots, sem_w)
    distinct_list(ids_ref, slot_ref, seen, list_id, list_pos)
    outs = (out_pages_ref.at[0], out_pages_ref.at[1])
    page_copies(pages_ref, outs, list_pos, sem_page, False)
    for c in fetch:
        c.start()
    query = query_ref[...]
    lanes = lax.broadcasted_iota(jnp.int32, (heads, span), 1)
    fetch_len.wait()
    for i in range(rows // 2):
        keys = suf_keys_ref[2 * i : 2 * i + 2].reshape(2 * span, head_dim)
        both = nt_dot(query[2 * heads * i : 2 * heads * (i + 1)], keys)
        for a in range(2):
            mine = both[a * heads : (a + 1) * heads, a * span : (a + 1) * span]
            row = 2 * i + a
            tail_ref[row * heads : (row + 1) * heads, :] = jnp.where(lanes < lens[row], mine, -1.0e30)
    vals_t_ref[head_dim:, :] = jnp.ones((vals_t_ref.shape[0] - head_dim, tokens), BF16)
    step = min(1024, size)
    for j in range(parts):
        val_copies[j].wait()
        for base in range(j * size, (j + 1) * size, step):
            vals_t_ref[:head_dim, base : base + step] = vals_ref[base : base + step, :].astype(F32).T.astype(BF16)
    best = jnp.maximum(tail_ref[:, :128], tail_ref[:, 128:256])
    for b in range(2, span // 128):
        best = jnp.maximum(best, tail_ref[:, b * 128 : (b + 1) * 128])
    across_rows = jnp.broadcast_to(jnp.max(peak_ref[...], axis=0, keepdims=True), (128, peak_ref.shape[1]))
    high = jnp.maximum(across_rows.T, jnp.max(best, axis=1, keepdims=True))
    high_ref[...] = high
    high_row_ref[...] = high.T[:8]
    page_copies(pages_ref, outs, list_pos, sem_page, True)
    for c in fetch:
        c.wait()


def values_kernel(spots, ids_ref, slot_ref, scores, tail, peak, peak_row, vals_t_ref, suffix_ref, *rest):
    pages_ref, weight_ref, residual_ref = rest[:3]
    att_ref, shrink_ref, expand_ref, row_slot_ref, slot_mine_ref, res_ref = rest[3:9]
    w_refs = rest[9 : 9 + len(spots)]
    suf_vals_ref, rowbuf, total, acc, acc_t, seen, list_id, list_pos, sem, sem_page, sem_w = rest[9 + len(spots) :]
    rows, span, head_dim = suf_vals_ref.shape
    fetch_vals = pltpu.make_async_copy(suffix_ref.at[:, 0, 1], suf_vals_ref, sem.at[1])
    fetch_vals.start()
    tokens = vals_t_ref.shape[1]
    heads = att_ref.shape[1] // head_dim
    width = res_ref.shape[1]
    me = lax.axis_index("tensor")
    scale2 = float(head_dim) ** -0.5 * LOG2E
    fetch = weight_copies(weight_ref, w_refs, spots, sem_w)
    fetch.append(
        pltpu.make_async_copy(
            residual_ref.at[:, pl.ds(pl.multiple_of(me * width, width), width)], res_ref, sem.at[0]
        )
    )
    for c in fetch:
        c.start()
    distinct_list(ids_ref, slot_ref, seen, list_id, list_pos)
    page_copies(pages_ref, (shrink_ref, expand_ref), list_pos, sem_page, False)
    row_index = lax.broadcasted_iota(jnp.int32, (rows, 128), 0)
    row_id = jnp.full((rows, 128), -2, jnp.int32)
    for r in range(rows):
        row_id = jnp.where(row_index == r, ids_ref[r], row_id)
    row_slot = jnp.full((rows, 128), -1, jnp.int32)
    slot_index = lax.broadcasted_iota(jnp.int32, (DISTINCT, 128), 0)
    slot_mine = jnp.zeros((DISTINCT, 128), jnp.int32)
    mine = lax.axis_index("req")
    for j in range(DISTINCT):
        row_slot = jnp.where(row_id == list_id[j], j, row_slot)
        owned = (list_pos[j] // pages_ref.shape[0] == mine).astype(jnp.int32)
        slot_mine = jnp.where(slot_index == j, owned, slot_mine)
    row_slot_ref[...] = row_slot
    slot_mine_ref[...] = slot_mine

    acc_t[...] = jnp.zeros(acc_t.shape, F32)
    n_q = acc_t.shape[1]
    chunk = min(2048, tokens)

    @pl.loop(0, tokens // chunk)
    def _(i):
        base = pl.multiple_of(i * chunk, chunk)
        high_row = peak_row[...]
        block = scores[pl.ds(base, chunk), :].reshape(chunk // 8, 8, n_q)
        e = jnp.exp2((block - high_row[None]) * scale2)
        weights = e.reshape(chunk, n_q).astype(BF16)
        acc_t[...] += nn_dot(vals_t_ref[:, pl.ds(base, chunk)], weights)

    across_rows = jnp.broadcast_to(acc_t[head_dim : head_dim + 1, :], (128, n_q))
    acc[...] = acc_t[:head_dim, :].T
    fetch_vals.wait()
    zeros = jnp.zeros((heads, span), F32)
    for i in range(rows // 2):
        lo = 2 * heads * i
        high = jnp.concatenate([peak[lo : lo + 2 * heads, :]] * (span // 128), axis=1)
        e = jnp.exp2((tail[lo : lo + 2 * heads, :] - high) * scale2)
        part_sum = e[:, :128]
        for b in range(1, span // 128):
            part_sum = part_sum + e[:, b * 128 : (b + 1) * 128]
        total[lo : lo + 2 * heads, :] = part_sum
        diag = jnp.concatenate(
            [
                jnp.concatenate([e[:heads], zeros], axis=1),
                jnp.concatenate([zeros, e[heads:]], axis=1),
            ],
            axis=0,
        ).astype(BF16)
        vals = suf_vals_ref[2 * i : 2 * i + 2].reshape(2 * span, head_dim)
        acc[lo : lo + 2 * heads, :] += nn_dot(diag, vals)

    norm = across_rows.T + jnp.sum(total[...], axis=1, keepdims=True)
    rowbuf[...] = acc[...] / norm
    for h in range(heads):
        att_ref[:, h * head_dim : (h + 1) * head_dim] = rowbuf[pl.ds(h, rows, stride=heads), :].astype(BF16)
    page_copies(pages_ref, (shrink_ref, expand_ref), list_pos, sem_page, True)
    for c in fetch:
        c.wait()


def kernel_call(kernel, name, out_shape, specs, scratch, operands, mib, flops, bytes_accessed):
    return pl.pallas_call(
        kernel,
        out_shape=out_shape,
        in_specs=specs,
        out_specs=[VMEM] * len(out_shape),
        scratch_shapes=scratch,
        compiler_params=params(mib),
        cost_estimate=pl.CostEstimate(flops=flops, bytes_accessed=bytes_accessed, transcendentals=0),
        name=name,
    )(*operands)


def attend(
    suffix_len, ids, other_ids, pool_slot, queries, prefix_kv, suffix_kv, out_weight, pages, residual, n_tensor, across
):
    rows = queries.shape[0]
    n_z = n_tensor // 2
    in_rows = out_weight.shape[0]
    width = out_weight.shape[1] // n_tensor
    tokens, head_dim = prefix_kv.shape[2:]
    n_q = rows * queries.shape[1] // head_dim
    span = suffix_kv.shape[3]
    prefix_kv, suffix_kv, out_weight = in_hbm(prefix_kv), in_hbm(suffix_kv), in_hbm(out_weight)
    pages, residual = in_hbm(pages), in_hbm(residual)
    query, scores, peak, suf_keys = kernel_call(
        prefix_scores_kernel,
        "prefix_scores",
        [
            pltpu.VMEM((n_q, head_dim), BF16),
            pltpu.VMEM((tokens, n_q), F32),
            pltpu.VMEM((8, n_q), F32),
            pltpu.VMEM((rows, span, head_dim), BF16),
        ],
        [ANY, ANY, ANY],
        [
            pltpu.VMEM(queries.shape, BF16),
            pltpu.VMEM((tokens, head_dim), BF16),
            pltpu.VMEM((n_q, head_dim), F32),
            pltpu.SemaphoreType.DMA((2,)),
            pltpu.SemaphoreType.DMA((4,)),
        ],
        [in_hbm(queries), prefix_kv, suffix_kv],
        8,
        2 * n_q * tokens * head_dim,
        6 * MIB,
    )
    far = list(range(n_z - 1, -1, -1))
    early = [(0, k) for k in far[: n_z // 4]]
    late = [(1, k) for k in far if k > 1] + [(0, k) for k in far[n_z // 4 :] if k > 1]
    tail, high, high_row, vals_t, out_pages, *early_w = kernel_call(
        functools.partial(suffix_scores_kernel, early),
        "suffix_scores",
        [
            pltpu.VMEM((n_q, span), F32),
            pltpu.VMEM((n_q, 128), F32),
            pltpu.VMEM((8, n_q), F32),
            pltpu.VMEM((head_dim + 16, tokens), BF16),
            pltpu.VMEM((2, DISTINCT) + pages.shape[2:], BF16),
        ]
        + [pltpu.VMEM((in_rows, width), BF16)] * len(early),
        [SMEM, SMEM, VMEM, VMEM, VMEM, ANY, ANY, ANY, ANY],
        [pltpu.SMEM((rows,), jnp.int32), pltpu.VMEM((tokens, head_dim), BF16)]
        + list_scratch(pool_slot)
        + [
            pltpu.SemaphoreType.DMA((5,)),
            pltpu.SemaphoreType.DMA((2, DISTINCT)),
            pltpu.SemaphoreType.DMA((len(early),)),
        ],
        [other_ids, pool_slot, query, suf_keys, peak, in_hbm(suffix_len), prefix_kv, pages, out_weight],
        8,
        1 << 29,
        7 * MIB,
    )
    other_pages = across(out_pages)
    attended, own_shrink, own_expand, row_slot, slot_mine, res, *late_w = kernel_call(
        functools.partial(values_kernel, late),
        "values",
        [
            pltpu.VMEM(queries.shape, BF16),
            pltpu.VMEM((DISTINCT,) + pages.shape[2:], BF16),
            pltpu.VMEM((DISTINCT,) + pages.shape[2:], BF16),
            pltpu.VMEM((rows, 128), jnp.int32),
            pltpu.VMEM((DISTINCT, 128), jnp.int32),
            pltpu.VMEM((rows, width), BF16),
        ]
        + [pltpu.VMEM((in_rows, width), BF16)] * len(late),
        [SMEM, SMEM, VMEM, VMEM, VMEM, VMEM, VMEM, ANY, ANY, ANY, ANY],
        [
            pltpu.VMEM((rows, span, head_dim), BF16),
            pltpu.VMEM((n_q, head_dim), F32),
            pltpu.VMEM((n_q, 128), F32),
            pltpu.VMEM((n_q, head_dim), F32),
            pltpu.VMEM((head_dim + 16, n_q), F32),
        ]
        + list_scratch(pool_slot)
        + [
            pltpu.SemaphoreType.DMA((2,)),
            pltpu.SemaphoreType.DMA((2, DISTINCT)),
            pltpu.SemaphoreType.DMA((len(late),)),
        ],
        [ids, pool_slot, scores, tail, high, high_row, vals_t, suffix_kv, pages, out_weight, residual],
        8,
        2 * n_q * tokens * head_dim,
        14 * MIB,
    )
    weights = dict(zip(early + late, list(early_w) + list(late_w)))
    return attended, own_shrink, own_expand, other_pages, row_slot, slot_mine, res, weights


def small_call(kernel, name, out_shape, operands, flops=1 << 27):
    return pl.pallas_call(
        kernel,
        out_shape=out_shape,
        in_specs=[VMEM] * len(operands),
        out_specs=jax.tree.map(lambda _: VMEM, out_shape),
        compiler_params=params(8),
        cost_estimate=pl.CostEstimate(flops=flops, bytes_accessed=2 * MIB, transcendentals=0),
        name=name,
    )(*operands)


def merged(own_ref, other, half, slot_mine):
    rank = own_ref.shape[1]
    tiles = []
    for j in range(DISTINCT):
        hit = jnp.broadcast_to(slot_mine[j : j + 1, :1], (rank, 1)) == 1
        tiles.append(jnp.where(hit, own_ref[j].astype(F32), other[half, j].astype(F32)).astype(BF16))
    return jnp.concatenate(tiles, axis=0)


def lane_place(shape, rank):
    return lax.broadcasted_iota(jnp.int32, shape, 1) // rank


def far_kernel(n, att_ref, row_slot_ref, slot_mine_ref, own_ref, other_ref, *rest):
    w_refs = rest[:n]
    out_ref, rank_ref = rest[n:]
    width = w_refs[0].shape[1]
    attended = att_ref[...]
    for k in range(n):
        out_ref[:, k * width : (k + 1) * width] = nn_dot(attended, w_refs[k][...]).astype(BF16)
    rank = own_ref.shape[1]
    per_tile = 128 // rank
    low = nt_dot(attended, merged(own_ref, other_ref, 0, slot_mine_ref[...]))
    row_slot = row_slot_ref[...]
    place = lane_place(row_slot.shape, rank)
    picked = jnp.zeros(row_slot.shape, F32)
    for tile in range(DISTINCT // per_tile):
        hit = row_slot == place + tile * per_tile
        picked = jnp.where(hit, low[:, tile * 128 : (tile + 1) * 128], picked)
    rank_ref[...] = picked
    out_ref[:, n * width :] = picked.astype(BF16)


def near_kernel(spots, att_ref, rank_ref, weight_ref, *rest):
    outs, (wbuf, sem) = rest[: len(spots)], rest[len(spots) :]
    width = wbuf.shape[2]
    copies = weight_copies(weight_ref, [wbuf.at[i] for i in range(len(spots))], spots, sem)
    for c in copies:
        c.start()
    attended = att_ref[...]
    rank = rank_ref[...].astype(BF16)
    for i, out in enumerate(outs):
        copies[i].wait()
        out[:, :width] = nn_dot(attended, wbuf[i]).astype(BF16)
        if out.shape[1] > width:
            out[:, width:] = rank


def near_blocks(spots, columns, attended, rank_own, weight, after, n_tensor):
    rows = attended.shape[0]
    width = weight.shape[1] // n_tensor

    def kernel(att_ref, rank_ref, weight_ref, *rest):
        near_kernel(spots, att_ref, rank_ref, weight_ref, *rest[len(after) :])

    return kernel_call(
        kernel,
        "near_blocks",
        [pltpu.VMEM((rows, columns), BF16)] * len(spots),
        [VMEM, VMEM, ANY] + [VMEM] * len(after),
        [pltpu.VMEM((len(spots), weight.shape[0], width), BF16), pltpu.SemaphoreType.DMA((len(spots),))],
        [attended, rank_own, in_hbm(weight)] + after,
        8,
        1 << 27,
        2 * len(spots) * MIB,
    )


def own_kernel(
    att_ref, res_ref, slot_mine_ref, own_ref, other_ref, weight_ref, after_ref, out_ref, pages_ref, wbuf, sem
):
    (copy,) = weight_copies(weight_ref, [wbuf], [(0, 0)], sem)
    copy.start()
    pages_ref[...] = merged(own_ref, other_ref, 1, slot_mine_ref[...])
    copy.wait()
    out_ref[...] = nn_dot(att_ref[...], wbuf[...]) + res_ref[...].astype(F32)


def own_block(attended, res, slot_mine, own_pages, other_pages, weight, after):
    rows, width = res.shape
    return kernel_call(
        own_kernel,
        "own_block",
        [pltpu.VMEM((rows, width), F32), pltpu.VMEM((DISTINCT * own_pages.shape[1], width), BF16)],
        [VMEM, VMEM, VMEM, VMEM, VMEM, ANY, VMEM],
        [pltpu.VMEM((weight.shape[0], width), BF16), pltpu.SemaphoreType.DMA((1,))],
        [attended, res, slot_mine, own_pages, other_pages, in_hbm(weight), after],
        8,
        0,
        2 * MIB,
    )


def add_kernel(spot, att_ref, w_ref, from_ref, rank_ref, *rest):
    out_ref = rest[-1]
    width = w_ref.shape[1]
    both = nn_dot(att_ref[...], w_ref[...]) + from_ref[:, spot * width : (spot + 1) * width].astype(F32)
    out_ref[:, :width] = both.astype(BF16)
    rank_both = rank_ref[...] + from_ref[:, from_ref.shape[1] - 128 :].astype(F32)
    out_ref[:, width:] = rank_both.astype(BF16)


def finish_kernel(*refs):
    own_ref, pages_ref, row_slot_ref, rank_ref, far_ref, from_ref = refs[:6]
    moved, out_ref = refs[6:-1], refs[-1]
    rank = pages_ref.shape[0] // DISTINCT
    per_tile = 128 // rank
    width = own_ref.shape[1]
    low = rank_ref[...] + far_ref[:, far_ref.shape[1] - 128 :].astype(F32)
    for ref in moved:
        low = low + ref[:, width:].astype(F32)
    row_slot = row_slot_ref[...]
    place = lane_place(row_slot.shape, rank)
    tiles = []
    for tile in range(DISTINCT // per_tile):
        tiles.append(jnp.where(row_slot == place + tile * per_tile, low, 0.0).astype(BF16))
    total = nn_dot(jnp.concatenate(tiles, axis=1), pages_ref[...])
    total = total + (own_ref[...] + from_ref[...].astype(F32))
    for ref in moved:
        total = total + ref[:, :width].astype(F32)
    out_ref[...] = total.astype(BF16)


def place_kernel(spots, *refs):
    blocks = refs[: len(spots)]
    out_ref, sem = refs[-2:]
    width = blocks[0].shape[1]
    me = lax.axis_index("tensor")
    z, y = me // 2, me % 2
    copies = []
    for i, (k, side) in enumerate(spots):
        column = pl.multiple_of(((z ^ k) * 2 + (y ^ side)) * width, width)
        copies.append(pltpu.make_async_copy(blocks[i], out_ref.at[:, pl.ds(column, width)], sem.at[i]))
    for c in copies:
        c.start()
    for c in copies:
        c.wait()


def place(blocks, spots, n_tensor, held=None):
    rows, width = blocks[0].shape
    extra = [] if held is None else [held]
    return pl.pallas_call(
        functools.partial(place_kernel, spots),
        out_shape=pltpu.HBM((rows, width * n_tensor), BF16),
        in_specs=[VMEM] * len(blocks) + [ANY] * len(extra),
        out_specs=ANY,
        scratch_shapes=[pltpu.SemaphoreType.DMA((len(blocks),))],
        input_output_aliases={len(blocks): 0} if extra else {},
        compiler_params=params(4),
        cost_estimate=pl.CostEstimate(flops=0, bytes_accessed=1 * MIB, transcendentals=0),
        name="place",
    )(*blocks, *extra)


def body(
    n_tensor,
    queries,
    prefix_kv,
    suffix_kv,
    suffix_len,
    residual,
    out_weight,
    adapter_pages,
    adapter_ids,
    pool_slot,
):
    n_z = n_tensor // 2

    def along_y(x):
        return lax.ppermute(x, "tensor", [(t, t ^ 1) for t in range(n_tensor)])

    def along_z(x, k):
        return lax.ppermute(x, "tensor", [(t, t ^ (2 * k)) for t in range(n_tensor)])

    def along_both(x, k):
        return lax.ppermute(x, "tensor", [(t, t ^ (2 * k) ^ 1) for t in range(n_tensor)])

    def across(x):
        return lax.ppermute(x, "req", [(0, 1), (1, 0)])

    rows = queries.shape[0]
    width = out_weight.shape[1] // n_tensor
    attended, own_shrink, own_expand, other_pages, row_slot, slot_mine, res, weights = attend(
        suffix_len,
        adapter_ids,
        across(adapter_ids),
        pool_slot,
        queries,
        prefix_kv,
        suffix_kv,
        out_weight,
        adapter_pages,
        residual,
        n_tensor,
        across,
    )
    far = list(range(n_z - 1, 1, -1))
    piece_shape = pltpu.VMEM((rows, width + 128), BF16)
    far_out, rank_own = small_call(
        functools.partial(far_kernel, len(far)),
        "far_blocks",
        [pltpu.VMEM((rows, len(far) * width + 128), BF16), pltpu.VMEM((rows, 128), F32)],
        [attended, row_slot, slot_mine, own_shrink, other_pages] + [weights[1, k] for k in far],
    )
    from_far = along_y(far_out)
    straight, cross = near_blocks(
        [(0, 1), (1, 1)], width + 128, attended, rank_own, out_weight, [], n_tensor
    )
    moved = [along_z(straight, 1), along_both(cross, 1)]
    after = []
    for spot, k in enumerate(far):
        piece = small_call(
            functools.partial(add_kernel, spot),
            "add_block",
            piece_shape,
            [attended, weights[0, k], from_far, rank_own] + after,
        )
        moved.append(along_z(piece, k))
        after = [piece]
    (own_far,) = near_blocks([(1, 0)], width, attended, rank_own, out_weight, [piece], n_tensor)
    from_own = along_y(own_far)
    own, expand_pages = own_block(attended, res, slot_mine, own_expand, other_pages, out_weight, own_far)
    result = small_call(
        finish_kernel,
        "finish",
        pltpu.VMEM((rows, width), BF16),
        [own, expand_pages, row_slot, rank_own, from_far, from_own] + moved,
    )
    held = [result] + [along_z(result, k) for k in range(1, n_z)]
    crossed = [along_both(result, k) if k < 2 else along_y(held[k]) for k in range(n_z)]
    spots = [(0, 0), (1, 1), (1, 0)] + [(k, side) for k in range(2, n_z) for side in (0, 1)]
    spots.insert(len(spots) - 2, (0, 1))
    forwarded = [(k, side) for k, side in spots if k > 1 and side]
    placed = None
    for group in ([p for p in spots if p not in forwarded], forwarded):
        placed = place([(crossed if side else held)[k] for k, side in group], group, n_tensor, placed)
    return placed


def solution(mesh):
    return jax.shard_map(
        functools.partial(body, mesh.shape["tensor"]),
        mesh=mesh,
        in_specs=(
            P(("group", "req"), "tensor"),
            P(("group", "tensor"), None, None, None),
            P(("group", "req"), "tensor", None, None, None),
            P(("group", "req")),
            P(("group", "req"), None),
            P("tensor", None),
            P("req", None, None, "tensor"),
            P(("group", "req")),
            P(),
        ),
        out_specs=P(("group", "req"), None),
        check_vma=False,
    )
```

```python
import functools

import jax
import jax.numpy as jnp
from jax import lax
from jax.experimental import pallas as pl
from jax.experimental.pallas import tpu as pltpu
from jax.sharding import PartitionSpec as P

F32 = jnp.float32
BF16 = jnp.bfloat16
LOG2E = 1.4426950408889634
ANY = pl.BlockSpec(memory_space=pl.ANY)
VMEM = pl.BlockSpec(memory_space=pltpu.VMEM)
SMEM = pl.BlockSpec(memory_space=pltpu.SMEM)
MIB = 1 << 20
DISTINCT = 8


def in_hbm(x):
    return pltpu.with_memory_space_constraint(x, pltpu.HBM)


def params(mib):
    return pltpu.CompilerParams(vmem_limit_bytes=mib * MIB)


def nt_dot(a, b):
    return lax.dot_general(a, b, (((1,), (1,)), ((), ())), preferred_element_type=F32)


def nn_dot(a, b):
    return jnp.dot(a, b, preferred_element_type=F32)


def distinct_list(ids_ref, pool_slot_ref, seen, list_id, list_pos):
    rows = ids_ref.shape[0]
    for i in range(pool_slot_ref.shape[0]):
        seen[i] = 0
    for j in range(DISTINCT + 1):
        list_id[j] = -1
        list_pos[j] = 0
    found = jnp.int32(0)
    for r in range(rows):
        one = ids_ref[r]
        fresh = 1 - seen[one]
        seen[one] = 1
        spot = jnp.minimum(found, DISTINCT)
        list_id[spot] = jnp.where(fresh == 1, one, list_id[spot])
        list_pos[spot] = jnp.where(fresh == 1, pool_slot_ref[one], list_pos[spot])
        found = found + fresh


def list_scratch(pool_slot):
    return [
        pltpu.SMEM((pool_slot.shape[0],), jnp.int32),
        pltpu.SMEM((DISTINCT + 1,), jnp.int32),
        pltpu.SMEM((DISTINCT + 1,), jnp.int32),
    ]


def page_copies(pages_ref, outs, list_pos, sem, wait):
    pool = pages_ref.shape[0]
    me = lax.axis_index("req")
    for j in range(DISTINCT):
        pos = list_pos[j]

        @pl.when(pos // pool == me)
        def _():
            for i, out in enumerate(outs):
                copy = pltpu.make_async_copy(pages_ref.at[pos % pool, i], out.at[j], sem.at[i, j])
                if wait:
                    copy.wait()
                else:
                    copy.start()


def prefix_scores_kernel(
    q_ref, prefix_ref, suffix_ref, query_ref, scores_ref, peak_ref, vals_ref, suf_keys_ref, qbuf, keys, rowbuf, sem, sem_keys
):
    rows = q_ref.shape[0]
    tokens, head_dim = keys.shape
    heads = q_ref.shape[1] // head_dim
    parts = sem_keys.shape[0]
    size = tokens // parts
    key_copies = [
        pltpu.make_async_copy(
            prefix_ref.at[0, 0, pl.ds(j * size, size)], keys.at[pl.ds(j * size, size)], sem_keys.at[j]
        )
        for j in range(parts)
    ]
    fetch_q = pltpu.make_async_copy(q_ref, qbuf, sem.at[0])
    fetch = [
        pltpu.make_async_copy(suffix_ref.at[:, 0, 0], suf_keys_ref, sem.at[1]),
        pltpu.make_async_copy(prefix_ref.at[0, 1], vals_ref, sem.at[2]),
    ]
    for c in [fetch_q] + key_copies + fetch:
        c.start()
    fetch_q.wait()
    for h in range(heads):
        rowbuf[pl.ds(h, rows, stride=heads), :] = qbuf[:, h * head_dim : (h + 1) * head_dim].astype(F32)
    query = rowbuf[...].astype(BF16)
    query_ref[...] = query
    best = jnp.full(peak_ref.shape, -3.0e38, F32)
    step = min(512, size)
    for j in range(parts):
        key_copies[j].wait()
        for base in range(j * size, (j + 1) * size, step):
            block = nt_dot(keys[base : base + step, :], query)
            scores_ref[base : base + step, :] = block
            best = jnp.maximum(best, jnp.max(block.reshape(step // 8, 8, block.shape[1]), axis=0))
    peak_ref[...] = best
    for c in fetch:
        c.wait()


def weight_copies(weight_ref, outs, spots, sem):
    me = lax.axis_index("tensor")
    z, y = me // 2, me % 2
    copies = []
    for i, (side, k) in enumerate(spots):
        width = outs[i].shape[1]
        column = pl.multiple_of(((z ^ k) * 2 + (y ^ side)) * width, width)
        copies.append(pltpu.make_async_copy(weight_ref.at[:, pl.ds(column, width)], outs[i], sem.at[i]))
    return copies


def suffix_scores_kernel(spots, ids_ref, slot_ref, query_ref, suf_keys_ref, vals_ref, peak_ref, *rest):
    len_ref, suffix_ref, pages_ref, weight_ref = rest[:4]
    tail_ref, high_ref, high_row_ref, vals_t_ref, out_pages_ref, suf_vals_ref = rest[4:10]
    w_refs = rest[10 : 10 + len(spots)]
    lens, seen, list_id, list_pos, sem, sem_page, sem_w = rest[10 + len(spots) :]
    rows, span, head_dim = suf_keys_ref.shape
    tokens = vals_ref.shape[0]
    heads = query_ref.shape[0] // rows
    fetch_len = pltpu.make_async_copy(len_ref, lens, sem.at[1])
    fetch_len.start()
    fetch = [pltpu.make_async_copy(suffix_ref.at[:, 0, 1], suf_vals_ref, sem.at[0])]
    fetch += weight_copies(weight_ref, w_refs, spots, sem_w)
    distinct_list(ids_ref, slot_ref, seen, list_id, list_pos)
    outs = (out_pages_ref.at[0], out_pages_ref.at[1])
    page_copies(pages_ref, outs, list_pos, sem_page, False)
    for c in fetch:
        c.start()
    query = query_ref[...]
    lanes = lax.broadcasted_iota(jnp.int32, (heads, span), 1)
    fetch_len.wait()
    for i in range(rows // 2):
        keys = suf_keys_ref[2 * i : 2 * i + 2].reshape(2 * span, head_dim)
        both = nt_dot(query[2 * heads * i : 2 * heads * (i + 1)], keys)
        for a in range(2):
            mine = both[a * heads : (a + 1) * heads, a * span : (a + 1) * span]
            row = 2 * i + a
            tail_ref[row * heads : (row + 1) * heads, :] = jnp.where(lanes < lens[row], mine, -1.0e30)
    vals_t_ref[head_dim:, :] = jnp.ones((vals_t_ref.shape[0] - head_dim, tokens), BF16)
    step = min(1024, tokens)
    for base in range(0, tokens, step):
        vals_t_ref[:head_dim, base : base + step] = vals_ref[base : base + step, :].astype(F32).T.astype(BF16)
    best = jnp.maximum(tail_ref[:, :128], tail_ref[:, 128:256])
    for b in range(2, span // 128):
        best = jnp.maximum(best, tail_ref[:, b * 128 : (b + 1) * 128])
    across_rows = jnp.broadcast_to(jnp.max(peak_ref[...], axis=0, keepdims=True), (128, peak_ref.shape[1]))
    high = jnp.maximum(across_rows.T, jnp.max(best, axis=1, keepdims=True))
    high_ref[...] = high
    high_row_ref[...] = high.T[:8]
    page_copies(pages_ref, outs, list_pos, sem_page, True)
    for c in fetch:
        c.wait()


def values_kernel(spots, ids_ref, slot_ref, scores, tail, peak, peak_row, vals_t_ref, suf_vals_ref, *rest):
    pages_ref, weight_ref, residual_ref = rest[:3]
    att_ref, shrink_ref, expand_ref, row_slot_ref, slot_mine_ref, res_ref = rest[3:9]
    w_refs = rest[9 : 9 + len(spots)]
    rowbuf, total, acc, acc_t, seen, list_id, list_pos, sem, sem_page, sem_w = rest[9 + len(spots) :]
    rows, span, head_dim = suf_vals_ref.shape
    tokens = vals_t_ref.shape[1]
    heads = att_ref.shape[1] // head_dim
    width = res_ref.shape[1]
    me = lax.axis_index("tensor")
    scale2 = float(head_dim) ** -0.5 * LOG2E
    fetch = weight_copies(weight_ref, w_refs, spots, sem_w)
    fetch.append(
        pltpu.make_async_copy(
            residual_ref.at[:, pl.ds(pl.multiple_of(me * width, width), width)], res_ref, sem.at[0]
        )
    )
    for c in fetch:
        c.start()
    distinct_list(ids_ref, slot_ref, seen, list_id, list_pos)
    page_copies(pages_ref, (shrink_ref, expand_ref), list_pos, sem_page, False)
    row_index = lax.broadcasted_iota(jnp.int32, (rows, 128), 0)
    row_id = jnp.full((rows, 128), -2, jnp.int32)
    for r in range(rows):
        row_id = jnp.where(row_index == r, ids_ref[r], row_id)
    row_slot = jnp.full((rows, 128), -1, jnp.int32)
    slot_index = lax.broadcasted_iota(jnp.int32, (DISTINCT, 128), 0)
    slot_mine = jnp.zeros((DISTINCT, 128), jnp.int32)
    mine = lax.axis_index("req")
    for j in range(DISTINCT):
        row_slot = jnp.where(row_id == list_id[j], j, row_slot)
        owned = (list_pos[j] // pages_ref.shape[0] == mine).astype(jnp.int32)
        slot_mine = jnp.where(slot_index == j, owned, slot_mine)
    row_slot_ref[...] = row_slot
    slot_mine_ref[...] = slot_mine

    acc_t[...] = jnp.zeros(acc_t.shape, F32)
    n_q = acc_t.shape[1]
    chunk = min(2048, tokens)

    @pl.loop(0, tokens // chunk)
    def _(i):
        base = pl.multiple_of(i * chunk, chunk)
        high_row = peak_row[...]
        block = scores[pl.ds(base, chunk), :].reshape(chunk // 8, 8, n_q)
        e = jnp.exp2((block - high_row[None]) * scale2)
        weights = e.reshape(chunk, n_q).astype(BF16)
        acc_t[...] += nn_dot(vals_t_ref[:, pl.ds(base, chunk)], weights)

    across_rows = jnp.broadcast_to(acc_t[head_dim : head_dim + 1, :], (128, n_q))
    acc[...] = acc_t[:head_dim, :].T
    zeros = jnp.zeros((heads, span), F32)
    for i in range(rows // 2):
        lo = 2 * heads * i
        high = jnp.concatenate([peak[lo : lo + 2 * heads, :]] * (span // 128), axis=1)
        e = jnp.exp2((tail[lo : lo + 2 * heads, :] - high) * scale2)
        part_sum = e[:, :128]
        for b in range(1, span // 128):
            part_sum = part_sum + e[:, b * 128 : (b + 1) * 128]
        total[lo : lo + 2 * heads, :] = part_sum
        diag = jnp.concatenate(
            [
                jnp.concatenate([e[:heads], zeros], axis=1),
                jnp.concatenate([zeros, e[heads:]], axis=1),
            ],
            axis=0,
        ).astype(BF16)
        vals = suf_vals_ref[2 * i : 2 * i + 2].reshape(2 * span, head_dim)
        acc[lo : lo + 2 * heads, :] += nn_dot(diag, vals)

    norm = across_rows.T + jnp.sum(total[...], axis=1, keepdims=True)
    rowbuf[...] = acc[...] / norm
    for h in range(heads):
        att_ref[:, h * head_dim : (h + 1) * head_dim] = rowbuf[pl.ds(h, rows, stride=heads), :].astype(BF16)
    page_copies(pages_ref, (shrink_ref, expand_ref), list_pos, sem_page, True)
    for c in fetch:
        c.wait()


def kernel_call(kernel, name, out_shape, specs, scratch, operands, mib, flops, bytes_accessed):
    return pl.pallas_call(
        kernel,
        out_shape=out_shape,
        in_specs=specs,
        out_specs=[VMEM] * len(out_shape),
        scratch_shapes=scratch,
        compiler_params=params(mib),
        cost_estimate=pl.CostEstimate(flops=flops, bytes_accessed=bytes_accessed, transcendentals=0),
        name=name,
    )(*operands)


def attend(
    suffix_len, ids, other_ids, pool_slot, queries, prefix_kv, suffix_kv, out_weight, pages, residual, n_tensor, across
):
    rows = queries.shape[0]
    n_z = n_tensor // 2
    in_rows = out_weight.shape[0]
    width = out_weight.shape[1] // n_tensor
    tokens, head_dim = prefix_kv.shape[2:]
    n_q = rows * queries.shape[1] // head_dim
    span = suffix_kv.shape[3]
    prefix_kv, suffix_kv, out_weight = in_hbm(prefix_kv), in_hbm(suffix_kv), in_hbm(out_weight)
    pages, residual = in_hbm(pages), in_hbm(residual)
    query, scores, peak, vals, suf_keys = kernel_call(
        prefix_scores_kernel,
        "prefix_scores",
        [
            pltpu.VMEM((n_q, head_dim), BF16),
            pltpu.VMEM((tokens, n_q), F32),
            pltpu.VMEM((8, n_q), F32),
            pltpu.VMEM((tokens, head_dim), BF16),
            pltpu.VMEM((rows, span, head_dim), BF16),
        ],
        [ANY, ANY, ANY],
        [
            pltpu.VMEM(queries.shape, BF16),
            pltpu.VMEM((tokens, head_dim), BF16),
            pltpu.VMEM((n_q, head_dim), F32),
            pltpu.SemaphoreType.DMA((3,)),
            pltpu.SemaphoreType.DMA((4,)),
        ],
        [in_hbm(queries), prefix_kv, suffix_kv],
        8,
        2 * n_q * tokens * head_dim,
        6 * MIB,
    )
    far = list(range(n_z - 1, -1, -1))
    early = [(0, k) for k in far[: n_z // 4]]
    late = [(1, k) for k in far if k > 1] + [(0, k) for k in far[n_z // 4 :] if k > 1]
    tail, high, high_row, vals_t, out_pages, suf_vals, *early_w = kernel_call(
        functools.partial(suffix_scores_kernel, early),
        "suffix_scores",
        [
            pltpu.VMEM((n_q, span), F32),
            pltpu.VMEM((n_q, 128), F32),
            pltpu.VMEM((8, n_q), F32),
            pltpu.VMEM((head_dim + 16, tokens), BF16),
            pltpu.VMEM((2, DISTINCT) + pages.shape[2:], BF16),
            pltpu.VMEM((rows, span, head_dim), BF16),
        ]
        + [pltpu.VMEM((in_rows, width), BF16)] * len(early),
        [SMEM, SMEM, VMEM, VMEM, VMEM, VMEM, ANY, ANY, ANY, ANY],
        [pltpu.SMEM((rows,), jnp.int32)]
        + list_scratch(pool_slot)
        + [
            pltpu.SemaphoreType.DMA((2,)),
            pltpu.SemaphoreType.DMA((2, DISTINCT)),
            pltpu.SemaphoreType.DMA((len(early),)),
        ],
        [other_ids, pool_slot, query, suf_keys, vals, peak, in_hbm(suffix_len), suffix_kv, pages, out_weight],
        8,
        1 << 29,
        7 * MIB,
    )
    other_pages = across(out_pages)
    attended, own_shrink, own_expand, row_slot, slot_mine, res, *late_w = kernel_call(
        functools.partial(values_kernel, late),
        "values",
        [
            pltpu.VMEM(queries.shape, BF16),
            pltpu.VMEM((DISTINCT,) + pages.shape[2:], BF16),
            pltpu.VMEM((DISTINCT,) + pages.shape[2:], BF16),
            pltpu.VMEM((rows, 128), jnp.int32),
            pltpu.VMEM((DISTINCT, 128), jnp.int32),
            pltpu.VMEM((rows, width), BF16),
        ]
        + [pltpu.VMEM((in_rows, width), BF16)] * len(late),
        [SMEM, SMEM, VMEM, VMEM, VMEM, VMEM, VMEM, VMEM, ANY, ANY, ANY],
        [
            pltpu.VMEM((n_q, head_dim), F32),
            pltpu.VMEM((n_q, 128), F32),
            pltpu.VMEM((n_q, head_dim), F32),
            pltpu.VMEM((head_dim + 16, n_q), F32),
        ]
        + list_scratch(pool_slot)
        + [
            pltpu.SemaphoreType.DMA((2,)),
            pltpu.SemaphoreType.DMA((2, DISTINCT)),
            pltpu.SemaphoreType.DMA((len(late),)),
        ],
        [ids, pool_slot, scores, tail, high, high_row, vals_t, suf_vals, pages, out_weight, residual],
        8,
        2 * n_q * tokens * head_dim,
        14 * MIB,
    )
    weights = dict(zip(early + late, list(early_w) + list(late_w)))
    return attended, own_shrink, own_expand, other_pages, row_slot, slot_mine, res, weights


def small_call(kernel, name, out_shape, operands, flops=1 << 27):
    return pl.pallas_call(
        kernel,
        out_shape=out_shape,
        in_specs=[VMEM] * len(operands),
        out_specs=jax.tree.map(lambda _: VMEM, out_shape),
        compiler_params=params(8),
        cost_estimate=pl.CostEstimate(flops=flops, bytes_accessed=2 * MIB, transcendentals=0),
        name=name,
    )(*operands)


def merged(own_ref, other, half, slot_mine):
    rank = own_ref.shape[1]
    tiles = []
    for j in range(DISTINCT):
        hit = jnp.broadcast_to(slot_mine[j : j + 1, :1], (rank, 1)) == 1
        tiles.append(jnp.where(hit, own_ref[j].astype(F32), other[half, j].astype(F32)).astype(BF16))
    return jnp.concatenate(tiles, axis=0)


def lane_place(shape, rank):
    return lax.broadcasted_iota(jnp.int32, shape, 1) // rank


def far_kernel(n, att_ref, row_slot_ref, slot_mine_ref, own_ref, other_ref, *rest):
    w_refs = rest[:n]
    out_ref, rank_ref = rest[n:]
    width = w_refs[0].shape[1]
    attended = att_ref[...]
    for k in range(n):
        out_ref[:, k * width : (k + 1) * width] = nn_dot(attended, w_refs[k][...]).astype(BF16)
    rank = own_ref.shape[1]
    per_tile = 128 // rank
    low = nt_dot(attended, merged(own_ref, other_ref, 0, slot_mine_ref[...]))
    row_slot = row_slot_ref[...]
    place = lane_place(row_slot.shape, rank)
    picked = jnp.zeros(row_slot.shape, F32)
    for tile in range(DISTINCT // per_tile):
        hit = row_slot == place + tile * per_tile
        picked = jnp.where(hit, low[:, tile * 128 : (tile + 1) * 128], picked)
    rank_ref[...] = picked
    out_ref[:, n * width :] = picked.astype(BF16)


def near_kernel(spots, att_ref, rank_ref, weight_ref, *rest):
    outs, (wbuf, sem) = rest[: len(spots)], rest[len(spots) :]
    width = wbuf.shape[2]
    copies = weight_copies(weight_ref, [wbuf.at[i] for i in range(len(spots))], spots, sem)
    for c in copies:
        c.start()
    attended = att_ref[...]
    rank = rank_ref[...].astype(BF16)
    for i, out in enumerate(outs):
        copies[i].wait()
        out[:, :width] = nn_dot(attended, wbuf[i]).astype(BF16)
        if out.shape[1] > width:
            out[:, width:] = rank


def near_blocks(spots, columns, attended, rank_own, weight, after, n_tensor):
    rows = attended.shape[0]
    width = weight.shape[1] // n_tensor

    def kernel(att_ref, rank_ref, weight_ref, *rest):
        near_kernel(spots, att_ref, rank_ref, weight_ref, *rest[len(after) :])

    return kernel_call(
        kernel,
        "near_blocks",
        [pltpu.VMEM((rows, columns), BF16)] * len(spots),
        [VMEM, VMEM, ANY] + [VMEM] * len(after),
        [pltpu.VMEM((len(spots), weight.shape[0], width), BF16), pltpu.SemaphoreType.DMA((len(spots),))],
        [attended, rank_own, in_hbm(weight)] + after,
        8,
        1 << 27,
        2 * len(spots) * MIB,
    )


def own_kernel(
    att_ref, res_ref, slot_mine_ref, own_ref, other_ref, weight_ref, after_ref, out_ref, pages_ref, wbuf, sem
):
    (copy,) = weight_copies(weight_ref, [wbuf], [(0, 0)], sem)
    copy.start()
    pages_ref[...] = merged(own_ref, other_ref, 1, slot_mine_ref[...])
    copy.wait()
    out_ref[...] = nn_dot(att_ref[...], wbuf[...]) + res_ref[...].astype(F32)


def own_block(attended, res, slot_mine, own_pages, other_pages, weight, after):
    rows, width = res.shape
    return kernel_call(
        own_kernel,
        "own_block",
        [pltpu.VMEM((rows, width), F32), pltpu.VMEM((DISTINCT * own_pages.shape[1], width), BF16)],
        [VMEM, VMEM, VMEM, VMEM, VMEM, ANY, VMEM],
        [pltpu.VMEM((weight.shape[0], width), BF16), pltpu.SemaphoreType.DMA((1,))],
        [attended, res, slot_mine, own_pages, other_pages, in_hbm(weight), after],
        8,
        0,
        2 * MIB,
    )


def add_kernel(spot, att_ref, w_ref, from_ref, rank_ref, *rest):
    out_ref = rest[-1]
    width = w_ref.shape[1]
    both = nn_dot(att_ref[...], w_ref[...]) + from_ref[:, spot * width : (spot + 1) * width].astype(F32)
    out_ref[:, :width] = both.astype(BF16)
    rank_both = rank_ref[...] + from_ref[:, from_ref.shape[1] - 128 :].astype(F32)
    out_ref[:, width:] = rank_both.astype(BF16)


def finish_kernel(*refs):
    own_ref, pages_ref, row_slot_ref, rank_ref, far_ref, from_ref = refs[:6]
    moved, out_ref = refs[6:-1], refs[-1]
    rank = pages_ref.shape[0] // DISTINCT
    per_tile = 128 // rank
    width = own_ref.shape[1]
    low = rank_ref[...] + far_ref[:, far_ref.shape[1] - 128 :].astype(F32)
    for ref in moved:
        low = low + ref[:, width:].astype(F32)
    row_slot = row_slot_ref[...]
    place = lane_place(row_slot.shape, rank)
    tiles = []
    for tile in range(DISTINCT // per_tile):
        tiles.append(jnp.where(row_slot == place + tile * per_tile, low, 0.0).astype(BF16))
    total = nn_dot(jnp.concatenate(tiles, axis=1), pages_ref[...])
    total = total + (own_ref[...] + from_ref[...].astype(F32))
    for ref in moved:
        total = total + ref[:, :width].astype(F32)
    out_ref[...] = total.astype(BF16)


def place_kernel(spots, *refs):
    blocks = refs[: len(spots)]
    out_ref, sem = refs[-2:]
    width = blocks[0].shape[1]
    me = lax.axis_index("tensor")
    z, y = me // 2, me % 2
    copies = []
    for i, (k, side) in enumerate(spots):
        column = pl.multiple_of(((z ^ k) * 2 + (y ^ side)) * width, width)
        copies.append(pltpu.make_async_copy(blocks[i], out_ref.at[:, pl.ds(column, width)], sem.at[i]))
    for c in copies:
        c.start()
    for c in copies:
        c.wait()


def place(blocks, spots, n_tensor, held=None):
    rows, width = blocks[0].shape
    extra = [] if held is None else [held]
    return pl.pallas_call(
        functools.partial(place_kernel, spots),
        out_shape=pltpu.HBM((rows, width * n_tensor), BF16),
        in_specs=[VMEM] * len(blocks) + [ANY] * len(extra),
        out_specs=ANY,
        scratch_shapes=[pltpu.SemaphoreType.DMA((len(blocks),))],
        input_output_aliases={len(blocks): 0} if extra else {},
        compiler_params=params(4),
        cost_estimate=pl.CostEstimate(flops=0, bytes_accessed=1 * MIB, transcendentals=0),
        name="place",
    )(*blocks, *extra)


def body(
    n_tensor,
    queries,
    prefix_kv,
    suffix_kv,
    suffix_len,
    residual,
    out_weight,
    adapter_pages,
    adapter_ids,
    pool_slot,
):
    n_z = n_tensor // 2

    def along_y(x):
        return lax.ppermute(x, "tensor", [(t, t ^ 1) for t in range(n_tensor)])

    def along_z(x, k):
        return lax.ppermute(x, "tensor", [(t, t ^ (2 * k)) for t in range(n_tensor)])

    def along_both(x, k):
        return lax.ppermute(x, "tensor", [(t, t ^ (2 * k) ^ 1) for t in range(n_tensor)])

    def across(x):
        return lax.ppermute(x, "req", [(0, 1), (1, 0)])

    rows = queries.shape[0]
    width = out_weight.shape[1] // n_tensor
    attended, own_shrink, own_expand, other_pages, row_slot, slot_mine, res, weights = attend(
        suffix_len,
        adapter_ids,
        across(adapter_ids),
        pool_slot,
        queries,
        prefix_kv,
        suffix_kv,
        out_weight,
        adapter_pages,
        residual,
        n_tensor,
        across,
    )
    far = list(range(n_z - 1, 1, -1))
    piece_shape = pltpu.VMEM((rows, width + 128), BF16)
    far_out, rank_own = small_call(
        functools.partial(far_kernel, len(far)),
        "far_blocks",
        [pltpu.VMEM((rows, len(far) * width + 128), BF16), pltpu.VMEM((rows, 128), F32)],
        [attended, row_slot, slot_mine, own_shrink, other_pages] + [weights[1, k] for k in far],
    )
    from_far = along_y(far_out)
    straight, cross = near_blocks(
        [(0, 1), (1, 1)], width + 128, attended, rank_own, out_weight, [], n_tensor
    )
    moved = [along_z(straight, 1), along_both(cross, 1)]
    after = []
    for spot, k in enumerate(far):
        piece = small_call(
            functools.partial(add_kernel, spot),
            "add_block",
            piece_shape,
            [attended, weights[0, k], from_far, rank_own] + after,
        )
        moved.append(along_z(piece, k))
        after = [piece]
    (own_far,) = near_blocks([(1, 0)], width, attended, rank_own, out_weight, [piece], n_tensor)
    from_own = along_y(own_far)
    own, expand_pages = own_block(attended, res, slot_mine, own_expand, other_pages, out_weight, own_far)
    result = small_call(
        finish_kernel,
        "finish",
        pltpu.VMEM((rows, width), BF16),
        [own, expand_pages, row_slot, rank_own, from_far, from_own] + moved,
    )
    held = [result] + [along_z(result, k) for k in range(1, n_z)]
    crossed = [along_both(result, k) if k < 2 else along_y(held[k]) for k in range(n_z)]
    spots = [(0, 0), (1, 1), (1, 0)] + [(k, side) for k in range(2, n_z) for side in (0, 1)]
    spots.insert(len(spots) - 2, (0, 1))
    forwarded = [(k, side) for k, side in spots if k and side]
    placed = None
    for group in ([p for p in spots if p not in forwarded], forwarded):
        placed = place([(crossed if side else held)[k] for k, side in group], group, n_tensor, placed)
    return placed


def solution(mesh):
    return jax.shard_map(
        functools.partial(body, mesh.shape["tensor"]),
        mesh=mesh,
        in_specs=(
            P(("group", "req"), "tensor"),
            P(("group", "tensor"), None, None, None),
            P(("group", "req"), "tensor", None, None, None),
            P(("group", "req")),
            P(("group", "req"), None),
            P("tensor", None),
            P("req", None, None, "tensor"),
            P(("group", "req")),
            P(),
        ),
        out_specs=P(("group", "req"), None),
        check_vma=False,
    )
```

```python
import functools

import jax
import jax.numpy as jnp
from jax import lax
from jax.experimental import pallas as pl
from jax.experimental.pallas import tpu as pltpu
from jax.sharding import PartitionSpec as P

F32 = jnp.float32
BF16 = jnp.bfloat16
LOG2E = 1.4426950408889634
ANY = pl.BlockSpec(memory_space=pl.ANY)
VMEM = pl.BlockSpec(memory_space=pltpu.VMEM)
SMEM = pl.BlockSpec(memory_space=pltpu.SMEM)
MIB = 1 << 20
DISTINCT = 8


def in_hbm(x):
    return pltpu.with_memory_space_constraint(x, pltpu.HBM)


def params(mib):
    return pltpu.CompilerParams(vmem_limit_bytes=mib * MIB)


def nt_dot(a, b):
    return lax.dot_general(a, b, (((1,), (1,)), ((), ())), preferred_element_type=F32)


def nn_dot(a, b):
    return jnp.dot(a, b, preferred_element_type=F32)


def distinct_list(ids_ref, pool_slot_ref, seen, list_id, list_pos):
    rows = ids_ref.shape[0]
    for i in range(pool_slot_ref.shape[0]):
        seen[i] = 0
    for j in range(DISTINCT + 1):
        list_id[j] = -1
        list_pos[j] = 0
    found = jnp.int32(0)
    for r in range(rows):
        one = ids_ref[r]
        fresh = 1 - seen[one]
        seen[one] = 1
        spot = jnp.minimum(found, DISTINCT)
        list_id[spot] = jnp.where(fresh == 1, one, list_id[spot])
        list_pos[spot] = jnp.where(fresh == 1, pool_slot_ref[one], list_pos[spot])
        found = found + fresh


def list_scratch(pool_slot):
    return [
        pltpu.SMEM((pool_slot.shape[0],), jnp.int32),
        pltpu.SMEM((DISTINCT + 1,), jnp.int32),
        pltpu.SMEM((DISTINCT + 1,), jnp.int32),
    ]


def page_copies(pages_ref, outs, list_pos, sem, wait):
    pool = pages_ref.shape[0]
    me = lax.axis_index("req")
    for j in range(DISTINCT):
        pos = list_pos[j]

        @pl.when(pos // pool == me)
        def _():
            for i, out in enumerate(outs):
                copy = pltpu.make_async_copy(pages_ref.at[pos % pool, i], out.at[j], sem.at[i, j])
                if wait:
                    copy.wait()
                else:
                    copy.start()


def prefix_scores_kernel(
    q_ref, prefix_ref, suffix_ref, query_ref, scores_ref, peak_ref, vals_ref, suf_keys_ref, qbuf, keys, rowbuf, sem, sem_keys
):
    rows = q_ref.shape[0]
    tokens, head_dim = keys.shape
    heads = q_ref.shape[1] // head_dim
    parts = sem_keys.shape[0]
    size = tokens // parts
    key_copies = [
        pltpu.make_async_copy(
            prefix_ref.at[0, 0, pl.ds(j * size, size)], keys.at[pl.ds(j * size, size)], sem_keys.at[j]
        )
        for j in range(parts)
    ]
    fetch_q = pltpu.make_async_copy(q_ref, qbuf, sem.at[0])
    fetch = [
        pltpu.make_async_copy(suffix_ref.at[:, 0, 0], suf_keys_ref, sem.at[1]),
        pltpu.make_async_copy(prefix_ref.at[0, 1], vals_ref, sem.at[2]),
    ]
    for c in [fetch_q] + key_copies + fetch:
        c.start()
    fetch_q.wait()
    for h in range(heads):
        rowbuf[pl.ds(h, rows, stride=heads), :] = qbuf[:, h * head_dim : (h + 1) * head_dim].astype(F32)
    query = rowbuf[...].astype(BF16)
    query_ref[...] = query
    best = jnp.full(peak_ref.shape, -3.0e38, F32)
    step = min(512, size)
    for j in range(parts):
        key_copies[j].wait()
        for base in range(j * size, (j + 1) * size, step):
            block = nt_dot(keys[base : base + step, :], query)
            scores_ref[base : base + step, :] = block
            best = jnp.maximum(best, jnp.max(block.reshape(step // 8, 8, block.shape[1]), axis=0))
    peak_ref[...] = best
    for c in fetch:
        c.wait()


def weight_copies(weight_ref, outs, spots, sem):
    me = lax.axis_index("tensor")
    z, y = me // 2, me % 2
    copies = []
    for i, (side, k) in enumerate(spots):
        width = outs[i].shape[1]
        column = pl.multiple_of(((z ^ k) * 2 + (y ^ side)) * width, width)
        copies.append(pltpu.make_async_copy(weight_ref.at[:, pl.ds(column, width)], outs[i], sem.at[i]))
    return copies


def suffix_scores_kernel(spots, ids_ref, slot_ref, query_ref, suf_keys_ref, vals_ref, peak_ref, *rest):
    len_ref, suffix_ref, pages_ref, weight_ref = rest[:4]
    tail_ref, high_ref, high_row_ref, vals_t_ref, out_pages_ref, suf_vals_ref = rest[4:10]
    w_refs = rest[10 : 10 + len(spots)]
    lens, seen, list_id, list_pos, sem, sem_page, sem_w = rest[10 + len(spots) :]
    rows, span, head_dim = suf_keys_ref.shape
    tokens = vals_ref.shape[0]
    heads = query_ref.shape[0] // rows
    fetch_len = pltpu.make_async_copy(len_ref, lens, sem.at[1])
    fetch_len.start()
    fetch = [pltpu.make_async_copy(suffix_ref.at[:, 0, 1], suf_vals_ref, sem.at[0])]
    fetch += weight_copies(weight_ref, w_refs, spots, sem_w)
    distinct_list(ids_ref, slot_ref, seen, list_id, list_pos)
    outs = (out_pages_ref.at[0], out_pages_ref.at[1])
    page_copies(pages_ref, outs, list_pos, sem_page, False)
    for c in fetch:
        c.start()
    query = query_ref[...]
    lanes = lax.broadcasted_iota(jnp.int32, (heads, span), 1)
    fetch_len.wait()
    for i in range(rows // 2):
        keys = suf_keys_ref[2 * i : 2 * i + 2].reshape(2 * span, head_dim)
        both = nt_dot(query[2 * heads * i : 2 * heads * (i + 1)], keys)
        for a in range(2):
            mine = both[a * heads : (a + 1) * heads, a * span : (a + 1) * span]
            row = 2 * i + a
            tail_ref[row * heads : (row + 1) * heads, :] = jnp.where(lanes < lens[row], mine, -1.0e30)
    vals_t_ref[head_dim:, :] = jnp.ones((vals_t_ref.shape[0] - head_dim, tokens), BF16)
    step = min(1024, tokens)
    for base in range(0, tokens, step):
        vals_t_ref[:head_dim, base : base + step] = vals_ref[base : base + step, :].astype(F32).T.astype(BF16)
    best = jnp.maximum(tail_ref[:, :128], tail_ref[:, 128:256])
    for b in range(2, span // 128):
        best = jnp.maximum(best, tail_ref[:, b * 128 : (b + 1) * 128])
    across_rows = jnp.broadcast_to(jnp.max(peak_ref[...], axis=0, keepdims=True), (128, peak_ref.shape[1]))
    high = jnp.maximum(across_rows.T, jnp.max(best, axis=1, keepdims=True))
    high_ref[...] = high
    high_row_ref[...] = high.T[:8]
    page_copies(pages_ref, outs, list_pos, sem_page, True)
    for c in fetch:
        c.wait()


def values_kernel(spots, ids_ref, slot_ref, scores, tail, peak, peak_row, vals_t_ref, suf_vals_ref, *rest):
    pages_ref, weight_ref, residual_ref = rest[:3]
    att_ref, shrink_ref, expand_ref, row_slot_ref, slot_mine_ref, res_ref = rest[3:9]
    w_refs = rest[9 : 9 + len(spots)]
    rowbuf, total, acc, acc_t, seen, list_id, list_pos, sem, sem_page, sem_w = rest[9 + len(spots) :]
    rows, span, head_dim = suf_vals_ref.shape
    tokens = vals_t_ref.shape[1]
    heads = att_ref.shape[1] // head_dim
    width = res_ref.shape[1]
    me = lax.axis_index("tensor")
    scale2 = float(head_dim) ** -0.5 * LOG2E
    fetch = weight_copies(weight_ref, w_refs, spots, sem_w)
    fetch.append(
        pltpu.make_async_copy(
            residual_ref.at[:, pl.ds(pl.multiple_of(me * width, width), width)], res_ref, sem.at[0]
        )
    )
    for c in fetch:
        c.start()
    distinct_list(ids_ref, slot_ref, seen, list_id, list_pos)
    page_copies(pages_ref, (shrink_ref, expand_ref), list_pos, sem_page, False)
    row_index = lax.broadcasted_iota(jnp.int32, (rows, 128), 0)
    row_id = jnp.full((rows, 128), -2, jnp.int32)
    for r in range(rows):
        row_id = jnp.where(row_index == r, ids_ref[r], row_id)
    row_slot = jnp.full((rows, 128), -1, jnp.int32)
    slot_index = lax.broadcasted_iota(jnp.int32, (DISTINCT, 128), 0)
    slot_mine = jnp.zeros((DISTINCT, 128), jnp.int32)
    mine = lax.axis_index("req")
    for j in range(DISTINCT):
        row_slot = jnp.where(row_id == list_id[j], j, row_slot)
        owned = (list_pos[j] // pages_ref.shape[0] == mine).astype(jnp.int32)
        slot_mine = jnp.where(slot_index == j, owned, slot_mine)
    row_slot_ref[...] = row_slot
    slot_mine_ref[...] = slot_mine

    acc_t[...] = jnp.zeros(acc_t.shape, F32)
    n_q = acc_t.shape[1]
    chunk = min(2048, tokens)

    @pl.loop(0, tokens // chunk)
    def _(i):
        base = pl.multiple_of(i * chunk, chunk)
        high_row = peak_row[...]
        block = scores[pl.ds(base, chunk), :].reshape(chunk // 8, 8, n_q)
        e = jnp.exp2((block - high_row[None]) * scale2)
        weights = e.reshape(chunk, n_q).astype(BF16)
        acc_t[...] += nn_dot(vals_t_ref[:, pl.ds(base, chunk)], weights)

    across_rows = jnp.broadcast_to(acc_t[head_dim : head_dim + 1, :], (128, n_q))
    acc[...] = acc_t[:head_dim, :].T
    zeros = jnp.zeros((heads, span), F32)
    for i in range(rows // 2):
        lo = 2 * heads * i
        high = jnp.concatenate([peak[lo : lo + 2 * heads, :]] * (span // 128), axis=1)
        e = jnp.exp2((tail[lo : lo + 2 * heads, :] - high) * scale2)
        part_sum = e[:, :128]
        for b in range(1, span // 128):
            part_sum = part_sum + e[:, b * 128 : (b + 1) * 128]
        total[lo : lo + 2 * heads, :] = part_sum
        diag = jnp.concatenate(
            [
                jnp.concatenate([e[:heads], zeros], axis=1),
                jnp.concatenate([zeros, e[heads:]], axis=1),
            ],
            axis=0,
        ).astype(BF16)
        vals = suf_vals_ref[2 * i : 2 * i + 2].reshape(2 * span, head_dim)
        acc[lo : lo + 2 * heads, :] += nn_dot(diag, vals)

    norm = across_rows.T + jnp.sum(total[...], axis=1, keepdims=True)
    rowbuf[...] = acc[...] / norm
    for h in range(heads):
        att_ref[:, h * head_dim : (h + 1) * head_dim] = rowbuf[pl.ds(h, rows, stride=heads), :].astype(BF16)
    page_copies(pages_ref, (shrink_ref, expand_ref), list_pos, sem_page, True)
    for c in fetch:
        c.wait()


def kernel_call(kernel, name, out_shape, specs, scratch, operands, mib, flops, bytes_accessed):
    return pl.pallas_call(
        kernel,
        out_shape=out_shape,
        in_specs=specs,
        out_specs=[VMEM] * len(out_shape),
        scratch_shapes=scratch,
        compiler_params=params(mib),
        cost_estimate=pl.CostEstimate(flops=flops, bytes_accessed=bytes_accessed, transcendentals=0),
        name=name,
    )(*operands)


def attend(
    suffix_len, ids, other_ids, pool_slot, queries, prefix_kv, suffix_kv, out_weight, pages, residual, n_tensor, across
):
    rows = queries.shape[0]
    n_z = n_tensor // 2
    in_rows = out_weight.shape[0]
    width = out_weight.shape[1] // n_tensor
    tokens, head_dim = prefix_kv.shape[2:]
    n_q = rows * queries.shape[1] // head_dim
    span = suffix_kv.shape[3]
    prefix_kv, suffix_kv, out_weight = in_hbm(prefix_kv), in_hbm(suffix_kv), in_hbm(out_weight)
    pages, residual = in_hbm(pages), in_hbm(residual)
    query, scores, peak, vals, suf_keys = kernel_call(
        prefix_scores_kernel,
        "prefix_scores",
        [
            pltpu.VMEM((n_q, head_dim), BF16),
            pltpu.VMEM((tokens, n_q), F32),
            pltpu.VMEM((8, n_q), F32),
            pltpu.VMEM((tokens, head_dim), BF16),
            pltpu.VMEM((rows, span, head_dim), BF16),
        ],
        [ANY, ANY, ANY],
        [
            pltpu.VMEM(queries.shape, BF16),
            pltpu.VMEM((tokens, head_dim), BF16),
            pltpu.VMEM((n_q, head_dim), F32),
            pltpu.SemaphoreType.DMA((3,)),
            pltpu.SemaphoreType.DMA((4,)),
        ],
        [in_hbm(queries), prefix_kv, suffix_kv],
        8,
        2 * n_q * tokens * head_dim,
        6 * MIB,
    )
    far = list(range(n_z - 1, -1, -1))
    early = [(0, k) for k in far[: n_z // 4]]
    late = [(1, k) for k in far if k > 1] + [(0, k) for k in far[n_z // 4 :] if k > 1]
    tail, high, high_row, vals_t, out_pages, suf_vals, *early_w = kernel_call(
        functools.partial(suffix_scores_kernel, early),
        "suffix_scores",
        [
            pltpu.VMEM((n_q, span), F32),
            pltpu.VMEM((n_q, 128), F32),
            pltpu.VMEM((8, n_q), F32),
            pltpu.VMEM((head_dim + 16, tokens), BF16),
            pltpu.VMEM((2, DISTINCT) + pages.shape[2:], BF16),
            pltpu.VMEM((rows, span, head_dim), BF16),
        ]
        + [pltpu.VMEM((in_rows, width), BF16)] * len(early),
        [SMEM, SMEM, VMEM, VMEM, VMEM, VMEM, ANY, ANY, ANY, ANY],
        [pltpu.SMEM((rows,), jnp.int32)]
        + list_scratch(pool_slot)
        + [
            pltpu.SemaphoreType.DMA((2,)),
            pltpu.SemaphoreType.DMA((2, DISTINCT)),
            pltpu.SemaphoreType.DMA((len(early),)),
        ],
        [other_ids, pool_slot, query, suf_keys, vals, peak, in_hbm(suffix_len), suffix_kv, pages, out_weight],
        8,
        1 << 29,
        7 * MIB,
    )
    other_pages = across(out_pages)
    attended, own_shrink, own_expand, row_slot, slot_mine, res, *late_w = kernel_call(
        functools.partial(values_kernel, late),
        "values",
        [
            pltpu.VMEM(queries.shape, BF16),
            pltpu.VMEM((DISTINCT,) + pages.shape[2:], BF16),
            pltpu.VMEM((DISTINCT,) + pages.shape[2:], BF16),
            pltpu.VMEM((rows, 128), jnp.int32),
            pltpu.VMEM((DISTINCT, 128), jnp.int32),
            pltpu.VMEM((rows, width), BF16),
        ]
        + [pltpu.VMEM((in_rows, width), BF16)] * len(late),
        [SMEM, SMEM, VMEM, VMEM, VMEM, VMEM, VMEM, VMEM, ANY, ANY, ANY],
        [
            pltpu.VMEM((n_q, head_dim), F32),
            pltpu.VMEM((n_q, 128), F32),
            pltpu.VMEM((n_q, head_dim), F32),
            pltpu.VMEM((head_dim + 16, n_q), F32),
        ]
        + list_scratch(pool_slot)
        + [
            pltpu.SemaphoreType.DMA((2,)),
            pltpu.SemaphoreType.DMA((2, DISTINCT)),
            pltpu.SemaphoreType.DMA((len(late),)),
        ],
        [ids, pool_slot, scores, tail, high, high_row, vals_t, suf_vals, pages, out_weight, residual],
        8,
        2 * n_q * tokens * head_dim,
        14 * MIB,
    )
    weights = dict(zip(early + late, list(early_w) + list(late_w)))
    return attended, own_shrink, own_expand, other_pages, row_slot, slot_mine, res, weights


def small_call(kernel, name, out_shape, operands, flops=1 << 27):
    return pl.pallas_call(
        kernel,
        out_shape=out_shape,
        in_specs=[VMEM] * len(operands),
        out_specs=jax.tree.map(lambda _: VMEM, out_shape),
        compiler_params=params(8),
        cost_estimate=pl.CostEstimate(flops=flops, bytes_accessed=2 * MIB, transcendentals=0),
        name=name,
    )(*operands)


def merged(own_ref, other, half, slot_mine):
    rank = own_ref.shape[1]
    tiles = []
    for j in range(DISTINCT):
        hit = jnp.broadcast_to(slot_mine[j : j + 1, :1], (rank, 1)) == 1
        tiles.append(jnp.where(hit, own_ref[j].astype(F32), other[half, j].astype(F32)).astype(BF16))
    return jnp.concatenate(tiles, axis=0)


def lane_place(shape, rank):
    return lax.broadcasted_iota(jnp.int32, shape, 1) // rank


def far_kernel(n, att_ref, row_slot_ref, slot_mine_ref, own_ref, other_ref, *rest):
    w_refs = rest[:n]
    out_ref, rank_ref = rest[n:]
    width = w_refs[0].shape[1]
    attended = att_ref[...]
    for k in range(n):
        out_ref[:, k * width : (k + 1) * width] = nn_dot(attended, w_refs[k][...]).astype(BF16)
    rank = own_ref.shape[1]
    per_tile = 128 // rank
    low = nt_dot(attended, merged(own_ref, other_ref, 0, slot_mine_ref[...]))
    row_slot = row_slot_ref[...]
    place = lane_place(row_slot.shape, rank)
    picked = jnp.zeros(row_slot.shape, F32)
    for tile in range(DISTINCT // per_tile):
        hit = row_slot == place + tile * per_tile
        picked = jnp.where(hit, low[:, tile * 128 : (tile + 1) * 128], picked)
    rank_ref[...] = picked
    out_ref[:, n * width :] = picked.astype(BF16)


def near_kernel(spots, att_ref, rank_ref, weight_ref, *rest):
    outs, (wbuf, sem) = rest[: len(spots)], rest[len(spots) :]
    width = wbuf.shape[2]
    copies = weight_copies(weight_ref, [wbuf.at[i] for i in range(len(spots))], spots, sem)
    for c in copies:
        c.start()
    attended = att_ref[...]
    rank = rank_ref[...].astype(BF16)
    for i, out in enumerate(outs):
        copies[i].wait()
        out[:, :width] = nn_dot(attended, wbuf[i]).astype(BF16)
        if out.shape[1] > width:
            out[:, width:] = rank


def near_blocks(spots, columns, attended, rank_own, weight, after, n_tensor):
    rows = attended.shape[0]
    width = weight.shape[1] // n_tensor

    def kernel(att_ref, rank_ref, weight_ref, *rest):
        near_kernel(spots, att_ref, rank_ref, weight_ref, *rest[len(after) :])

    return kernel_call(
        kernel,
        "near_blocks",
        [pltpu.VMEM((rows, columns), BF16)] * len(spots),
        [VMEM, VMEM, ANY] + [VMEM] * len(after),
        [pltpu.VMEM((len(spots), weight.shape[0], width), BF16), pltpu.SemaphoreType.DMA((len(spots),))],
        [attended, rank_own, in_hbm(weight)] + after,
        8,
        1 << 27,
        2 * len(spots) * MIB,
    )


def own_kernel(
    att_ref, res_ref, slot_mine_ref, own_ref, other_ref, weight_ref, after_ref, out_ref, pages_ref, wbuf, sem
):
    (copy,) = weight_copies(weight_ref, [wbuf], [(0, 0)], sem)
    copy.start()
    pages_ref[...] = merged(own_ref, other_ref, 1, slot_mine_ref[...])
    copy.wait()
    out_ref[...] = nn_dot(att_ref[...], wbuf[...]) + res_ref[...].astype(F32)


def own_block(attended, res, slot_mine, own_pages, other_pages, weight, after):
    rows, width = res.shape
    return kernel_call(
        own_kernel,
        "own_block",
        [pltpu.VMEM((rows, width), F32), pltpu.VMEM((DISTINCT * own_pages.shape[1], width), BF16)],
        [VMEM, VMEM, VMEM, VMEM, VMEM, ANY, VMEM],
        [pltpu.VMEM((weight.shape[0], width), BF16), pltpu.SemaphoreType.DMA((1,))],
        [attended, res, slot_mine, own_pages, other_pages, in_hbm(weight), after],
        8,
        0,
        2 * MIB,
    )


def add_kernel(spot, att_ref, w_ref, from_ref, rank_ref, *rest):
    out_ref = rest[-1]
    width = w_ref.shape[1]
    both = nn_dot(att_ref[...], w_ref[...]) + from_ref[:, spot * width : (spot + 1) * width].astype(F32)
    out_ref[:, :width] = both.astype(BF16)
    rank_both = rank_ref[...] + from_ref[:, from_ref.shape[1] - 128 :].astype(F32)
    out_ref[:, width:] = rank_both.astype(BF16)


def finish_kernel(*refs):
    own_ref, pages_ref, row_slot_ref, rank_ref, far_ref, from_ref = refs[:6]
    moved, out_ref = refs[6:-1], refs[-1]
    rank = pages_ref.shape[0] // DISTINCT
    per_tile = 128 // rank
    width = own_ref.shape[1]
    low = rank_ref[...] + far_ref[:, far_ref.shape[1] - 128 :].astype(F32)
    for ref in moved:
        low = low + ref[:, width:].astype(F32)
    row_slot = row_slot_ref[...]
    place = lane_place(row_slot.shape, rank)
    tiles = []
    for tile in range(DISTINCT // per_tile):
        tiles.append(jnp.where(row_slot == place + tile * per_tile, low, 0.0).astype(BF16))
    total = nn_dot(jnp.concatenate(tiles, axis=1), pages_ref[...])
    total = total + (own_ref[...] + from_ref[...].astype(F32))
    for ref in moved:
        total = total + ref[:, :width].astype(F32)
    out_ref[...] = total.astype(BF16)


def place_kernel(spots, *refs):
    blocks = refs[: len(spots)]
    out_ref, sem = refs[-2:]
    width = blocks[0].shape[1]
    me = lax.axis_index("tensor")
    z, y = me // 2, me % 2
    copies = []
    for i, (k, side) in enumerate(spots):
        column = pl.multiple_of(((z ^ k) * 2 + (y ^ side)) * width, width)
        copies.append(pltpu.make_async_copy(blocks[i], out_ref.at[:, pl.ds(column, width)], sem.at[i]))
    for c in copies:
        c.start()
    for c in copies:
        c.wait()


def place(blocks, spots, n_tensor, held=None):
    rows, width = blocks[0].shape
    extra = [] if held is None else [held]
    return pl.pallas_call(
        functools.partial(place_kernel, spots),
        out_shape=pltpu.HBM((rows, width * n_tensor), BF16),
        in_specs=[VMEM] * len(blocks) + [ANY] * len(extra),
        out_specs=ANY,
        scratch_shapes=[pltpu.SemaphoreType.DMA((len(blocks),))],
        input_output_aliases={len(blocks): 0} if extra else {},
        compiler_params=params(4),
        cost_estimate=pl.CostEstimate(flops=0, bytes_accessed=1 * MIB, transcendentals=0),
        name="place",
    )(*blocks, *extra)


def body(
    n_tensor,
    queries,
    prefix_kv,
    suffix_kv,
    suffix_len,
    residual,
    out_weight,
    adapter_pages,
    adapter_ids,
    pool_slot,
):
    n_z = n_tensor // 2

    def along_y(x):
        return lax.ppermute(x, "tensor", [(t, t ^ 1) for t in range(n_tensor)])

    def along_z(x, k):
        return lax.ppermute(x, "tensor", [(t, t ^ (2 * k)) for t in range(n_tensor)])

    def along_both(x, k):
        return lax.ppermute(x, "tensor", [(t, t ^ (2 * k) ^ 1) for t in range(n_tensor)])

    def across(x):
        return lax.ppermute(x, "req", [(0, 1), (1, 0)])

    rows = queries.shape[0]
    width = out_weight.shape[1] // n_tensor
    attended, own_shrink, own_expand, other_pages, row_slot, slot_mine, res, weights = attend(
        suffix_len,
        adapter_ids,
        across(adapter_ids),
        pool_slot,
        queries,
        prefix_kv,
        suffix_kv,
        out_weight,
        adapter_pages,
        residual,
        n_tensor,
        across,
    )
    far = list(range(n_z - 1, 1, -1))
    piece_shape = pltpu.VMEM((rows, width + 128), BF16)
    far_out, rank_own = small_call(
        functools.partial(far_kernel, len(far)),
        "far_blocks",
        [pltpu.VMEM((rows, len(far) * width + 128), BF16), pltpu.VMEM((rows, 128), F32)],
        [attended, row_slot, slot_mine, own_shrink, other_pages] + [weights[1, k] for k in far],
    )
    from_far = along_y(far_out)
    straight, cross = near_blocks(
        [(0, 1), (1, 1)], width + 128, attended, rank_own, out_weight, [], n_tensor
    )
    moved = [along_z(straight, 1), along_both(cross, 1)]
    after = []
    for spot, k in enumerate(far):
        piece = small_call(
            functools.partial(add_kernel, spot),
            "add_block",
            piece_shape,
            [attended, weights[0, k], from_far, rank_own] + after,
        )
        moved.append(along_z(piece, k))
        after = [piece]
    (own_far,) = near_blocks([(1, 0)], width, attended, rank_own, out_weight, [piece], n_tensor)
    from_own = along_y(own_far)
    own, expand_pages = own_block(attended, res, slot_mine, own_expand, other_pages, out_weight, own_far)
    result = small_call(
        finish_kernel,
        "finish",
        pltpu.VMEM((rows, width), BF16),
        [own, expand_pages, row_slot, rank_own, from_far, from_own] + moved,
    )
    held = [result] + [along_z(result, k) for k in range(1, n_z)]
    crossed = [along_y(held[k]) for k in range(n_z)]
    spots = [(k, side) for k in range(n_z) for side in (0, 1) if (k, side) != (0, 1)]
    spots.insert(len(spots) - 2, (0, 1))
    forwarded = [(k, side) for k, side in spots if k and side]
    placed = None
    for group in ([p for p in spots if p not in forwarded], forwarded):
        placed = place([(crossed if side else held)[k] for k, side in group], group, n_tensor, placed)
    return placed


def solution(mesh):
    return jax.shard_map(
        functools.partial(body, mesh.shape["tensor"]),
        mesh=mesh,
        in_specs=(
            P(("group", "req"), "tensor"),
            P(("group", "tensor"), None, None, None),
            P(("group", "req"), "tensor", None, None, None),
            P(("group", "req")),
            P(("group", "req"), None),
            P("tensor", None),
            P("req", None, None, "tensor"),
            P(("group", "req")),
            P(),
        ),
        out_specs=P(("group", "req"), None),
        check_vma=False,
    )
```

```python
import functools

import jax
import jax.numpy as jnp
from jax import lax
from jax.experimental import pallas as pl
from jax.experimental.pallas import tpu as pltpu
from jax.sharding import PartitionSpec as P

F32 = jnp.float32
BF16 = jnp.bfloat16
LOG2E = 1.4426950408889634
ANY = pl.BlockSpec(memory_space=pl.ANY)
VMEM = pl.BlockSpec(memory_space=pltpu.VMEM)
SMEM = pl.BlockSpec(memory_space=pltpu.SMEM)
MIB = 1 << 20
DISTINCT = 8


def in_hbm(x):
    return pltpu.with_memory_space_constraint(x, pltpu.HBM)


def params(mib):
    return pltpu.CompilerParams(vmem_limit_bytes=mib * MIB)


def nt_dot(a, b):
    return lax.dot_general(a, b, (((1,), (1,)), ((), ())), preferred_element_type=F32)


def nn_dot(a, b):
    return jnp.dot(a, b, preferred_element_type=F32)


def distinct_list(ids_ref, pool_slot_ref, seen, list_id, list_pos):
    rows = ids_ref.shape[0]
    for i in range(pool_slot_ref.shape[0]):
        seen[i] = 0
    for j in range(DISTINCT + 1):
        list_id[j] = -1
        list_pos[j] = 0
    found = jnp.int32(0)
    for r in range(rows):
        one = ids_ref[r]
        fresh = 1 - seen[one]
        seen[one] = 1
        spot = jnp.minimum(found, DISTINCT)
        list_id[spot] = jnp.where(fresh == 1, one, list_id[spot])
        list_pos[spot] = jnp.where(fresh == 1, pool_slot_ref[one], list_pos[spot])
        found = found + fresh


def list_scratch(pool_slot):
    return [
        pltpu.SMEM((pool_slot.shape[0],), jnp.int32),
        pltpu.SMEM((DISTINCT + 1,), jnp.int32),
        pltpu.SMEM((DISTINCT + 1,), jnp.int32),
    ]


def page_copies(pages_ref, outs, list_pos, sem, wait):
    pool = pages_ref.shape[0]
    me = lax.axis_index("req")
    for j in range(DISTINCT):
        pos = list_pos[j]

        @pl.when(pos // pool == me)
        def _():
            for i, out in enumerate(outs):
                copy = pltpu.make_async_copy(pages_ref.at[pos % pool, i], out.at[j], sem.at[i, j])
                if wait:
                    copy.wait()
                else:
                    copy.start()


def prefix_scores_kernel(
    q_ref, prefix_ref, suffix_ref, query_ref, scores_ref, peak_ref, vals_ref, suf_keys_ref, qbuf, keys, rowbuf, sem, sem_keys
):
    rows = q_ref.shape[0]
    tokens, head_dim = keys.shape
    heads = q_ref.shape[1] // head_dim
    parts = sem_keys.shape[0]
    size = tokens // parts
    key_copies = [
        pltpu.make_async_copy(
            prefix_ref.at[0, 0, pl.ds(j * size, size)], keys.at[pl.ds(j * size, size)], sem_keys.at[j]
        )
        for j in range(parts)
    ]
    fetch_q = pltpu.make_async_copy(q_ref, qbuf, sem.at[0])
    fetch = [
        pltpu.make_async_copy(suffix_ref.at[:, 0, 0], suf_keys_ref, sem.at[1]),
        pltpu.make_async_copy(prefix_ref.at[0, 1], vals_ref, sem.at[2]),
    ]
    for c in [fetch_q] + key_copies + fetch:
        c.start()
    fetch_q.wait()
    for h in range(heads):
        rowbuf[pl.ds(h, rows, stride=heads), :] = qbuf[:, h * head_dim : (h + 1) * head_dim].astype(F32)
    query = rowbuf[...].astype(BF16)
    query_ref[...] = query
    best = jnp.full(peak_ref.shape, -3.0e38, F32)
    step = min(512, size)
    for j in range(parts):
        key_copies[j].wait()
        for base in range(j * size, (j + 1) * size, step):
            block = nt_dot(keys[base : base + step, :], query)
            scores_ref[base : base + step, :] = block
            best = jnp.maximum(best, jnp.max(block.reshape(step // 8, 8, block.shape[1]), axis=0))
    peak_ref[...] = best
    for c in fetch:
        c.wait()


def weight_copies(weight_ref, outs, spots, sem):
    me = lax.axis_index("tensor")
    z, y = me // 2, me % 2
    copies = []
    for i, (side, k) in enumerate(spots):
        width = outs[i].shape[1]
        column = pl.multiple_of(((z ^ k) * 2 + (y ^ side)) * width, width)
        copies.append(pltpu.make_async_copy(weight_ref.at[:, pl.ds(column, width)], outs[i], sem.at[i]))
    return copies


def suffix_scores_kernel(spots, ids_ref, slot_ref, query_ref, suf_keys_ref, vals_ref, peak_ref, *rest):
    len_ref, suffix_ref, pages_ref, weight_ref = rest[:4]
    tail_ref, high_ref, high_row_ref, vals_t_ref, out_pages_ref, suf_vals_ref = rest[4:10]
    w_refs = rest[10 : 10 + len(spots)]
    lens, seen, list_id, list_pos, sem, sem_page, sem_w = rest[10 + len(spots) :]
    rows, span, head_dim = suf_keys_ref.shape
    tokens = vals_ref.shape[0]
    heads = query_ref.shape[0] // rows
    fetch_len = pltpu.make_async_copy(len_ref, lens, sem.at[1])
    fetch_len.start()
    fetch = [pltpu.make_async_copy(suffix_ref.at[:, 0, 1], suf_vals_ref, sem.at[0])]
    fetch += weight_copies(weight_ref, w_refs, spots, sem_w)
    distinct_list(ids_ref, slot_ref, seen, list_id, list_pos)
    outs = (out_pages_ref.at[0], out_pages_ref.at[1])
    page_copies(pages_ref, outs, list_pos, sem_page, False)
    for c in fetch:
        c.start()
    query = query_ref[...]
    lanes = lax.broadcasted_iota(jnp.int32, (heads, span), 1)
    fetch_len.wait()
    for i in range(rows // 2):
        keys = suf_keys_ref[2 * i : 2 * i + 2].reshape(2 * span, head_dim)
        both = nt_dot(query[2 * heads * i : 2 * heads * (i + 1)], keys)
        for a in range(2):
            mine = both[a * heads : (a + 1) * heads, a * span : (a + 1) * span]
            row = 2 * i + a
            tail_ref[row * heads : (row + 1) * heads, :] = jnp.where(lanes < lens[row], mine, -1.0e30)
    vals_t_ref[head_dim:, :] = jnp.ones((vals_t_ref.shape[0] - head_dim, tokens), BF16)
    step = min(1024, tokens)
    for base in range(0, tokens, step):
        vals_t_ref[:head_dim, base : base + step] = vals_ref[base : base + step, :].T
    best = jnp.maximum(tail_ref[:, :128], tail_ref[:, 128:256])
    for b in range(2, span // 128):
        best = jnp.maximum(best, tail_ref[:, b * 128 : (b + 1) * 128])
    across_rows = jnp.broadcast_to(jnp.max(peak_ref[...], axis=0, keepdims=True), (128, peak_ref.shape[1]))
    high = jnp.maximum(across_rows.T, jnp.max(best, axis=1, keepdims=True))
    high_ref[...] = high
    high_row_ref[...] = high.T[:8]
    page_copies(pages_ref, outs, list_pos, sem_page, True)
    for c in fetch:
        c.wait()


def values_kernel(spots, ids_ref, slot_ref, scores, tail, peak, peak_row, vals_t_ref, suf_vals_ref, *rest):
    pages_ref, weight_ref, residual_ref = rest[:3]
    att_ref, shrink_ref, expand_ref, row_slot_ref, slot_mine_ref, res_ref = rest[3:9]
    w_refs = rest[9 : 9 + len(spots)]
    rowbuf, total, acc, acc_t, seen, list_id, list_pos, sem, sem_page, sem_w = rest[9 + len(spots) :]
    rows, span, head_dim = suf_vals_ref.shape
    tokens = vals_t_ref.shape[1]
    heads = att_ref.shape[1] // head_dim
    width = res_ref.shape[1]
    me = lax.axis_index("tensor")
    scale2 = float(head_dim) ** -0.5 * LOG2E
    fetch = weight_copies(weight_ref, w_refs, spots, sem_w)
    fetch.append(
        pltpu.make_async_copy(
            residual_ref.at[:, pl.ds(pl.multiple_of(me * width, width), width)], res_ref, sem.at[0]
        )
    )
    for c in fetch:
        c.start()
    distinct_list(ids_ref, slot_ref, seen, list_id, list_pos)
    page_copies(pages_ref, (shrink_ref, expand_ref), list_pos, sem_page, False)
    row_index = lax.broadcasted_iota(jnp.int32, (rows, 128), 0)
    row_id = jnp.full((rows, 128), -2, jnp.int32)
    for r in range(rows):
        row_id = jnp.where(row_index == r, ids_ref[r], row_id)
    row_slot = jnp.full((rows, 128), -1, jnp.int32)
    slot_index = lax.broadcasted_iota(jnp.int32, (DISTINCT, 128), 0)
    slot_mine = jnp.zeros((DISTINCT, 128), jnp.int32)
    mine = lax.axis_index("req")
    for j in range(DISTINCT):
        row_slot = jnp.where(row_id == list_id[j], j, row_slot)
        owned = (list_pos[j] // pages_ref.shape[0] == mine).astype(jnp.int32)
        slot_mine = jnp.where(slot_index == j, owned, slot_mine)
    row_slot_ref[...] = row_slot
    slot_mine_ref[...] = slot_mine

    acc_t[...] = jnp.zeros(acc_t.shape, F32)
    n_q = acc_t.shape[1]
    chunk = min(2048, tokens)

    @pl.loop(0, tokens // chunk)
    def _(i):
        base = pl.multiple_of(i * chunk, chunk)
        high_row = peak_row[...]
        block = scores[pl.ds(base, chunk), :].reshape(chunk // 8, 8, n_q)
        e = jnp.exp2((block - high_row[None]) * scale2)
        weights = e.reshape(chunk, n_q).astype(BF16)
        acc_t[...] += nn_dot(vals_t_ref[:, pl.ds(base, chunk)], weights)

    across_rows = jnp.broadcast_to(acc_t[head_dim : head_dim + 1, :], (128, n_q))
    acc[...] = acc_t[:head_dim, :].T
    zeros = jnp.zeros((heads, span), F32)
    for i in range(rows // 2):
        lo = 2 * heads * i
        high = jnp.concatenate([peak[lo : lo + 2 * heads, :]] * (span // 128), axis=1)
        e = jnp.exp2((tail[lo : lo + 2 * heads, :] - high) * scale2)
        part_sum = e[:, :128]
        for b in range(1, span // 128):
            part_sum = part_sum + e[:, b * 128 : (b + 1) * 128]
        total[lo : lo + 2 * heads, :] = part_sum
        diag = jnp.concatenate(
            [
                jnp.concatenate([e[:heads], zeros], axis=1),
                jnp.concatenate([zeros, e[heads:]], axis=1),
            ],
            axis=0,
        ).astype(BF16)
        vals = suf_vals_ref[2 * i : 2 * i + 2].reshape(2 * span, head_dim)
        acc[lo : lo + 2 * heads, :] += nn_dot(diag, vals)

    norm = across_rows.T + jnp.sum(total[...], axis=1, keepdims=True)
    rowbuf[...] = acc[...] / norm
    for h in range(heads):
        att_ref[:, h * head_dim : (h + 1) * head_dim] = rowbuf[pl.ds(h, rows, stride=heads), :].astype(BF16)
    page_copies(pages_ref, (shrink_ref, expand_ref), list_pos, sem_page, True)
    for c in fetch:
        c.wait()


def kernel_call(kernel, name, out_shape, specs, scratch, operands, mib, flops, bytes_accessed):
    return pl.pallas_call(
        kernel,
        out_shape=out_shape,
        in_specs=specs,
        out_specs=[VMEM] * len(out_shape),
        scratch_shapes=scratch,
        compiler_params=params(mib),
        cost_estimate=pl.CostEstimate(flops=flops, bytes_accessed=bytes_accessed, transcendentals=0),
        name=name,
    )(*operands)


def attend(
    suffix_len, ids, other_ids, pool_slot, queries, prefix_kv, suffix_kv, out_weight, pages, residual, n_tensor, across
):
    rows = queries.shape[0]
    n_z = n_tensor // 2
    in_rows = out_weight.shape[0]
    width = out_weight.shape[1] // n_tensor
    tokens, head_dim = prefix_kv.shape[2:]
    n_q = rows * queries.shape[1] // head_dim
    span = suffix_kv.shape[3]
    prefix_kv, suffix_kv, out_weight = in_hbm(prefix_kv), in_hbm(suffix_kv), in_hbm(out_weight)
    pages, residual = in_hbm(pages), in_hbm(residual)
    query, scores, peak, vals, suf_keys = kernel_call(
        prefix_scores_kernel,
        "prefix_scores",
        [
            pltpu.VMEM((n_q, head_dim), BF16),
            pltpu.VMEM((tokens, n_q), F32),
            pltpu.VMEM((8, n_q), F32),
            pltpu.VMEM((tokens, head_dim), BF16),
            pltpu.VMEM((rows, span, head_dim), BF16),
        ],
        [ANY, ANY, ANY],
        [
            pltpu.VMEM(queries.shape, BF16),
            pltpu.VMEM((tokens, head_dim), BF16),
            pltpu.VMEM((n_q, head_dim), F32),
            pltpu.SemaphoreType.DMA((3,)),
            pltpu.SemaphoreType.DMA((4,)),
        ],
        [in_hbm(queries), prefix_kv, suffix_kv],
        8,
        2 * n_q * tokens * head_dim,
        6 * MIB,
    )
    far = list(range(n_z - 1, -1, -1))
    early = [(0, k) for k in far[: n_z // 4]]
    late = [(1, k) for k in far if k > 1] + [(0, k) for k in far[n_z // 4 :] if k > 1]
    tail, high, high_row, vals_t, out_pages, suf_vals, *early_w = kernel_call(
        functools.partial(suffix_scores_kernel, early),
        "suffix_scores",
        [
            pltpu.VMEM((n_q, span), F32),
            pltpu.VMEM((n_q, 128), F32),
            pltpu.VMEM((8, n_q), F32),
            pltpu.VMEM((head_dim + 16, tokens), BF16),
            pltpu.VMEM((2, DISTINCT) + pages.shape[2:], BF16),
            pltpu.VMEM((rows, span, head_dim), BF16),
        ]
        + [pltpu.VMEM((in_rows, width), BF16)] * len(early),
        [SMEM, SMEM, VMEM, VMEM, VMEM, VMEM, ANY, ANY, ANY, ANY],
        [pltpu.SMEM((rows,), jnp.int32)]
        + list_scratch(pool_slot)
        + [
            pltpu.SemaphoreType.DMA((2,)),
            pltpu.SemaphoreType.DMA((2, DISTINCT)),
            pltpu.SemaphoreType.DMA((len(early),)),
        ],
        [other_ids, pool_slot, query, suf_keys, vals, peak, in_hbm(suffix_len), suffix_kv, pages, out_weight],
        8,
        1 << 29,
        7 * MIB,
    )
    other_pages = across(out_pages)
    attended, own_shrink, own_expand, row_slot, slot_mine, res, *late_w = kernel_call(
        functools.partial(values_kernel, late),
        "values",
        [
            pltpu.VMEM(queries.shape, BF16),
            pltpu.VMEM((DISTINCT,) + pages.shape[2:], BF16),
            pltpu.VMEM((DISTINCT,) + pages.shape[2:], BF16),
            pltpu.VMEM((rows, 128), jnp.int32),
            pltpu.VMEM((DISTINCT, 128), jnp.int32),
            pltpu.VMEM((rows, width), BF16),
        ]
        + [pltpu.VMEM((in_rows, width), BF16)] * len(late),
        [SMEM, SMEM, VMEM, VMEM, VMEM, VMEM, VMEM, VMEM, ANY, ANY, ANY],
        [
            pltpu.VMEM((n_q, head_dim), F32),
            pltpu.VMEM((n_q, 128), F32),
            pltpu.VMEM((n_q, head_dim), F32),
            pltpu.VMEM((head_dim + 16, n_q), F32),
        ]
        + list_scratch(pool_slot)
        + [
            pltpu.SemaphoreType.DMA((2,)),
            pltpu.SemaphoreType.DMA((2, DISTINCT)),
            pltpu.SemaphoreType.DMA((len(late),)),
        ],
        [ids, pool_slot, scores, tail, high, high_row, vals_t, suf_vals, pages, out_weight, residual],
        8,
        2 * n_q * tokens * head_dim,
        14 * MIB,
    )
    weights = dict(zip(early + late, list(early_w) + list(late_w)))
    return attended, own_shrink, own_expand, other_pages, row_slot, slot_mine, res, weights


def small_call(kernel, name, out_shape, operands, flops=1 << 27):
    return pl.pallas_call(
        kernel,
        out_shape=out_shape,
        in_specs=[VMEM] * len(operands),
        out_specs=jax.tree.map(lambda _: VMEM, out_shape),
        compiler_params=params(8),
        cost_estimate=pl.CostEstimate(flops=flops, bytes_accessed=2 * MIB, transcendentals=0),
        name=name,
    )(*operands)


def merged(own_ref, other, half, slot_mine):
    rank = own_ref.shape[1]
    tiles = []
    for j in range(DISTINCT):
        hit = jnp.broadcast_to(slot_mine[j : j + 1, :1], (rank, 1)) == 1
        tiles.append(jnp.where(hit, own_ref[j].astype(F32), other[half, j].astype(F32)).astype(BF16))
    return jnp.concatenate(tiles, axis=0)


def lane_place(shape, rank):
    return lax.broadcasted_iota(jnp.int32, shape, 1) // rank


def far_kernel(n, att_ref, row_slot_ref, slot_mine_ref, own_ref, other_ref, *rest):
    w_refs = rest[:n]
    out_ref, rank_ref = rest[n:]
    width = w_refs[0].shape[1]
    attended = att_ref[...]
    for k in range(n):
        out_ref[:, k * width : (k + 1) * width] = nn_dot(attended, w_refs[k][...]).astype(BF16)
    rank = own_ref.shape[1]
    per_tile = 128 // rank
    low = nt_dot(attended, merged(own_ref, other_ref, 0, slot_mine_ref[...]))
    row_slot = row_slot_ref[...]
    place = lane_place(row_slot.shape, rank)
    picked = jnp.zeros(row_slot.shape, F32)
    for tile in range(DISTINCT // per_tile):
        hit = row_slot == place + tile * per_tile
        picked = jnp.where(hit, low[:, tile * 128 : (tile + 1) * 128], picked)
    rank_ref[...] = picked
    out_ref[:, n * width :] = picked.astype(BF16)


def near_kernel(spots, att_ref, rank_ref, weight_ref, *rest):
    outs, (wbuf, sem) = rest[: len(spots)], rest[len(spots) :]
    width = wbuf.shape[2]
    copies = weight_copies(weight_ref, [wbuf.at[i] for i in range(len(spots))], spots, sem)
    for c in copies:
        c.start()
    attended = att_ref[...]
    rank = rank_ref[...].astype(BF16)
    for i, out in enumerate(outs):
        copies[i].wait()
        out[:, :width] = nn_dot(attended, wbuf[i]).astype(BF16)
        if out.shape[1] > width:
            out[:, width:] = rank


def near_blocks(spots, columns, attended, rank_own, weight, after, n_tensor):
    rows = attended.shape[0]
    width = weight.shape[1] // n_tensor

    def kernel(att_ref, rank_ref, weight_ref, *rest):
        near_kernel(spots, att_ref, rank_ref, weight_ref, *rest[len(after) :])

    return kernel_call(
        kernel,
        "near_blocks",
        [pltpu.VMEM((rows, columns), BF16)] * len(spots),
        [VMEM, VMEM, ANY] + [VMEM] * len(after),
        [pltpu.VMEM((len(spots), weight.shape[0], width), BF16), pltpu.SemaphoreType.DMA((len(spots),))],
        [attended, rank_own, in_hbm(weight)] + after,
        8,
        1 << 27,
        2 * len(spots) * MIB,
    )


def own_kernel(
    att_ref, res_ref, slot_mine_ref, own_ref, other_ref, weight_ref, after_ref, out_ref, pages_ref, wbuf, sem
):
    (copy,) = weight_copies(weight_ref, [wbuf], [(0, 0)], sem)
    copy.start()
    pages_ref[...] = merged(own_ref, other_ref, 1, slot_mine_ref[...])
    copy.wait()
    out_ref[...] = nn_dot(att_ref[...], wbuf[...]) + res_ref[...].astype(F32)


def own_block(attended, res, slot_mine, own_pages, other_pages, weight, after):
    rows, width = res.shape
    return kernel_call(
        own_kernel,
        "own_block",
        [pltpu.VMEM((rows, width), F32), pltpu.VMEM((DISTINCT * own_pages.shape[1], width), BF16)],
        [VMEM, VMEM, VMEM, VMEM, VMEM, ANY, VMEM],
        [pltpu.VMEM((weight.shape[0], width), BF16), pltpu.SemaphoreType.DMA((1,))],
        [attended, res, slot_mine, own_pages, other_pages, in_hbm(weight), after],
        8,
        0,
        2 * MIB,
    )


def add_kernel(spot, att_ref, w_ref, from_ref, rank_ref, *rest):
    out_ref = rest[-1]
    width = w_ref.shape[1]
    both = nn_dot(att_ref[...], w_ref[...]) + from_ref[:, spot * width : (spot + 1) * width].astype(F32)
    out_ref[:, :width] = both.astype(BF16)
    rank_both = rank_ref[...] + from_ref[:, from_ref.shape[1] - 128 :].astype(F32)
    out_ref[:, width:] = rank_both.astype(BF16)


def finish_kernel(*refs):
    own_ref, pages_ref, row_slot_ref, rank_ref, far_ref, from_ref = refs[:6]
    moved, out_ref = refs[6:-1], refs[-1]
    rank = pages_ref.shape[0] // DISTINCT
    per_tile = 128 // rank
    width = own_ref.shape[1]
    low = rank_ref[...] + far_ref[:, far_ref.shape[1] - 128 :].astype(F32)
    for ref in moved:
        low = low + ref[:, width:].astype(F32)
    row_slot = row_slot_ref[...]
    place = lane_place(row_slot.shape, rank)
    tiles = []
    for tile in range(DISTINCT // per_tile):
        tiles.append(jnp.where(row_slot == place + tile * per_tile, low, 0.0).astype(BF16))
    total = nn_dot(jnp.concatenate(tiles, axis=1), pages_ref[...])
    total = total + (own_ref[...] + from_ref[...].astype(F32))
    for ref in moved:
        total = total + ref[:, :width].astype(F32)
    out_ref[...] = total.astype(BF16)


def place_kernel(spots, *refs):
    blocks = refs[: len(spots)]
    out_ref, sem = refs[-2:]
    width = blocks[0].shape[1]
    me = lax.axis_index("tensor")
    z, y = me // 2, me % 2
    copies = []
    for i, (k, side) in enumerate(spots):
        column = pl.multiple_of(((z ^ k) * 2 + (y ^ side)) * width, width)
        copies.append(pltpu.make_async_copy(blocks[i], out_ref.at[:, pl.ds(column, width)], sem.at[i]))
    for c in copies:
        c.start()
    for c in copies:
        c.wait()


def place(blocks, spots, n_tensor, held=None):
    rows, width = blocks[0].shape
    extra = [] if held is None else [held]
    return pl.pallas_call(
        functools.partial(place_kernel, spots),
        out_shape=pltpu.HBM((rows, width * n_tensor), BF16),
        in_specs=[VMEM] * len(blocks) + [ANY] * len(extra),
        out_specs=ANY,
        scratch_shapes=[pltpu.SemaphoreType.DMA((len(blocks),))],
        input_output_aliases={len(blocks): 0} if extra else {},
        compiler_params=params(4),
        cost_estimate=pl.CostEstimate(flops=0, bytes_accessed=1 * MIB, transcendentals=0),
        name="place",
    )(*blocks, *extra)


def body(
    n_tensor,
    queries,
    prefix_kv,
    suffix_kv,
    suffix_len,
    residual,
    out_weight,
    adapter_pages,
    adapter_ids,
    pool_slot,
):
    n_z = n_tensor // 2

    def along_y(x):
        return lax.ppermute(x, "tensor", [(t, t ^ 1) for t in range(n_tensor)])

    def along_z(x, k):
        return lax.ppermute(x, "tensor", [(t, t ^ (2 * k)) for t in range(n_tensor)])

    def along_both(x, k):
        return lax.ppermute(x, "tensor", [(t, t ^ (2 * k) ^ 1) for t in range(n_tensor)])

    def across(x):
        return lax.ppermute(x, "req", [(0, 1), (1, 0)])

    rows = queries.shape[0]
    width = out_weight.shape[1] // n_tensor
    attended, own_shrink, own_expand, other_pages, row_slot, slot_mine, res, weights = attend(
        suffix_len,
        adapter_ids,
        across(adapter_ids),
        pool_slot,
        queries,
        prefix_kv,
        suffix_kv,
        out_weight,
        adapter_pages,
        residual,
        n_tensor,
        across,
    )
    far = list(range(n_z - 1, 1, -1))
    piece_shape = pltpu.VMEM((rows, width + 128), BF16)
    far_out, rank_own = small_call(
        functools.partial(far_kernel, len(far)),
        "far_blocks",
        [pltpu.VMEM((rows, len(far) * width + 128), BF16), pltpu.VMEM((rows, 128), F32)],
        [attended, row_slot, slot_mine, own_shrink, other_pages] + [weights[1, k] for k in far],
    )
    from_far = along_y(far_out)
    straight, cross = near_blocks(
        [(0, 1), (1, 1)], width + 128, attended, rank_own, out_weight, [], n_tensor
    )
    moved = [along_z(straight, 1), along_both(cross, 1)]
    after = []
    for spot, k in enumerate(far):
        piece = small_call(
            functools.partial(add_kernel, spot),
            "add_block",
            piece_shape,
            [attended, weights[0, k], from_far, rank_own] + after,
        )
        moved.append(along_z(piece, k))
        after = [piece]
    (own_far,) = near_blocks([(1, 0)], width, attended, rank_own, out_weight, [piece], n_tensor)
    from_own = along_y(own_far)
    own, expand_pages = own_block(attended, res, slot_mine, own_expand, other_pages, out_weight, own_far)
    result = small_call(
        finish_kernel,
        "finish",
        pltpu.VMEM((rows, width), BF16),
        [own, expand_pages, row_slot, rank_own, from_far, from_own] + moved,
    )
    held = [result] + [along_z(result, k) for k in range(1, n_z)]
    crossed = [along_both(result, k) if k < 2 else along_y(held[k]) for k in range(n_z)]
    spots = [(0, 0), (1, 1), (1, 0)] + [(k, side) for k in range(2, n_z) for side in (0, 1)]
    spots.insert(len(spots) - 2, (0, 1))
    forwarded = [(k, side) for k, side in spots if k and side]
    placed = None
    for group in ([p for p in spots if p not in forwarded], forwarded):
        placed = place([(crossed if side else held)[k] for k, side in group], group, n_tensor, placed)
    return placed


def solution(mesh):
    return jax.shard_map(
        functools.partial(body, mesh.shape["tensor"]),
        mesh=mesh,
        in_specs=(
            P(("group", "req"), "tensor"),
            P(("group", "tensor"), None, None, None),
            P(("group", "req"), "tensor", None, None, None),
            P(("group", "req")),
            P(("group", "req"), None),
            P("tensor", None),
            P("req", None, None, "tensor"),
            P(("group", "req")),
            P(),
        ),
        out_specs=P(("group", "req"), None),
        check_vma=False,
    )
```

```python
import functools

import jax
import jax.numpy as jnp
from jax import lax
from jax.experimental import pallas as pl
from jax.experimental.pallas import tpu as pltpu
from jax.sharding import PartitionSpec as P

F32 = jnp.float32
BF16 = jnp.bfloat16
LOG2E = 1.4426950408889634
ANY = pl.BlockSpec(memory_space=pl.ANY)
VMEM = pl.BlockSpec(memory_space=pltpu.VMEM)
SMEM = pl.BlockSpec(memory_space=pltpu.SMEM)
MIB = 1 << 20
DISTINCT = 8


def in_hbm(x):
    return pltpu.with_memory_space_constraint(x, pltpu.HBM)


def params(mib):
    return pltpu.CompilerParams(vmem_limit_bytes=mib * MIB)


def nt_dot(a, b):
    return lax.dot_general(a, b, (((1,), (1,)), ((), ())), preferred_element_type=F32)


def nn_dot(a, b):
    return jnp.dot(a, b, preferred_element_type=F32)


def distinct_list(ids_ref, pool_slot_ref, seen, list_id, list_pos):
    rows = ids_ref.shape[0]
    for i in range(pool_slot_ref.shape[0]):
        seen[i] = 0
    for j in range(DISTINCT + 1):
        list_id[j] = -1
        list_pos[j] = 0
    found = jnp.int32(0)
    for r in range(rows):
        one = ids_ref[r]
        fresh = 1 - seen[one]
        seen[one] = 1
        spot = jnp.minimum(found, DISTINCT)
        list_id[spot] = jnp.where(fresh == 1, one, list_id[spot])
        list_pos[spot] = jnp.where(fresh == 1, pool_slot_ref[one], list_pos[spot])
        found = found + fresh


def list_scratch(pool_slot):
    return [
        pltpu.SMEM((pool_slot.shape[0],), jnp.int32),
        pltpu.SMEM((DISTINCT + 1,), jnp.int32),
        pltpu.SMEM((DISTINCT + 1,), jnp.int32),
    ]


def page_copies(pages_ref, outs, list_pos, sem, wait):
    pool = pages_ref.shape[0]
    me = lax.axis_index("req")
    for j in range(DISTINCT):
        pos = list_pos[j]

        @pl.when(pos // pool == me)
        def _():
            for i, out in enumerate(outs):
                copy = pltpu.make_async_copy(pages_ref.at[pos % pool, i], out.at[j], sem.at[i, j])
                if wait:
                    copy.wait()
                else:
                    copy.start()


def prefix_scores_kernel(
    q_ref,
    prefix_ref,
    suffix_ref,
    weight_ref,
    query_ref,
    scores_ref,
    peak_ref,
    vals_ref,
    suf_keys_ref,
    w_ref,
    qbuf,
    keys,
    rowbuf,
    sem,
    sem_keys,
    sem_w,
):
    rows = q_ref.shape[0]
    tokens, head_dim = keys.shape
    heads = q_ref.shape[1] // head_dim
    parts = sem_keys.shape[0]
    size = tokens // parts
    key_copies = [
        pltpu.make_async_copy(
            prefix_ref.at[0, 0, pl.ds(j * size, size)], keys.at[pl.ds(j * size, size)], sem_keys.at[j]
        )
        for j in range(parts)
    ]
    fetch_q = pltpu.make_async_copy(q_ref, qbuf, sem.at[0])
    fetch = [
        pltpu.make_async_copy(suffix_ref.at[:, 0, 0], suf_keys_ref, sem.at[1]),
        pltpu.make_async_copy(prefix_ref.at[0, 1], vals_ref, sem.at[2]),
    ] + weight_copies(weight_ref, [w_ref], [(1, 0)], sem_w)
    for c in [fetch_q] + key_copies + fetch:
        c.start()
    fetch_q.wait()
    for h in range(heads):
        rowbuf[pl.ds(h, rows, stride=heads), :] = qbuf[:, h * head_dim : (h + 1) * head_dim].astype(F32)
    query = rowbuf[...].astype(BF16)
    query_ref[...] = query
    best = jnp.full(peak_ref.shape, -3.0e38, F32)
    step = min(512, size)
    for j in range(parts):
        key_copies[j].wait()
        for base in range(j * size, (j + 1) * size, step):
            block = nt_dot(keys[base : base + step, :], query)
            scores_ref[base : base + step, :] = block
            best = jnp.maximum(best, jnp.max(block.reshape(step // 8, 8, block.shape[1]), axis=0))
    peak_ref[...] = best
    for c in fetch:
        c.wait()


def weight_copies(weight_ref, outs, spots, sem):
    me = lax.axis_index("tensor")
    z, y = me // 2, me % 2
    copies = []
    for i, (side, k) in enumerate(spots):
        width = outs[i].shape[1]
        column = pl.multiple_of(((z ^ k) * 2 + (y ^ side)) * width, width)
        copies.append(pltpu.make_async_copy(weight_ref.at[:, pl.ds(column, width)], outs[i], sem.at[i]))
    return copies


def suffix_scores_kernel(spots, ids_ref, slot_ref, query_ref, suf_keys_ref, vals_ref, peak_ref, *rest):
    len_ref, suffix_ref, pages_ref, weight_ref = rest[:4]
    tail_ref, high_ref, high_row_ref, vals_t_ref, out_pages_ref, suf_vals_ref = rest[4:10]
    w_refs = rest[10 : 10 + len(spots)]
    lens, seen, list_id, list_pos, sem, sem_page, sem_w = rest[10 + len(spots) :]
    rows, span, head_dim = suf_keys_ref.shape
    tokens = vals_ref.shape[0]
    heads = query_ref.shape[0] // rows
    fetch_len = pltpu.make_async_copy(len_ref, lens, sem.at[1])
    fetch_len.start()
    fetch = [pltpu.make_async_copy(suffix_ref.at[:, 0, 1], suf_vals_ref, sem.at[0])]
    fetch += weight_copies(weight_ref, w_refs, spots, sem_w)
    distinct_list(ids_ref, slot_ref, seen, list_id, list_pos)
    outs = (out_pages_ref.at[0], out_pages_ref.at[1])
    page_copies(pages_ref, outs, list_pos, sem_page, False)
    for c in fetch:
        c.start()
    query = query_ref[...]
    lanes = lax.broadcasted_iota(jnp.int32, (heads, span), 1)
    fetch_len.wait()
    for i in range(rows // 2):
        keys = suf_keys_ref[2 * i : 2 * i + 2].reshape(2 * span, head_dim)
        both = nt_dot(query[2 * heads * i : 2 * heads * (i + 1)], keys)
        for a in range(2):
            mine = both[a * heads : (a + 1) * heads, a * span : (a + 1) * span]
            row = 2 * i + a
            tail_ref[row * heads : (row + 1) * heads, :] = jnp.where(lanes < lens[row], mine, -1.0e30)
    vals_t_ref[head_dim:, :] = jnp.ones((vals_t_ref.shape[0] - head_dim, tokens), BF16)
    step = min(1024, tokens)
    for base in range(0, tokens, step):
        vals_t_ref[:head_dim, base : base + step] = vals_ref[base : base + step, :].astype(F32).T.astype(BF16)
    best = jnp.maximum(tail_ref[:, :128], tail_ref[:, 128:256])
    for b in range(2, span // 128):
        best = jnp.maximum(best, tail_ref[:, b * 128 : (b + 1) * 128])
    across_rows = jnp.broadcast_to(jnp.max(peak_ref[...], axis=0, keepdims=True), (128, peak_ref.shape[1]))
    high = jnp.maximum(across_rows.T, jnp.max(best, axis=1, keepdims=True))
    high_ref[...] = high
    high_row_ref[...] = high.T[:8]
    page_copies(pages_ref, outs, list_pos, sem_page, True)
    for c in fetch:
        c.wait()


def values_kernel(spots, ids_ref, slot_ref, scores, tail, peak, peak_row, vals_t_ref, suf_vals_ref, *rest):
    pages_ref, weight_ref, residual_ref = rest[:3]
    att_ref, shrink_ref, expand_ref, row_slot_ref, slot_mine_ref, res_ref = rest[3:9]
    w_refs = rest[9 : 9 + len(spots)]
    rowbuf, total, acc, acc_t, seen, list_id, list_pos, sem, sem_page, sem_w = rest[9 + len(spots) :]
    rows, span, head_dim = suf_vals_ref.shape
    tokens = vals_t_ref.shape[1]
    heads = att_ref.shape[1] // head_dim
    width = res_ref.shape[1]
    me = lax.axis_index("tensor")
    scale2 = float(head_dim) ** -0.5 * LOG2E
    fetch = weight_copies(weight_ref, w_refs, spots, sem_w)
    fetch.append(
        pltpu.make_async_copy(
            residual_ref.at[:, pl.ds(pl.multiple_of(me * width, width), width)], res_ref, sem.at[0]
        )
    )
    for c in fetch:
        c.start()
    distinct_list(ids_ref, slot_ref, seen, list_id, list_pos)
    page_copies(pages_ref, (shrink_ref, expand_ref), list_pos, sem_page, False)
    row_index = lax.broadcasted_iota(jnp.int32, (rows, 128), 0)
    row_id = jnp.full((rows, 128), -2, jnp.int32)
    for r in range(rows):
        row_id = jnp.where(row_index == r, ids_ref[r], row_id)
    row_slot = jnp.full((rows, 128), -1, jnp.int32)
    slot_index = lax.broadcasted_iota(jnp.int32, (DISTINCT, 128), 0)
    slot_mine = jnp.zeros((DISTINCT, 128), jnp.int32)
    mine = lax.axis_index("req")
    for j in range(DISTINCT):
        row_slot = jnp.where(row_id == list_id[j], j, row_slot)
        owned = (list_pos[j] // pages_ref.shape[0] == mine).astype(jnp.int32)
        slot_mine = jnp.where(slot_index == j, owned, slot_mine)
    row_slot_ref[...] = row_slot
    slot_mine_ref[...] = slot_mine

    acc_t[...] = jnp.zeros(acc_t.shape, F32)
    n_q = acc_t.shape[1]
    chunk = min(2048, tokens)

    @pl.loop(0, tokens // chunk)
    def _(i):
        base = pl.multiple_of(i * chunk, chunk)
        high_row = peak_row[...]
        block = scores[pl.ds(base, chunk), :].reshape(chunk // 8, 8, n_q)
        e = jnp.exp2((block - high_row[None]) * scale2)
        weights = e.reshape(chunk, n_q).astype(BF16)
        acc_t[...] += nn_dot(vals_t_ref[:, pl.ds(base, chunk)], weights)

    across_rows = jnp.broadcast_to(acc_t[head_dim : head_dim + 1, :], (128, n_q))
    acc[...] = acc_t[:head_dim, :].T
    zeros = jnp.zeros((heads, span), F32)
    for i in range(rows // 2):
        lo = 2 * heads * i
        high = jnp.concatenate([peak[lo : lo + 2 * heads, :]] * (span // 128), axis=1)
        e = jnp.exp2((tail[lo : lo + 2 * heads, :] - high) * scale2)
        part_sum = e[:, :128]
        for b in range(1, span // 128):
            part_sum = part_sum + e[:, b * 128 : (b + 1) * 128]
        total[lo : lo + 2 * heads, :] = part_sum
        diag = jnp.concatenate(
            [
                jnp.concatenate([e[:heads], zeros], axis=1),
                jnp.concatenate([zeros, e[heads:]], axis=1),
            ],
            axis=0,
        ).astype(BF16)
        vals = suf_vals_ref[2 * i : 2 * i + 2].reshape(2 * span, head_dim)
        acc[lo : lo + 2 * heads, :] += nn_dot(diag, vals)

    norm = across_rows.T + jnp.sum(total[...], axis=1, keepdims=True)
    rowbuf[...] = acc[...] / norm
    for h in range(heads):
        att_ref[:, h * head_dim : (h + 1) * head_dim] = rowbuf[pl.ds(h, rows, stride=heads), :].astype(BF16)
    page_copies(pages_ref, (shrink_ref, expand_ref), list_pos, sem_page, True)
    for c in fetch:
        c.wait()


def kernel_call(kernel, name, out_shape, specs, scratch, operands, mib, flops, bytes_accessed):
    return pl.pallas_call(
        kernel,
        out_shape=out_shape,
        in_specs=specs,
        out_specs=[VMEM] * len(out_shape),
        scratch_shapes=scratch,
        compiler_params=params(mib),
        cost_estimate=pl.CostEstimate(flops=flops, bytes_accessed=bytes_accessed, transcendentals=0),
        name=name,
    )(*operands)


def attend(
    suffix_len, ids, other_ids, pool_slot, queries, prefix_kv, suffix_kv, out_weight, pages, residual, n_tensor, across
):
    rows = queries.shape[0]
    n_z = n_tensor // 2
    in_rows = out_weight.shape[0]
    width = out_weight.shape[1] // n_tensor
    tokens, head_dim = prefix_kv.shape[2:]
    n_q = rows * queries.shape[1] // head_dim
    span = suffix_kv.shape[3]
    prefix_kv, suffix_kv, out_weight = in_hbm(prefix_kv), in_hbm(suffix_kv), in_hbm(out_weight)
    pages, residual = in_hbm(pages), in_hbm(residual)
    query, scores, peak, vals, suf_keys, own_far_w = kernel_call(
        prefix_scores_kernel,
        "prefix_scores",
        [
            pltpu.VMEM((n_q, head_dim), BF16),
            pltpu.VMEM((tokens, n_q), F32),
            pltpu.VMEM((8, n_q), F32),
            pltpu.VMEM((tokens, head_dim), BF16),
            pltpu.VMEM((rows, span, head_dim), BF16),
            pltpu.VMEM((in_rows, width), BF16),
        ],
        [ANY, ANY, ANY, ANY],
        [
            pltpu.VMEM(queries.shape, BF16),
            pltpu.VMEM((tokens, head_dim), BF16),
            pltpu.VMEM((n_q, head_dim), F32),
            pltpu.SemaphoreType.DMA((3,)),
            pltpu.SemaphoreType.DMA((4,)),
            pltpu.SemaphoreType.DMA((1,)),
        ],
        [in_hbm(queries), prefix_kv, suffix_kv, out_weight],
        8,
        2 * n_q * tokens * head_dim,
        6 * MIB,
    )
    far = list(range(n_z - 1, -1, -1))
    early = [(0, k) for k in far[: n_z // 4]]
    late = [(1, k) for k in far if k > 1] + [(0, k) for k in far[n_z // 4 :] if k > 1]
    tail, high, high_row, vals_t, out_pages, suf_vals, *early_w = kernel_call(
        functools.partial(suffix_scores_kernel, early),
        "suffix_scores",
        [
            pltpu.VMEM((n_q, span), F32),
            pltpu.VMEM((n_q, 128), F32),
            pltpu.VMEM((8, n_q), F32),
            pltpu.VMEM((head_dim + 16, tokens), BF16),
            pltpu.VMEM((2, DISTINCT) + pages.shape[2:], BF16),
            pltpu.VMEM((rows, span, head_dim), BF16),
        ]
        + [pltpu.VMEM((in_rows, width), BF16)] * len(early),
        [SMEM, SMEM, VMEM, VMEM, VMEM, VMEM, ANY, ANY, ANY, ANY],
        [pltpu.SMEM((rows,), jnp.int32)]
        + list_scratch(pool_slot)
        + [
            pltpu.SemaphoreType.DMA((2,)),
            pltpu.SemaphoreType.DMA((2, DISTINCT)),
            pltpu.SemaphoreType.DMA((len(early),)),
        ],
        [other_ids, pool_slot, query, suf_keys, vals, peak, in_hbm(suffix_len), suffix_kv, pages, out_weight],
        8,
        1 << 29,
        7 * MIB,
    )
    other_pages = across(out_pages)
    attended, own_shrink, own_expand, row_slot, slot_mine, res, *late_w = kernel_call(
        functools.partial(values_kernel, late),
        "values",
        [
            pltpu.VMEM(queries.shape, BF16),
            pltpu.VMEM((DISTINCT,) + pages.shape[2:], BF16),
            pltpu.VMEM((DISTINCT,) + pages.shape[2:], BF16),
            pltpu.VMEM((rows, 128), jnp.int32),
            pltpu.VMEM((DISTINCT, 128), jnp.int32),
            pltpu.VMEM((rows, width), BF16),
        ]
        + [pltpu.VMEM((in_rows, width), BF16)] * len(late),
        [SMEM, SMEM, VMEM, VMEM, VMEM, VMEM, VMEM, VMEM, ANY, ANY, ANY],
        [
            pltpu.VMEM((n_q, head_dim), F32),
            pltpu.VMEM((n_q, 128), F32),
            pltpu.VMEM((n_q, head_dim), F32),
            pltpu.VMEM((head_dim + 16, n_q), F32),
        ]
        + list_scratch(pool_slot)
        + [
            pltpu.SemaphoreType.DMA((2,)),
            pltpu.SemaphoreType.DMA((2, DISTINCT)),
            pltpu.SemaphoreType.DMA((len(late),)),
        ],
        [ids, pool_slot, scores, tail, high, high_row, vals_t, suf_vals, pages, out_weight, residual],
        8,
        2 * n_q * tokens * head_dim,
        14 * MIB,
    )
    weights = dict(zip(early + late, list(early_w) + list(late_w)))
    weights[1, 0] = own_far_w
    return attended, own_shrink, own_expand, other_pages, row_slot, slot_mine, res, weights


def small_call(kernel, name, out_shape, operands, flops=1 << 27):
    return pl.pallas_call(
        kernel,
        out_shape=out_shape,
        in_specs=[VMEM] * len(operands),
        out_specs=jax.tree.map(lambda _: VMEM, out_shape),
        compiler_params=params(8),
        cost_estimate=pl.CostEstimate(flops=flops, bytes_accessed=2 * MIB, transcendentals=0),
        name=name,
    )(*operands)


def merged(own_ref, other, half, slot_mine):
    rank = own_ref.shape[1]
    tiles = []
    for j in range(DISTINCT):
        hit = jnp.broadcast_to(slot_mine[j : j + 1, :1], (rank, 1)) == 1
        tiles.append(jnp.where(hit, own_ref[j].astype(F32), other[half, j].astype(F32)).astype(BF16))
    return jnp.concatenate(tiles, axis=0)


def lane_place(shape, rank):
    return lax.broadcasted_iota(jnp.int32, shape, 1) // rank


def far_kernel(n, att_ref, row_slot_ref, slot_mine_ref, own_ref, other_ref, *rest):
    w_refs = rest[:n]
    out_ref, rank_ref = rest[n:]
    width = w_refs[0].shape[1]
    attended = att_ref[...]
    for k in range(n):
        out_ref[:, k * width : (k + 1) * width] = nn_dot(attended, w_refs[k][...]).astype(BF16)
    rank = own_ref.shape[1]
    per_tile = 128 // rank
    low = nt_dot(attended, merged(own_ref, other_ref, 0, slot_mine_ref[...]))
    row_slot = row_slot_ref[...]
    place = lane_place(row_slot.shape, rank)
    picked = jnp.zeros(row_slot.shape, F32)
    for tile in range(DISTINCT // per_tile):
        hit = row_slot == place + tile * per_tile
        picked = jnp.where(hit, low[:, tile * 128 : (tile + 1) * 128], picked)
    rank_ref[...] = picked
    out_ref[:, n * width :] = picked.astype(BF16)


def block_kernel(att_ref, w_ref, after_ref, out_ref):
    out_ref[...] = nn_dot(att_ref[...], w_ref[...]).astype(BF16)


def near_kernel(spots, att_ref, rank_ref, weight_ref, *rest):
    outs, (wbuf, sem) = rest[: len(spots)], rest[len(spots) :]
    width = wbuf.shape[2]
    copies = weight_copies(weight_ref, [wbuf.at[i] for i in range(len(spots))], spots, sem)
    for c in copies:
        c.start()
    attended = att_ref[...]
    rank = rank_ref[...].astype(BF16)
    for i, out in enumerate(outs):
        copies[i].wait()
        out[:, :width] = nn_dot(attended, wbuf[i]).astype(BF16)
        if out.shape[1] > width:
            out[:, width:] = rank


def near_blocks(spots, columns, attended, rank_own, weight, after, n_tensor):
    rows = attended.shape[0]
    width = weight.shape[1] // n_tensor

    def kernel(att_ref, rank_ref, weight_ref, *rest):
        near_kernel(spots, att_ref, rank_ref, weight_ref, *rest[len(after) :])

    return kernel_call(
        kernel,
        "near_blocks",
        [pltpu.VMEM((rows, columns), BF16)] * len(spots),
        [VMEM, VMEM, ANY] + [VMEM] * len(after),
        [pltpu.VMEM((len(spots), weight.shape[0], width), BF16), pltpu.SemaphoreType.DMA((len(spots),))],
        [attended, rank_own, in_hbm(weight)] + after,
        8,
        1 << 27,
        2 * len(spots) * MIB,
    )


def own_kernel(
    att_ref, res_ref, slot_mine_ref, own_ref, other_ref, weight_ref, after_ref, out_ref, pages_ref, wbuf, sem
):
    (copy,) = weight_copies(weight_ref, [wbuf], [(0, 0)], sem)
    copy.start()
    pages_ref[...] = merged(own_ref, other_ref, 1, slot_mine_ref[...])
    copy.wait()
    out_ref[...] = nn_dot(att_ref[...], wbuf[...]) + res_ref[...].astype(F32)


def own_block(attended, res, slot_mine, own_pages, other_pages, weight, after):
    rows, width = res.shape
    return kernel_call(
        own_kernel,
        "own_block",
        [pltpu.VMEM((rows, width), F32), pltpu.VMEM((DISTINCT * own_pages.shape[1], width), BF16)],
        [VMEM, VMEM, VMEM, VMEM, VMEM, ANY, VMEM],
        [pltpu.VMEM((weight.shape[0], width), BF16), pltpu.SemaphoreType.DMA((1,))],
        [attended, res, slot_mine, own_pages, other_pages, in_hbm(weight), after],
        8,
        0,
        2 * MIB,
    )


def add_kernel(spot, att_ref, w_ref, from_ref, rank_ref, *rest):
    out_ref = rest[-1]
    width = w_ref.shape[1]
    both = nn_dot(att_ref[...], w_ref[...]) + from_ref[:, spot * width : (spot + 1) * width].astype(F32)
    out_ref[:, :width] = both.astype(BF16)
    rank_both = rank_ref[...] + from_ref[:, from_ref.shape[1] - 128 :].astype(F32)
    out_ref[:, width:] = rank_both.astype(BF16)


def finish_kernel(*refs):
    own_ref, pages_ref, row_slot_ref, rank_ref, far_ref, from_ref = refs[:6]
    moved, out_ref = refs[6:-1], refs[-1]
    rank = pages_ref.shape[0] // DISTINCT
    per_tile = 128 // rank
    width = own_ref.shape[1]
    low = rank_ref[...] + far_ref[:, far_ref.shape[1] - 128 :].astype(F32)
    for ref in moved:
        low = low + ref[:, width:].astype(F32)
    row_slot = row_slot_ref[...]
    place = lane_place(row_slot.shape, rank)
    tiles = []
    for tile in range(DISTINCT // per_tile):
        tiles.append(jnp.where(row_slot == place + tile * per_tile, low, 0.0).astype(BF16))
    total = nn_dot(jnp.concatenate(tiles, axis=1), pages_ref[...])
    total = total + (own_ref[...] + from_ref[...].astype(F32))
    for ref in moved:
        total = total + ref[:, :width].astype(F32)
    out_ref[...] = total.astype(BF16)


def place_kernel(spots, *refs):
    blocks = refs[: len(spots)]
    out_ref, sem = refs[-2:]
    width = blocks[0].shape[1]
    me = lax.axis_index("tensor")
    z, y = me // 2, me % 2
    copies = []
    for i, (k, side) in enumerate(spots):
        column = pl.multiple_of(((z ^ k) * 2 + (y ^ side)) * width, width)
        copies.append(pltpu.make_async_copy(blocks[i], out_ref.at[:, pl.ds(column, width)], sem.at[i]))
    for c in copies:
        c.start()
    for c in copies:
        c.wait()


def place(blocks, spots, n_tensor, held=None):
    rows, width = blocks[0].shape
    extra = [] if held is None else [held]
    return pl.pallas_call(
        functools.partial(place_kernel, spots),
        out_shape=pltpu.HBM((rows, width * n_tensor), BF16),
        in_specs=[VMEM] * len(blocks) + [ANY] * len(extra),
        out_specs=ANY,
        scratch_shapes=[pltpu.SemaphoreType.DMA((len(blocks),))],
        input_output_aliases={len(blocks): 0} if extra else {},
        compiler_params=params(4),
        cost_estimate=pl.CostEstimate(flops=0, bytes_accessed=1 * MIB, transcendentals=0),
        name="place",
    )(*blocks, *extra)


def body(
    n_tensor,
    queries,
    prefix_kv,
    suffix_kv,
    suffix_len,
    residual,
    out_weight,
    adapter_pages,
    adapter_ids,
    pool_slot,
):
    n_z = n_tensor // 2

    def along_y(x):
        return lax.ppermute(x, "tensor", [(t, t ^ 1) for t in range(n_tensor)])

    def along_z(x, k):
        return lax.ppermute(x, "tensor", [(t, t ^ (2 * k)) for t in range(n_tensor)])

    def along_both(x, k):
        return lax.ppermute(x, "tensor", [(t, t ^ (2 * k) ^ 1) for t in range(n_tensor)])

    def across(x):
        return lax.ppermute(x, "req", [(0, 1), (1, 0)])

    rows = queries.shape[0]
    width = out_weight.shape[1] // n_tensor
    attended, own_shrink, own_expand, other_pages, row_slot, slot_mine, res, weights = attend(
        suffix_len,
        adapter_ids,
        across(adapter_ids),
        pool_slot,
        queries,
        prefix_kv,
        suffix_kv,
        out_weight,
        adapter_pages,
        residual,
        n_tensor,
        across,
    )
    far = list(range(n_z - 1, 1, -1))
    piece_shape = pltpu.VMEM((rows, width + 128), BF16)
    far_out, rank_own = small_call(
        functools.partial(far_kernel, len(far)),
        "far_blocks",
        [pltpu.VMEM((rows, len(far) * width + 128), BF16), pltpu.VMEM((rows, 128), F32)],
        [attended, row_slot, slot_mine, own_shrink, other_pages] + [weights[1, k] for k in far],
    )
    from_far = along_y(far_out)
    straight, cross = near_blocks(
        [(0, 1), (1, 1)], width + 128, attended, rank_own, out_weight, [], n_tensor
    )
    moved = [along_z(straight, 1), along_both(cross, 1)]
    after = []
    for spot, k in enumerate(far):
        piece = small_call(
            functools.partial(add_kernel, spot),
            "add_block",
            piece_shape,
            [attended, weights[0, k], from_far, rank_own] + after,
        )
        moved.append(along_z(piece, k))
        after = [piece]
    own_far = small_call(
        block_kernel, "own_far_block", pltpu.VMEM((rows, width), BF16), [attended, weights[1, 0], piece]
    )
    from_own = along_y(own_far)
    own, expand_pages = own_block(attended, res, slot_mine, own_expand, other_pages, out_weight, own_far)
    result = small_call(
        finish_kernel,
        "finish",
        pltpu.VMEM((rows, width), BF16),
        [own, expand_pages, row_slot, rank_own, from_far, from_own] + moved,
    )
    held = [result] + [along_z(result, k) for k in range(1, n_z)]
    crossed = [along_both(result, k) if k < 2 else along_y(held[k]) for k in range(n_z)]
    spots = [(0, 0), (1, 1), (1, 0)] + [(k, side) for k in range(2, n_z) for side in (0, 1)]
    spots.insert(len(spots) - 2, (0, 1))
    forwarded = [(k, side) for k, side in spots if k and side]
    placed = None
    for group in ([p for p in spots if p not in forwarded], forwarded):
        placed = place([(crossed if side else held)[k] for k, side in group], group, n_tensor, placed)
    return placed


def solution(mesh):
    return jax.shard_map(
        functools.partial(body, mesh.shape["tensor"]),
        mesh=mesh,
        in_specs=(
            P(("group", "req"), "tensor"),
            P(("group", "tensor"), None, None, None),
            P(("group", "req"), "tensor", None, None, None),
            P(("group", "req")),
            P(("group", "req"), None),
            P("tensor", None),
            P("req", None, None, "tensor"),
            P(("group", "req")),
            P(),
        ),
        out_specs=P(("group", "req"), None),
        check_vma=False,
    )
```

```python
import functools

import jax
import jax.numpy as jnp
from jax import lax
from jax.experimental import pallas as pl
from jax.experimental.pallas import tpu as pltpu
from jax.sharding import PartitionSpec as P

F32 = jnp.float32
BF16 = jnp.bfloat16
LOG2E = 1.4426950408889634
ANY = pl.BlockSpec(memory_space=pl.ANY)
VMEM = pl.BlockSpec(memory_space=pltpu.VMEM)
SMEM = pl.BlockSpec(memory_space=pltpu.SMEM)
MIB = 1 << 20
DISTINCT = 8


def in_hbm(x):
    return pltpu.with_memory_space_constraint(x, pltpu.HBM)


def params(mib):
    return pltpu.CompilerParams(vmem_limit_bytes=mib * MIB)


def nt_dot(a, b):
    return lax.dot_general(a, b, (((1,), (1,)), ((), ())), preferred_element_type=F32)


def nn_dot(a, b):
    return jnp.dot(a, b, preferred_element_type=F32)


def distinct_list(ids_ref, pool_slot_ref, seen, list_id, list_pos):
    rows = ids_ref.shape[0]
    for i in range(pool_slot_ref.shape[0]):
        seen[i] = 0
    for j in range(DISTINCT + 1):
        list_id[j] = -1
        list_pos[j] = 0
    found = jnp.int32(0)
    for r in range(rows):
        one = ids_ref[r]
        fresh = 1 - seen[one]
        seen[one] = 1
        spot = jnp.minimum(found, DISTINCT)
        list_id[spot] = jnp.where(fresh == 1, one, list_id[spot])
        list_pos[spot] = jnp.where(fresh == 1, pool_slot_ref[one], list_pos[spot])
        found = found + fresh


def list_scratch(pool_slot):
    return [
        pltpu.SMEM((pool_slot.shape[0],), jnp.int32),
        pltpu.SMEM((DISTINCT + 1,), jnp.int32),
        pltpu.SMEM((DISTINCT + 1,), jnp.int32),
    ]


def page_copies(pages_ref, outs, list_pos, sem, wait):
    pool = pages_ref.shape[0]
    me = lax.axis_index("req")
    for j in range(DISTINCT):
        pos = list_pos[j]

        @pl.when(pos // pool == me)
        def _():
            for i, out in enumerate(outs):
                copy = pltpu.make_async_copy(pages_ref.at[pos % pool, i], out.at[j], sem.at[i, j])
                if wait:
                    copy.wait()
                else:
                    copy.start()


def prefix_scores_kernel(
    q_ref, prefix_ref, suffix_ref, query_ref, scores_ref, peak_ref, vals_ref, suf_keys_ref, qbuf, keys, rowbuf, sem, sem_keys
):
    rows = q_ref.shape[0]
    tokens, head_dim = keys.shape
    heads = q_ref.shape[1] // head_dim
    parts = sem_keys.shape[0]
    size = tokens // parts
    key_copies = [
        pltpu.make_async_copy(
            prefix_ref.at[0, 0, pl.ds(j * size, size)], keys.at[pl.ds(j * size, size)], sem_keys.at[j]
        )
        for j in range(parts)
    ]
    fetch_q = pltpu.make_async_copy(q_ref, qbuf, sem.at[0])
    fetch = [
        pltpu.make_async_copy(suffix_ref.at[:, 0, 0], suf_keys_ref, sem.at[1]),
        pltpu.make_async_copy(prefix_ref.at[0, 1], vals_ref, sem.at[2]),
    ]
    for c in [fetch_q] + key_copies + fetch:
        c.start()
    fetch_q.wait()
    for h in range(heads):
        rowbuf[pl.ds(h, rows, stride=heads), :] = qbuf[:, h * head_dim : (h + 1) * head_dim].astype(F32)
    query = rowbuf[...].astype(BF16)
    query_ref[...] = query
    best = jnp.full(peak_ref.shape, -3.0e38, F32)
    step = min(512, size)
    for j in range(parts):
        key_copies[j].wait()
        for base in range(j * size, (j + 1) * size, step):
            block = nt_dot(keys[base : base + step, :], query)
            scores_ref[base : base + step, :] = block
            best = jnp.maximum(best, jnp.max(block.reshape(step // 8, 8, block.shape[1]), axis=0))
    peak_ref[...] = best
    for c in fetch:
        c.wait()


def weight_copies(weight_ref, outs, spots, sem):
    me = lax.axis_index("tensor")
    z, y = me // 2, me % 2
    copies = []
    for i, (side, k) in enumerate(spots):
        width = outs[i].shape[1]
        column = pl.multiple_of(((z ^ k) * 2 + (y ^ side)) * width, width)
        copies.append(pltpu.make_async_copy(weight_ref.at[:, pl.ds(column, width)], outs[i], sem.at[i]))
    return copies


def suffix_scores_kernel(spots, ids_ref, slot_ref, query_ref, suf_keys_ref, vals_ref, peak_ref, *rest):
    len_ref, suffix_ref, pages_ref, weight_ref = rest[:4]
    tail_ref, high_ref, high_row_ref, vals_t_ref, out_pages_ref, suf_vals_ref = rest[4:10]
    w_refs = rest[10 : 10 + len(spots)]
    lens, seen, list_id, list_pos, sem, sem_page, sem_w = rest[10 + len(spots) :]
    rows, span, head_dim = suf_keys_ref.shape
    tokens = vals_ref.shape[0]
    heads = query_ref.shape[0] // rows
    fetch_len = pltpu.make_async_copy(len_ref, lens, sem.at[1])
    fetch_len.start()
    fetch = [pltpu.make_async_copy(suffix_ref.at[:, 0, 1], suf_vals_ref, sem.at[0])]
    fetch += weight_copies(weight_ref, w_refs, spots, sem_w)
    distinct_list(ids_ref, slot_ref, seen, list_id, list_pos)
    outs = (out_pages_ref.at[0], out_pages_ref.at[1])
    page_copies(pages_ref, outs, list_pos, sem_page, False)
    for c in fetch:
        c.start()
    query = query_ref[...]
    lanes = lax.broadcasted_iota(jnp.int32, (heads, span), 1)
    fetch_len.wait()
    for i in range(rows // 2):
        keys = suf_keys_ref[2 * i : 2 * i + 2].reshape(2 * span, head_dim)
        both = nt_dot(query[2 * heads * i : 2 * heads * (i + 1)], keys)
        for a in range(2):
            mine = both[a * heads : (a + 1) * heads, a * span : (a + 1) * span]
            row = 2 * i + a
            tail_ref[row * heads : (row + 1) * heads, :] = jnp.where(lanes < lens[row], mine, -1.0e30)
    vals_t_ref[head_dim:, :] = jnp.ones((vals_t_ref.shape[0] - head_dim, tokens), BF16)
    step = min(1024, tokens)
    for base in range(0, tokens, step):
        vals_t_ref[:head_dim, base : base + step] = vals_ref[base : base + step, :].astype(F32).T.astype(BF16)
    best = jnp.maximum(tail_ref[:, :128], tail_ref[:, 128:256])
    for b in range(2, span // 128):
        best = jnp.maximum(best, tail_ref[:, b * 128 : (b + 1) * 128])
    across_rows = jnp.broadcast_to(jnp.max(peak_ref[...], axis=0, keepdims=True), (128, peak_ref.shape[1]))
    high = jnp.maximum(across_rows.T, jnp.max(best, axis=1, keepdims=True))
    high_ref[...] = high
    high_row_ref[...] = high.T[:8]
    page_copies(pages_ref, outs, list_pos, sem_page, True)
    for c in fetch:
        c.wait()


def values_kernel(spots, ids_ref, slot_ref, scores, tail, peak, peak_row, vals_t_ref, suf_vals_ref, *rest):
    pages_ref, weight_ref, residual_ref = rest[:3]
    att_ref, shrink_ref, expand_ref, row_slot_ref, slot_mine_ref, res_ref = rest[3:9]
    w_refs = rest[9 : 9 + len(spots)]
    rowbuf, total, acc, acc_t, seen, list_id, list_pos, sem, sem_page, sem_w = rest[9 + len(spots) :]
    rows, span, head_dim = suf_vals_ref.shape
    tokens = vals_t_ref.shape[1]
    heads = att_ref.shape[1] // head_dim
    width = res_ref.shape[1]
    me = lax.axis_index("tensor")
    scale2 = float(head_dim) ** -0.5 * LOG2E
    fetch = weight_copies(weight_ref, w_refs, spots, sem_w)
    fetch.append(
        pltpu.make_async_copy(
            residual_ref.at[:, pl.ds(pl.multiple_of(me * width, width), width)], res_ref, sem.at[0]
        )
    )
    for c in fetch:
        c.start()
    distinct_list(ids_ref, slot_ref, seen, list_id, list_pos)
    page_copies(pages_ref, (shrink_ref, expand_ref), list_pos, sem_page, False)
    row_index = lax.broadcasted_iota(jnp.int32, (rows, 128), 0)
    row_id = jnp.full((rows, 128), -2, jnp.int32)
    for r in range(rows):
        row_id = jnp.where(row_index == r, ids_ref[r], row_id)
    row_slot = jnp.full((rows, 128), -1, jnp.int32)
    slot_index = lax.broadcasted_iota(jnp.int32, (DISTINCT, 128), 0)
    slot_mine = jnp.zeros((DISTINCT, 128), jnp.int32)
    mine = lax.axis_index("req")
    for j in range(DISTINCT):
        row_slot = jnp.where(row_id == list_id[j], j, row_slot)
        owned = (list_pos[j] // pages_ref.shape[0] == mine).astype(jnp.int32)
        slot_mine = jnp.where(slot_index == j, owned, slot_mine)
    row_slot_ref[...] = row_slot
    slot_mine_ref[...] = slot_mine

    acc_t[...] = jnp.zeros(acc_t.shape, F32)
    n_q = acc_t.shape[1]
    chunk = min(4096, tokens)

    @pl.loop(0, tokens // chunk)
    def _(i):
        base = pl.multiple_of(i * chunk, chunk)
        high_row = peak_row[...]
        block = scores[pl.ds(base, chunk), :].reshape(chunk // 8, 8, n_q)
        e = jnp.exp2((block - high_row[None]) * scale2)
        weights = e.reshape(chunk, n_q).astype(BF16)
        acc_t[...] += nn_dot(vals_t_ref[:, pl.ds(base, chunk)], weights)

    across_rows = jnp.broadcast_to(acc_t[head_dim : head_dim + 1, :], (128, n_q))
    acc[...] = acc_t[:head_dim, :].T
    zeros = jnp.zeros((heads, span), F32)
    for i in range(rows // 2):
        lo = 2 * heads * i
        high = jnp.concatenate([peak[lo : lo + 2 * heads, :]] * (span // 128), axis=1)
        e = jnp.exp2((tail[lo : lo + 2 * heads, :] - high) * scale2)
        part_sum = e[:, :128]
        for b in range(1, span // 128):
            part_sum = part_sum + e[:, b * 128 : (b + 1) * 128]
        total[lo : lo + 2 * heads, :] = part_sum
        diag = jnp.concatenate(
            [
                jnp.concatenate([e[:heads], zeros], axis=1),
                jnp.concatenate([zeros, e[heads:]], axis=1),
            ],
            axis=0,
        ).astype(BF16)
        vals = suf_vals_ref[2 * i : 2 * i + 2].reshape(2 * span, head_dim)
        acc[lo : lo + 2 * heads, :] += nn_dot(diag, vals)

    norm = across_rows.T + jnp.sum(total[...], axis=1, keepdims=True)
    rowbuf[...] = acc[...] / norm
    for h in range(heads):
        att_ref[:, h * head_dim : (h + 1) * head_dim] = rowbuf[pl.ds(h, rows, stride=heads), :].astype(BF16)
    page_copies(pages_ref, (shrink_ref, expand_ref), list_pos, sem_page, True)
    for c in fetch:
        c.wait()


def kernel_call(kernel, name, out_shape, specs, scratch, operands, mib, flops, bytes_accessed):
    return pl.pallas_call(
        kernel,
        out_shape=out_shape,
        in_specs=specs,
        out_specs=[VMEM] * len(out_shape),
        scratch_shapes=scratch,
        compiler_params=params(mib),
        cost_estimate=pl.CostEstimate(flops=flops, bytes_accessed=bytes_accessed, transcendentals=0),
        name=name,
    )(*operands)


def attend(
    suffix_len, ids, other_ids, pool_slot, queries, prefix_kv, suffix_kv, out_weight, pages, residual, n_tensor, across
):
    rows = queries.shape[0]
    n_z = n_tensor // 2
    in_rows = out_weight.shape[0]
    width = out_weight.shape[1] // n_tensor
    tokens, head_dim = prefix_kv.shape[2:]
    n_q = rows * queries.shape[1] // head_dim
    span = suffix_kv.shape[3]
    prefix_kv, suffix_kv, out_weight = in_hbm(prefix_kv), in_hbm(suffix_kv), in_hbm(out_weight)
    pages, residual = in_hbm(pages), in_hbm(residual)
    query, scores, peak, vals, suf_keys = kernel_call(
        prefix_scores_kernel,
        "prefix_scores",
        [
            pltpu.VMEM((n_q, head_dim), BF16),
            pltpu.VMEM((tokens, n_q), F32),
            pltpu.VMEM((8, n_q), F32),
            pltpu.VMEM((tokens, head_dim), BF16),
            pltpu.VMEM((rows, span, head_dim), BF16),
        ],
        [ANY, ANY, ANY],
        [
            pltpu.VMEM(queries.shape, BF16),
            pltpu.VMEM((tokens, head_dim), BF16),
            pltpu.VMEM((n_q, head_dim), F32),
            pltpu.SemaphoreType.DMA((3,)),
            pltpu.SemaphoreType.DMA((4,)),
        ],
        [in_hbm(queries), prefix_kv, suffix_kv],
        8,
        2 * n_q * tokens * head_dim,
        6 * MIB,
    )
    far = list(range(n_z - 1, -1, -1))
    early = [(0, k) for k in far[: n_z // 4]]
    late = [(1, k) for k in far if k > 1] + [(0, k) for k in far[n_z // 4 :] if k > 1]
    tail, high, high_row, vals_t, out_pages, suf_vals, *early_w = kernel_call(
        functools.partial(suffix_scores_kernel, early),
        "suffix_scores",
        [
            pltpu.VMEM((n_q, span), F32),
            pltpu.VMEM((n_q, 128), F32),
            pltpu.VMEM((8, n_q), F32),
            pltpu.VMEM((head_dim + 16, tokens), BF16),
            pltpu.VMEM((2, DISTINCT) + pages.shape[2:], BF16),
            pltpu.VMEM((rows, span, head_dim), BF16),
        ]
        + [pltpu.VMEM((in_rows, width), BF16)] * len(early),
        [SMEM, SMEM, VMEM, VMEM, VMEM, VMEM, ANY, ANY, ANY, ANY],
        [pltpu.SMEM((rows,), jnp.int32)]
        + list_scratch(pool_slot)
        + [
            pltpu.SemaphoreType.DMA((2,)),
            pltpu.SemaphoreType.DMA((2, DISTINCT)),
            pltpu.SemaphoreType.DMA((len(early),)),
        ],
        [other_ids, pool_slot, query, suf_keys, vals, peak, in_hbm(suffix_len), suffix_kv, pages, out_weight],
        8,
        1 << 29,
        7 * MIB,
    )
    other_pages = across(out_pages)
    attended, own_shrink, own_expand, row_slot, slot_mine, res, *late_w = kernel_call(
        functools.partial(values_kernel, late),
        "values",
        [
            pltpu.VMEM(queries.shape, BF16),
            pltpu.VMEM((DISTINCT,) + pages.shape[2:], BF16),
            pltpu.VMEM((DISTINCT,) + pages.shape[2:], BF16),
            pltpu.VMEM((rows, 128), jnp.int32),
            pltpu.VMEM((DISTINCT, 128), jnp.int32),
            pltpu.VMEM((rows, width), BF16),
        ]
        + [pltpu.VMEM((in_rows, width), BF16)] * len(late),
        [SMEM, SMEM, VMEM, VMEM, VMEM, VMEM, VMEM, VMEM, ANY, ANY, ANY],
        [
            pltpu.VMEM((n_q, head_dim), F32),
            pltpu.VMEM((n_q, 128), F32),
            pltpu.VMEM((n_q, head_dim), F32),
            pltpu.VMEM((head_dim + 16, n_q), F32),
        ]
        + list_scratch(pool_slot)
        + [
            pltpu.SemaphoreType.DMA((2,)),
            pltpu.SemaphoreType.DMA((2, DISTINCT)),
            pltpu.SemaphoreType.DMA((len(late),)),
        ],
        [ids, pool_slot, scores, tail, high, high_row, vals_t, suf_vals, pages, out_weight, residual],
        8,
        2 * n_q * tokens * head_dim,
        14 * MIB,
    )
    weights = dict(zip(early + late, list(early_w) + list(late_w)))
    return attended, own_shrink, own_expand, other_pages, row_slot, slot_mine, res, weights


def small_call(kernel, name, out_shape, operands, flops=1 << 27):
    return pl.pallas_call(
        kernel,
        out_shape=out_shape,
        in_specs=[VMEM] * len(operands),
        out_specs=jax.tree.map(lambda _: VMEM, out_shape),
        compiler_params=params(8),
        cost_estimate=pl.CostEstimate(flops=flops, bytes_accessed=2 * MIB, transcendentals=0),
        name=name,
    )(*operands)


def merged(own_ref, other, half, slot_mine):
    rank = own_ref.shape[1]
    tiles = []
    for j in range(DISTINCT):
        hit = jnp.broadcast_to(slot_mine[j : j + 1, :1], (rank, 1)) == 1
        tiles.append(jnp.where(hit, own_ref[j].astype(F32), other[half, j].astype(F32)).astype(BF16))
    return jnp.concatenate(tiles, axis=0)


def lane_place(shape, rank):
    return lax.broadcasted_iota(jnp.int32, shape, 1) // rank


def far_kernel(n, att_ref, row_slot_ref, slot_mine_ref, own_ref, other_ref, *rest):
    w_refs = rest[:n]
    out_ref, rank_ref = rest[n:]
    width = w_refs[0].shape[1]
    attended = att_ref[...]
    for k in range(n):
        out_ref[:, k * width : (k + 1) * width] = nn_dot(attended, w_refs[k][...]).astype(BF16)
    rank = own_ref.shape[1]
    per_tile = 128 // rank
    low = nt_dot(attended, merged(own_ref, other_ref, 0, slot_mine_ref[...]))
    row_slot = row_slot_ref[...]
    place = lane_place(row_slot.shape, rank)
    picked = jnp.zeros(row_slot.shape, F32)
    for tile in range(DISTINCT // per_tile):
        hit = row_slot == place + tile * per_tile
        picked = jnp.where(hit, low[:, tile * 128 : (tile + 1) * 128], picked)
    rank_ref[...] = picked
    out_ref[:, n * width :] = picked.astype(BF16)


def near_kernel(spots, att_ref, rank_ref, weight_ref, *rest):
    outs, (wbuf, sem) = rest[: len(spots)], rest[len(spots) :]
    width = wbuf.shape[2]
    copies = weight_copies(weight_ref, [wbuf.at[i] for i in range(len(spots))], spots, sem)
    for c in copies:
        c.start()
    attended = att_ref[...]
    rank = rank_ref[...].astype(BF16)
    for i, out in enumerate(outs):
        copies[i].wait()
        out[:, :width] = nn_dot(attended, wbuf[i]).astype(BF16)
        if out.shape[1] > width:
            out[:, width:] = rank


def near_blocks(spots, columns, attended, rank_own, weight, after, n_tensor):
    rows = attended.shape[0]
    width = weight.shape[1] // n_tensor

    def kernel(att_ref, rank_ref, weight_ref, *rest):
        near_kernel(spots, att_ref, rank_ref, weight_ref, *rest[len(after) :])

    return kernel_call(
        kernel,
        "near_blocks",
        [pltpu.VMEM((rows, columns), BF16)] * len(spots),
        [VMEM, VMEM, ANY] + [VMEM] * len(after),
        [pltpu.VMEM((len(spots), weight.shape[0], width), BF16), pltpu.SemaphoreType.DMA((len(spots),))],
        [attended, rank_own, in_hbm(weight)] + after,
        8,
        1 << 27,
        2 * len(spots) * MIB,
    )


def own_kernel(
    att_ref, res_ref, slot_mine_ref, own_ref, other_ref, weight_ref, after_ref, out_ref, pages_ref, wbuf, sem
):
    (copy,) = weight_copies(weight_ref, [wbuf], [(0, 0)], sem)
    copy.start()
    pages_ref[...] = merged(own_ref, other_ref, 1, slot_mine_ref[...])
    copy.wait()
    out_ref[...] = nn_dot(att_ref[...], wbuf[...]) + res_ref[...].astype(F32)


def own_block(attended, res, slot_mine, own_pages, other_pages, weight, after):
    rows, width = res.shape
    return kernel_call(
        own_kernel,
        "own_block",
        [pltpu.VMEM((rows, width), F32), pltpu.VMEM((DISTINCT * own_pages.shape[1], width), BF16)],
        [VMEM, VMEM, VMEM, VMEM, VMEM, ANY, VMEM],
        [pltpu.VMEM((weight.shape[0], width), BF16), pltpu.SemaphoreType.DMA((1,))],
        [attended, res, slot_mine, own_pages, other_pages, in_hbm(weight), after],
        8,
        0,
        2 * MIB,
    )


def add_kernel(spot, att_ref, w_ref, from_ref, rank_ref, *rest):
    out_ref = rest[-1]
    width = w_ref.shape[1]
    both = nn_dot(att_ref[...], w_ref[...]) + from_ref[:, spot * width : (spot + 1) * width].astype(F32)
    out_ref[:, :width] = both.astype(BF16)
    rank_both = rank_ref[...] + from_ref[:, from_ref.shape[1] - 128 :].astype(F32)
    out_ref[:, width:] = rank_both.astype(BF16)


def finish_kernel(*refs):
    own_ref, pages_ref, row_slot_ref, rank_ref, far_ref, from_ref = refs[:6]
    moved, out_ref = refs[6:-1], refs[-1]
    rank = pages_ref.shape[0] // DISTINCT
    per_tile = 128 // rank
    width = own_ref.shape[1]
    low = rank_ref[...] + far_ref[:, far_ref.shape[1] - 128 :].astype(F32)
    for ref in moved:
        low = low + ref[:, width:].astype(F32)
    row_slot = row_slot_ref[...]
    place = lane_place(row_slot.shape, rank)
    tiles = []
    for tile in range(DISTINCT // per_tile):
        tiles.append(jnp.where(row_slot == place + tile * per_tile, low, 0.0).astype(BF16))
    total = nn_dot(jnp.concatenate(tiles, axis=1), pages_ref[...])
    total = total + (own_ref[...] + from_ref[...].astype(F32))
    for ref in moved:
        total = total + ref[:, :width].astype(F32)
    out_ref[...] = total.astype(BF16)


def place_kernel(spots, *refs):
    blocks = refs[: len(spots)]
    out_ref, sem = refs[-2:]
    width = blocks[0].shape[1]
    me = lax.axis_index("tensor")
    z, y = me // 2, me % 2
    copies = []
    for i, (k, side) in enumerate(spots):
        column = pl.multiple_of(((z ^ k) * 2 + (y ^ side)) * width, width)
        copies.append(pltpu.make_async_copy(blocks[i], out_ref.at[:, pl.ds(column, width)], sem.at[i]))
    for c in copies:
        c.start()
    for c in copies:
        c.wait()


def place(blocks, spots, n_tensor, held=None):
    rows, width = blocks[0].shape
    extra = [] if held is None else [held]
    return pl.pallas_call(
        functools.partial(place_kernel, spots),
        out_shape=pltpu.HBM((rows, width * n_tensor), BF16),
        in_specs=[VMEM] * len(blocks) + [ANY] * len(extra),
        out_specs=ANY,
        scratch_shapes=[pltpu.SemaphoreType.DMA((len(blocks),))],
        input_output_aliases={len(blocks): 0} if extra else {},
        compiler_params=params(4),
        cost_estimate=pl.CostEstimate(flops=0, bytes_accessed=1 * MIB, transcendentals=0),
        name="place",
    )(*blocks, *extra)


def body(
    n_tensor,
    queries,
    prefix_kv,
    suffix_kv,
    suffix_len,
    residual,
    out_weight,
    adapter_pages,
    adapter_ids,
    pool_slot,
):
    n_z = n_tensor // 2

    def along_y(x):
        return lax.ppermute(x, "tensor", [(t, t ^ 1) for t in range(n_tensor)])

    def along_z(x, k):
        return lax.ppermute(x, "tensor", [(t, t ^ (2 * k)) for t in range(n_tensor)])

    def along_both(x, k):
        return lax.ppermute(x, "tensor", [(t, t ^ (2 * k) ^ 1) for t in range(n_tensor)])

    def across(x):
        return lax.ppermute(x, "req", [(0, 1), (1, 0)])

    rows = queries.shape[0]
    width = out_weight.shape[1] // n_tensor
    attended, own_shrink, own_expand, other_pages, row_slot, slot_mine, res, weights = attend(
        suffix_len,
        adapter_ids,
        across(adapter_ids),
        pool_slot,
        queries,
        prefix_kv,
        suffix_kv,
        out_weight,
        adapter_pages,
        residual,
        n_tensor,
        across,
    )
    far = list(range(n_z - 1, 1, -1))
    piece_shape = pltpu.VMEM((rows, width + 128), BF16)
    far_out, rank_own = small_call(
        functools.partial(far_kernel, len(far)),
        "far_blocks",
        [pltpu.VMEM((rows, len(far) * width + 128), BF16), pltpu.VMEM((rows, 128), F32)],
        [attended, row_slot, slot_mine, own_shrink, other_pages] + [weights[1, k] for k in far],
    )
    from_far = along_y(far_out)
    straight, cross = near_blocks(
        [(0, 1), (1, 1)], width + 128, attended, rank_own, out_weight, [], n_tensor
    )
    moved = [along_z(straight, 1), along_both(cross, 1)]
    after = []
    for spot, k in enumerate(far):
        piece = small_call(
            functools.partial(add_kernel, spot),
            "add_block",
            piece_shape,
            [attended, weights[0, k], from_far, rank_own] + after,
        )
        moved.append(along_z(piece, k))
        after = [piece]
    (own_far,) = near_blocks([(1, 0)], width, attended, rank_own, out_weight, [piece], n_tensor)
    from_own = along_y(own_far)
    own, expand_pages = own_block(attended, res, slot_mine, own_expand, other_pages, out_weight, own_far)
    result = small_call(
        finish_kernel,
        "finish",
        pltpu.VMEM((rows, width), BF16),
        [own, expand_pages, row_slot, rank_own, from_far, from_own] + moved,
    )
    held = [result] + [along_z(result, k) for k in range(1, n_z)]
    crossed = [along_both(result, k) if k < 2 else along_y(held[k]) for k in range(n_z)]
    spots = [(0, 0), (1, 1), (1, 0)] + [(k, side) for k in range(2, n_z) for side in (0, 1)]
    spots.insert(len(spots) - 2, (0, 1))
    forwarded = [(k, side) for k, side in spots if k and side]
    placed = None
    for group in ([p for p in spots if p not in forwarded], forwarded):
        placed = place([(crossed if side else held)[k] for k, side in group], group, n_tensor, placed)
    return placed


def solution(mesh):
    return jax.shard_map(
        functools.partial(body, mesh.shape["tensor"]),
        mesh=mesh,
        in_specs=(
            P(("group", "req"), "tensor"),
            P(("group", "tensor"), None, None, None),
            P(("group", "req"), "tensor", None, None, None),
            P(("group", "req")),
            P(("group", "req"), None),
            P("tensor", None),
            P("req", None, None, "tensor"),
            P(("group", "req")),
            P(),
        ),
        out_specs=P(("group", "req"), None),
        check_vma=False,
    )
```
